256 devices in a mesh: complex: 2 (over core), row: 8 (over z), col: 16 (over y, x).
Axes of the slice: x: 4, y: 4, z: 8, core: 2. Of those that a mesh axis runs over, the one named last changes fastest.
Arguments:
- pair_act: bfloat16 [768, 384, 128], P(('complex', 'row'), 'col'), parts along dimension 0, may hold values from -64 to 64, as said below
- cotangent: bfloat16 [768, 384, 128], P(('complex', 'row'), 'col'), parts along dimension 0, may hold values from -6 to 6
- ln_gain: float32 [128], replicated, may hold values from 0.1 to 1.9
- ln_shift: float32 [128], replicated, may hold values from -3 to 3
- w_proj: bfloat16 [128, 512], replicated, may hold values from -0.5 to 0.5
- gate_bias: float32 [128], replicated, may hold values from -4 to 4
- w_bias: bfloat16 [128, 4], replicated, may hold values from -64 to 64
- w_out: bfloat16 [128, 128], replicated, may hold values from -0.5 to 0.5
- residue_mask: int32 [768], P(('complex', 'col')), parts along dimension 0, may hold values 0 or 1
- valid_length: int32 [2], P('complex'), parts along dimension 0, may hold values from 96 to 384
Outputs:
- update: bfloat16 [768, 384, 128], P(('complex', 'row'), 'col'), parts along dimension 0
- pair_grad: bfloat16 [768, 384, 128], P(('complex', 'row'), 'col'), parts along dimension 0
- proj_grad: float32 [256, 512], P('complex'), parts along dimension 0
The draws below stay inside these ranges and needn't reach their ends.
There are 2 independent parts, one for each index of `complex`. The reference program is written for one: setup_inputs(seed, part) draws one part's arguments, and reference() takes and returns one part's arrays. A program takes and returns all parts, laid end to end along the dimension named above; an argument that names none is the same for every part. Nothing has to cross between parts.
Inputs may be any that keep to these rules, and one draw needn't show every extreme that they name: `pair_act`: finite values.
All inputs are finite; a program needn't handle non-finite values. No bound on the sum of `residue_mask` on one device may be relied on, other than what follows from the above.
Results may differ from the reference program's by a relative error of at most 0.012.
The reference program's roundings to bfloat16 on the way (of `normed`, `weights_b`, `gated_out`, `d_out`, `d_attn`, `d_score_b` and `d_proj`) count: a program that leaves them out, or rounds other values in their place, can miss the bound.
Values may be sent and summed in bfloat16 or wider, within the bound.
A program may use at most 128 MiB of HBM per device.

```python
import math
import jax
import jax.numpy as jnp
from jax import lax

N = 384
C = 128
H = 4
DH = 32
HD = 128


def draw_pair_act(key, part):
    key = jax.random.fold_in(key, 11)
    normal_key, entry_key, channel_key = jax.random.split(key, 3)
    normal_part = jax.random.normal(normal_key, (N, N, C), jnp.float32)
    entry_scale = jnp.exp(jax.random.uniform(entry_key, (N, N, 1), jnp.float32, 0.0, math.log(10.0)))
    channel_scale = jnp.exp(jax.random.uniform(channel_key, (1, 1, C), jnp.float32, 0.0, math.log(10.0)))
    values = normal_part * channel_scale * entry_scale * 0.1
    return jnp.clip(values, -64.0, 64.0).astype(jnp.bfloat16)


def draw_w_bias(key, part):
    key = jax.random.fold_in(key, 23)
    normal_part = jax.random.normal(key, (C, H), jnp.float32) * C ** (-0.5)
    values = normal_part * 2.0
    return jnp.clip(values, -64.0, 64.0).astype(jnp.bfloat16)


def touch_ends(values, stream_key, smallest, high):
    dims = values.shape
    spot = [jax.random.randint(jax.random.fold_in(stream_key, axis), (), 0, dims[axis]) for axis in range(len(dims))]
    values = values.at[tuple(spot)].set(smallest)
    longest = dims.index(max(dims))
    spot[longest] = (spot[longest] + 1) % dims[longest]
    return values.at[tuple(spot)].set(high)


def levels(stream_key, extent, pieces, smallest, top_value):
    gain = 1.0
    for dim, parts in pieces:
        steps = jax.random.uniform(jax.random.fold_in(jax.random.fold_in(stream_key, 6), dim), (parts,), jnp.float32, smallest / len(pieces), top_value / len(pieces))
        gain = gain * jnp.repeat(jnp.exp(steps), extent[dim] // parts).reshape((-1,) + (1,) * (len(extent) - 1 - dim))
    return gain


def normal_values(rng, shape, spread, most, pieces=(), held_as=jnp.bfloat16):
    gain = levels(rng, shape, pieces, -0.22, 0.18) if pieces else 1.0
    entries = jax.random.normal(rng, shape, jnp.float32) * spread * gain
    return jnp.minimum(jnp.maximum(entries, -most), most).astype(held_as)


def setup_inputs(seed: int = 0, part: int = 0) -> dict:
    seeds = jax.random.split(jax.random.key(seed), 11)
    own_keys = jax.random.split(jax.random.fold_in(seeds[10], part), 11)
    pair_act = draw_pair_act(jax.random.fold_in(jax.random.fold_in(seeds[10], part), 71), part)
    cotangent = normal_values(own_keys[1], (N, N, C), 1.0, 6.0, ((0, 8), (1, 16)))
    ln_gain = jnp.clip(1.0 + 0.18 * jax.random.normal(seeds[2], (C,), jnp.float32), 0.1, 1.9)
    ln_shift = normal_values(seeds[3], (C,), 0.5, 3.0, (), jnp.float32)
    w_proj = normal_values(seeds[4], (C, 4 * HD), C ** -0.5, 0.5)
    gate_bias = normal_values(seeds[5], (HD,), 1.0, 4.0, (), jnp.float32)
    w_bias = draw_w_bias(jax.random.fold_in(seeds[10], 71), part)
    w_out = normal_values(seeds[7], (HD, C), HD ** -0.5, 0.5)
    residue_mask = touch_ends((jax.random.randint(own_keys[8], (N,), 0, 10) < 9).astype(jnp.int32), jax.random.fold_in(own_keys[8], 1), 0, 1)
    valid_length = jax.random.randint(own_keys[9], (1,), N // 4, N + 1).astype(jnp.int32)
    return dict(pair_act=pair_act, cotangent=cotangent, ln_gain=ln_gain, ln_shift=ln_shift, w_proj=w_proj, gate_bias=gate_bias, w_bias=w_bias, w_out=w_out, residue_mask=residue_mask, valid_length=valid_length)


neg_large = -1000000000.0
ln_eps = 1e-05

def rounded(values):
    return lax.optimization_barrier(values.astype(jnp.bfloat16)).astype(jnp.float32)

def row_attention(queries, key_rows, value_rows, pair_bias, negative, d_attn):
    q_full = queries.astype(jnp.float32)
    k_full = key_rows.astype(jnp.float32)
    v_full = value_rows.astype(jnp.float32)
    d_full = d_attn.astype(jnp.float32)
    scores = jnp.einsum('jhd,khd->hjk', q_full, k_full) + pair_bias + negative
    row_max = lax.optimization_barrier(jnp.max(scores, axis=-1, keepdims=True))
    exponent = jnp.exp(scores - row_max)
    weights = exponent / lax.optimization_barrier(jnp.sum(exponent, axis=-1, keepdims=True))
    weights_b = rounded(weights)
    attended = jnp.einsum('hjk,khd->jhd', weights_b, v_full)
    d_prob = jnp.einsum('jhd,khd->hjk', d_full, v_full)
    d_score = weights * (d_prob - lax.optimization_barrier(jnp.sum(weights * d_prob, axis=-1, keepdims=True)))
    d_score_b = rounded(d_score)
    d_values = jnp.einsum('hjk,jhd->khd', weights_b, d_full)
    d_query = jnp.einsum('hjk,khd->jhd', d_score_b, k_full)
    d_keys = jnp.einsum('hjk,jhd->khd', d_score_b, q_full)
    return (attended, d_query, d_keys, d_values, d_score)

def reference(pair_act, cotangent, ln_gain, ln_shift, w_proj, gate_bias, w_bias, w_out, residue_mask, valid_length):
    query_scale = DH ** (-0.5)
    positions = jnp.arange(N, dtype=jnp.int32)
    key_valid = jnp.where(positions < valid_length[0], residue_mask, 0)
    values = pair_act.astype(jnp.float32)
    centre = values - lax.optimization_barrier(jnp.mean(values, axis=-1, keepdims=True))
    inverse = lax.rsqrt(lax.optimization_barrier(jnp.mean(centre * centre, axis=-1, keepdims=True)) + ln_eps)
    standard = centre * inverse
    normed = (standard * ln_gain + ln_shift).astype(jnp.bfloat16)
    flat_rows = normed.reshape(N * N, C)
    projected = jnp.dot(flat_rows, w_proj, preferred_element_type=jnp.float32)
    queries = (projected[:, :HD] * query_scale).astype(jnp.bfloat16).reshape(N, N, H, DH)
    key_rows = projected[:, HD:2 * HD].astype(jnp.bfloat16).reshape(N, N, H, DH)
    value_rows = projected[:, 2 * HD:3 * HD].astype(jnp.bfloat16).reshape(N, N, H, DH)
    gate_value = jax.nn.sigmoid(projected[:, 3 * HD:] + gate_bias)
    logits = jnp.dot(flat_rows, w_bias, preferred_element_type=jnp.float32)
    pair_bias = jnp.transpose(logits.reshape(N, N, H), (2, 0, 1))
    pair_mask = (key_valid[:, None] * key_valid[None, :]).astype(jnp.float32).reshape(N * N, 1)
    d_out = jnp.where(pair_mask > 0, cotangent.reshape(N * N, C), jnp.zeros((), jnp.bfloat16))
    d_gated = jnp.dot(d_out, w_out.T, preferred_element_type=jnp.float32)
    d_attn = (d_gated * gate_value).astype(jnp.bfloat16).reshape(N, N, H, DH)
    negative = jnp.where(key_valid > 0, 0.0, neg_large).astype(jnp.float32)

    def row_step(bias_total, row_index):
        attended, d_query, d_keys, d_values, d_score = row_attention(queries[row_index], key_rows[row_index], value_rows[row_index], pair_bias, negative, d_attn[row_index])
        return (bias_total + d_score, (attended, d_query, d_keys, d_values))
    d_bias, (attended, d_query, d_keys, d_values) = lax.scan(row_step, jnp.zeros((H, N, N), jnp.float32), positions)
    attended = attended.reshape(N * N, HD)
    gated_out = (gate_value * attended).astype(jnp.bfloat16)
    update = (jnp.dot(gated_out, w_out, preferred_element_type=jnp.float32) * pair_mask).astype(jnp.bfloat16).reshape(N, N, C)
    d_gate_in = d_gated * attended * gate_value * (1.0 - gate_value)
    d_proj = jnp.concatenate([d_query.reshape(N * N, HD) * query_scale, d_keys.reshape(N * N, HD), d_values.reshape(N * N, HD), d_gate_in], axis=1).astype(jnp.bfloat16)
    bias_term = jnp.dot(jnp.transpose(d_bias, (1, 2, 0)).reshape(N * N, H), w_bias.astype(jnp.float32).T, precision=lax.Precision.HIGHEST)
    d_normed = jnp.dot(d_proj, w_proj.T, preferred_element_type=jnp.float32) + bias_term
    proj_grad = jnp.dot(flat_rows.T, d_proj, preferred_element_type=jnp.float32)
    d_unit = d_normed.reshape(N, N, C) * ln_gain
    mean_grad = lax.optimization_barrier(jnp.mean(d_unit, axis=-1, keepdims=True))
    mean_cross = lax.optimization_barrier(jnp.mean(d_unit * standard, axis=-1, keepdims=True))
    pair_grad = (inverse * (d_unit - mean_grad - standard * mean_cross)).astype(jnp.bfloat16)
    return (update, pair_grad, proj_grad)
```

```python
import jax
import jax.numpy as jnp
from jax import lax
from jax.experimental import pallas as pl
from jax.experimental.pallas import tpu as pltpu
from jax.sharding import PartitionSpec as P

MESH = pl.DeviceIdType.MESH
F32 = jnp.float32
BF16 = jnp.bfloat16
N = 384
C = 128
H = 4
DH = 32
HD = H * DH
COLS = 16
WIDTH = N // COLS
OWN = 3
PART = OWN * WIDTH
INBOX = 176
VMEM_LIMIT = 60 * 1024 * 1024
NT = (((1,), (1,)), ((), ()))
TN = (((0,), (0,)), ((), ()))


class Place:
    def __init__(self):
        self.e = lax.axis_index("complex")
        self.z = lax.axis_index("row")
        self.c = lax.axis_index("col")
        self.part = lax.rem(self.z, 2)
        self.zz = lax.div(self.z, 2)
        self.y = lax.div(self.c, 4)
        self.x = lax.rem(self.c, 4)
        self.f, self.g = self.axes(self.e)
        self.swap_z = self.zz * 2 + self.e
        self.stays = self.part == self.e
        self.row0 = (self.zz * 2 + self.e) * (COLS * OWN) + self.c * OWN

    def axes(self, e):
        return self.x * (1 - e) + self.y * e, self.y * (1 - e) + self.x * e

    def col(self, e, f, g):
        return lax.rem(f, 4) * (1 + 3 * e) + lax.rem(g, 4) * (4 - 3 * e)

    def swapped(self, c):
        return (self.part, self.swap_z, c)

    def zpeer(self, d):
        return (self.e, lax.rem(self.zz + d, 4) * 2 + self.part, self.c)

    def fpeer(self, d):
        return (self.e, self.z, self.col(self.e, self.f + d, self.g))

    def gpeer(self, d):
        return (self.e, self.z, self.col(self.e, self.f, self.g + d))

    def partner(self):
        return (1 - self.e, self.z, self.c)


def remote(src, dst, send, recv, device):
    return pltpu.make_async_remote_copy(
        src_ref=src, dst_ref=dst, send_sem=send, recv_sem=recv, device_id=device, device_id_type=MESH
    )


def arrived(ref, sem):
    pltpu.make_async_copy(ref, ref, sem).wait()


def greet(device):
    pl.semaphore_signal(pltpu.get_barrier_semaphore(), inc=1, device_id=device, device_id_type=MESH)


def greet_common(at):
    def column(d, carry):
        @pl.when(jnp.logical_or(d > 0, jnp.logical_not(at.stays)))
        def _():
            greet(at.swapped(lax.rem(at.c + d, COLS)))

        return carry

    lax.fori_loop(0, COLS, column, 0)
    for d in (1, 2, 3):
        greet(at.zpeer(d))
        greet(at.fpeer(d))
        greet(at.gpeer(d))
    greet(at.partner())
    return COLS + 10 - at.stays.astype(jnp.int32)


def exchange_start(at, source, landing, send, recv):
    def column(d, carry):
        t = lax.rem(at.c + d, COLS)
        here = jnp.logical_and(d == 0, at.stays)

        @pl.when(here)
        def _():
            pltpu.make_async_copy(source.at[t], landing.at[at.c], recv.at[at.c]).start()

        @pl.when(jnp.logical_not(here))
        def _():
            remote(source.at[t], landing.at[at.c], send.at[t], recv.at[at.c], at.swapped(t)).start()

        return carry

    lax.fori_loop(0, COLS, column, 0)


def exchange_arrived(landing, recv):
    def column(d, carry):
        arrived(landing.at[d], recv.at[d])
        return carry

    lax.fori_loop(0, COLS, column, 0)


def exchange_sent(at, source, send):
    def column(d, carry):
        t = lax.rem(at.c + d, COLS)

        @pl.when(jnp.logical_or(d > 0, jnp.logical_not(at.stays)))
        def _():
            arrived(source.at[t], send.at[t])

        return carry

    lax.fori_loop(0, COLS, column, 0)


def gather_kernel(
    msg,
    gain,
    shift,
    w_proj,
    w_proj_t,
    gate_bias,
    w_bias_t,
    w_out,
    bias,
    normed,
    standard,
    rstd,
    q,
    k,
    v,
    d,
    q_t,
    k_t,
    v_t,
    d_t,
    gate,
    dgate,
    mask,
    inbox,
    in_send,
    in_recv,
    z_send,
    z_recv,
    f_send,
    f_recv,
    g_send,
    g_recv,
    p_send,
    p_recv,
):
    at = Place()
    count = greet_common(at)
    pl.semaphore_wait(pltpu.get_barrier_semaphore(), count)
    exchange_start(at, msg, inbox, in_send, in_recv)
    exchange_arrived(inbox, in_recv)
    mask[...] = inbox[:, 2 * PART : 2 * PART + WIDTH, :].astype(F32).reshape(N, C)


    for s in range(OWN):
        values = inbox[:, s * WIDTH : (s + 1) * WIDTH, :].astype(F32).reshape(N, C)
        centre = values - jnp.mean(values, axis=-1, keepdims=True)
        inverse = lax.rsqrt(jnp.mean(centre * centre, axis=-1, keepdims=True) + 1e-5)
        unit = centre * inverse
        standard[s] = unit
        rstd[s] = jnp.broadcast_to(inverse, (N, C))
        rows = (unit * gain[...] + shift[...]).astype(BF16)
        normed[s] = rows
        logits = lax.dot_general(w_bias_t[...], rows, NT, preferred_element_type=F32)
        bias[at.zz, at.e, at.c, s] = logits[:H]

    mine = bias.at[at.zz, at.e, at.c]
    for n in (1, 2, 3):
        remote(mine, mine, z_send.at[n - 1], z_recv.at[n - 1], at.zpeer(n)).start()

    def project(s):
        rows = normed[s]
        flat = jnp.dot(rows, w_proj[...], preferred_element_type=F32)
        q[s] = (flat[:, :HD] * DH ** (-0.5)).astype(BF16)
        k[s] = flat[:, HD : 2 * HD].astype(BF16)
        v[s] = flat[:, 2 * HD : 3 * HD].astype(BF16)
        gates = jax.nn.sigmoid(flat[:, 3 * HD :] + gate_bias[...])
        flat_t = lax.dot_general(w_proj_t[...], rows, NT, preferred_element_type=F32)
        q_t[s] = (flat_t[:HD] * DH ** (-0.5)).astype(BF16)
        k_t[s] = flat_t[HD : 2 * HD].astype(BF16)
        v_t[s] = flat_t[2 * HD : 3 * HD].astype(BF16)
        cot = inbox[:, PART + s * WIDTH : PART + (s + 1) * WIDTH, :].astype(F32).reshape(N, C)
        pair = mask[...] * mask[pl.ds(at.row0 + s, 1), :]
        d_out = jnp.where(pair > 0, cot, 0.0).astype(BF16)
        d_gated = lax.dot_general(d_out, w_out[...], NT, preferred_element_type=F32)
        d_attn = d_gated * gates
        d[s] = d_attn.astype(BF16)
        d_t[s] = d_attn.T.astype(BF16)
        gate[s] = gates
        dgate[s] = d_gated * gates * (1.0 - gates)

    def chunk(ref, e, c):
        return ref.at[:, e, c]

    def to_partner(a, b):
        part = chunk(bias, at.e, at.col(at.e, at.f - a + 4, at.g - b + 4))
        remote(part, part, p_send.at[a, b], p_recv.at[a, b], at.partner()).start()

    def to_second(a):
        part = chunk(bias, at.e, at.col(at.e, at.f - a + 4, at.g))
        for n in (1, 2, 3):
            remote(part, part, g_send.at[a, n - 1], g_recv.at[a, n - 1], at.gpeer(n)).start()

    project(0)
    for n in (1, 2, 3):
        arrived(bias.at[lax.rem(at.zz - n + 4, 4), at.e, at.c], z_recv.at[n - 1])
    own = chunk(bias, at.e, at.c)
    for n in (1, 2, 3):
        remote(own, own, f_send.at[n - 1], f_recv.at[n - 1], at.fpeer(n)).start()
    to_second(0)
    to_partner(0, 0)
    project(1)
    for n in (1, 2, 3):
        part = chunk(bias, at.e, at.col(at.e, at.f - n + 4, at.g))
        arrived(part, f_recv.at[n - 1])
        to_second(n)
        to_partner(n, 0)
    project(2)
    for a in range(4):
        for n in (1, 2, 3):
            part = chunk(bias, at.e, at.col(at.e, at.f - a + 4, at.g - n + 4))
            arrived(part, g_recv.at[a, n - 1])
            to_partner(a, n)
    other = 1 - at.e
    f_other, g_other = at.axes(other)
    for a in range(4):
        for b in range(4):
            part = chunk(bias, other, at.col(other, f_other - a + 4, g_other - b + 4))
            arrived(part, p_recv.at[a, b])
    for n in (1, 2, 3):
        arrived(mine, z_send.at[n - 1])
        arrived(own, f_send.at[n - 1])
        for a in range(4):
            arrived(own, g_send.at[a, n - 1])
    for a in range(4):
        for b in range(4):
            arrived(own, p_send.at[a, b])
    exchange_sent(at, msg, in_send)


def attend_kernel(
    bias,
    mask,
    q,
    k,
    v,
    d,
    q_t,
    k_t,
    v_t,
    d_t,
    gate,
    dgate,
    normed,
    w_out,
    w_proj,
    update,
    d_normed,
    proj,
    d_bias,
    bias_t,
    d_bias_t,
    att_t,
    dq_t,
    dk,
    dv,
):
    blocks = [slice(n * C, (n + 1) * C) for n in range(3)]
    negative = (mask[...] - 1.0) * 1e9
    for h in range(H):
        for lanes in blocks:
            bias_t[h, :, lanes] = bias[lanes, h, :].T + negative
    dk[...] = jnp.zeros_like(dk)
    dv[...] = jnp.zeros_like(dv)

    def head(h, carry):
        at_head = pl.multiple_of(h * DH, DH)
        here = pl.ds(at_head, DH)
        lane = lax.div(lax.broadcasted_iota(jnp.int32, (C, C), 1), DH)
        row = lax.div(lax.broadcasted_iota(jnp.int32, (C, C), 0), DH)
        by_lane = (lane == h).astype(F32).astype(BF16)
        by_row = (row == h).astype(F32).astype(BF16)
        for s in range(OWN):
            keys, values = k[s], v[s]
            keys_t, values_t = k_t[s, here, :], v_t[s, here, :]
            dk_sum = dv_sum = None
            for lanes in blocks:
                scores = jnp.dot(keys, q_t[s, :, lanes] * by_row, preferred_element_type=F32)
                scores = scores + bias_t[h, :, lanes]
                exponent = jnp.exp(scores - jnp.max(scores, axis=0, keepdims=True))
                weights = exponent * (1.0 / jnp.sum(exponent, axis=0, keepdims=True))
                weights_b = weights.astype(BF16)
                attended = jnp.dot(values_t, weights_b, preferred_element_type=F32)
                att_t[s, here, lanes] = attended
                delta = jnp.sum(attended * d_t[s, here, lanes].astype(F32), axis=0, keepdims=True)
                d_prob = jnp.dot(values, d_t[s, :, lanes] * by_row, preferred_element_type=F32)
                d_score = weights * (d_prob - delta)
                d_score_b = d_score.astype(BF16)
                if s == 0:
                    d_bias_t[h, :, lanes] = d_score
                else:
                    d_bias_t[h, :, lanes] += d_score
                dq_t[s, here, lanes] = jnp.dot(keys_t, d_score_b, preferred_element_type=F32)
                dv_part = jnp.dot(weights_b, d[s, lanes, :] * by_lane, preferred_element_type=F32)
                dk_part = jnp.dot(d_score_b, q[s, lanes, :] * by_lane, preferred_element_type=F32)
                dv_sum = dv_part if dv_sum is None else dv_sum + dv_part
                dk_sum = dk_part if dk_sum is None else dk_sum + dk_part
            dk[s] += dk_sum
            dv[s] += dv_sum
        return carry

    lax.fori_loop(0, H, head, 0)
    for h in range(H):
        for lanes in blocks:
            d_bias[lanes, h, :] = d_bias_t[h, :, lanes].T

    at = Place()
    for s in range(OWN):
        attended = att_t[s].T
        gated = (gate[s] * attended).astype(BF16)
        pair = mask[...] * mask[pl.ds(at.row0 + s, 1), :]
        update[s] = jnp.dot(gated, w_out[...], preferred_element_type=F32) * pair
        d_proj = jnp.concatenate(
            [dq_t[s].T * DH ** (-0.5), dk[s], dv[s], dgate[s] * attended], axis=1
        ).astype(BF16)
        d_normed[s] = lax.dot_general(d_proj, w_proj[...], NT, preferred_element_type=F32)
        normed_t = normed[s].astype(F32).T.astype(BF16)
        part = jnp.dot(normed_t, d_proj, preferred_element_type=F32)
        if s == 0:
            proj[...] = part
        else:
            proj[...] += part


def reduce_kernel(
    d_bias,
    proj,
    d_normed,
    update,
    standard,
    rstd,
    gain,
    w_bias_t,
    out,
    proj_out,
    ra,
    r2,
    tt,
    r3,
    uu,
    r4,
    r5,
    v5,
    r6,
    v6,
    stage,
    outbox,
    a_send,
    a_recv,
    g_send,
    g_recv,
    f_send,
    f_recv,
    z_send,
    z_recv,
    c_send,
    c_recv,
    w_send,
    w_recv,
    o_send,
    o_recv,
    m_send,
    m_recv,
):
    at = Place()
    e, f, g = at.e, at.f, at.g
    count = greet_common(at)

    def greet_column(n, carry):
        greet((e, at.z, lax.rem(at.c + n, COLS)))
        return carry

    lax.fori_loop(1, COLS, greet_column, 0)

    def greet_source(n, carry):
        z = lax.rem(n, 4) * 2 + e
        core = lax.div(n, 4)

        @pl.when(jnp.logical_not(jnp.logical_and(z == at.z, core == e)))
        def _():
            greet((core, z, at.c))

        return carry

    lax.fori_loop(0, 8, greet_source, 0)
    count = count + (COLS - 1) + 8 - at.stays.astype(jnp.int32)
    pl.semaphore_wait(pltpu.get_barrier_semaphore(), count)

    other = 1 - e
    for b in (1, 2, 3, 0):
        for a in range(4):
            column = at.col(other, g + a, f + b)
            remote(
                d_bias.at[:, other, column],
                ra.at[b, lax.rem(g + a, 4)],
                a_send.at[b, a],
                a_recv.at[b, a],
                at.partner(),
            ).start()

    def rows_of(ref, c):
        return ref.at[pl.ds(pl.multiple_of(c * 8, 8), 8), :]

    def scatter(n, carry):
        t = lax.rem(at.c + n, COLS)
        remote(rows_of(proj, t), r5.at[n], c_send.at[n], c_recv.at[n], (e, at.z, t)).start()
        return carry

    lax.fori_loop(1, COLS, scatter, 0)

    for b in (1, 2, 3, 0):
        for a in range(4):
            ff = lax.rem(f + a, 4)
            arrived(ra.at[b, ff], a_recv.at[b, a])
            ra[b, ff] += d_bias[:, e, at.col(e, f + a, g + b)]
        if b > 0:
            remote(ra.at[b], r2.at[b - 1], g_send.at[b - 1], g_recv.at[b - 1], at.gpeer(b)).start()

    def column_arrived(n, total):
        arrived(r5.at[n], c_recv.at[n])
        return total + r5[n]

    start = proj[pl.ds(pl.multiple_of(at.c * 8, 8), 8), :]
    v5[...] = lax.fori_loop(1, COLS, column_arrived, start)
    worker = e * 4 + at.zz

    def to_all(z, carry):
        here = jnp.logical_and(at.stays, z == at.z)

        @pl.when(here)
        def _():
            pltpu.make_async_copy(v5, r6.at[worker], w_recv.at[worker]).start()

        @pl.when(jnp.logical_not(here))
        def _():
            remote(v5, r6.at[worker], w_send.at[z], w_recv.at[worker], (at.part, z, at.c)).start()

        return carry

    lax.fori_loop(0, 8, to_all, 0)

    for n in (1, 2, 3):
        arrived(r2.at[n - 1], g_recv.at[n - 1])
    for a in (1, 2, 3, 0):
        ff = lax.rem(f + a, 4)
        tt[ff] = (ra[0, ff] + r2[0, ff]) + (r2[1, ff] + r2[2, ff])
        if a > 0:
            remote(tt.at[ff], r3.at[a - 1], f_send.at[a - 1], f_recv.at[a - 1], at.fpeer(a)).start()

    def worker_arrived(n, total):
        arrived(r6.at[n], w_recv.at[n])
        return total + r6[n]

    v6[...] = lax.fori_loop(0, 8, worker_arrived, jnp.zeros((8, 4 * HD), F32))
    own_rows = rows_of(proj_out, at.c)
    pltpu.make_async_copy(v6, own_rows, o_recv.at[0]).start()

    def spread(n, carry):
        t = lax.rem(at.c + n, COLS)
        remote(v6, own_rows, o_send.at[n], o_recv.at[n], (e, at.z, t)).start()
        return carry

    lax.fori_loop(1, COLS, spread, 0)

    for n in (1, 2, 3):
        arrived(r3.at[n - 1], f_recv.at[n - 1])
    uu[...] = (tt[f] + r3[0]) + (r3[1] + r3[2])
    for n in (1, 2, 3):
        there = lax.rem(at.zz + n, 4)
        remote(uu.at[there], r4.at[n - 1], z_send.at[n - 1], z_recv.at[n - 1], at.zpeer(n)).start()
    for n in (1, 2, 3):
        arrived(r4.at[n - 1], z_recv.at[n - 1])
    total = (uu[at.zz] + r4[0]) + (r4[1] + r4[2])

    for s in range(OWN):
        bias_term = lax.dot_general(
            total[s], w_bias_t[...], TN, preferred_element_type=F32, precision=lax.Precision.HIGHEST
        )
        unit = standard[s]
        grad = (d_normed[s] + bias_term) * gain[...]
        mean_grad = jnp.mean(grad, axis=-1, keepdims=True)
        mean_cross = jnp.mean(grad * unit, axis=-1, keepdims=True)
        result = rstd[s] * (grad - mean_grad - unit * mean_cross)
        stage[:, s * WIDTH : (s + 1) * WIDTH, :] = update[s].reshape(COLS, WIDTH, C)
        stage[:, PART + s * WIDTH : PART + (s + 1) * WIDTH, :] = result.reshape(COLS, WIDTH, C)
    outbox[...] = stage[...].astype(BF16)
    exchange_start(at, outbox, out, m_send, m_recv)
    exchange_arrived(out, m_recv)

    def out_arrived(n, carry):
        t = lax.rem(at.c - n + COLS, COLS)
        arrived(rows_of(proj_out, t), o_recv.at[n])
        return carry

    lax.fori_loop(0, COLS, out_arrived, 0)
    for b in range(4):
        for a in range(4):
            arrived(ra.at[0, 0], a_send.at[b, a])
    for n in range(3):
        arrived(r2.at[0], g_send.at[n])
        arrived(r3.at[0], f_send.at[n])
        arrived(r4.at[0], z_send.at[n])

    def column_sent(n, carry):
        arrived(v5, c_send.at[n])
        arrived(v6, o_send.at[n])
        return carry

    lax.fori_loop(1, COLS, column_sent, 0)

    def worker_sent(z, carry):
        @pl.when(jnp.logical_not(jnp.logical_and(at.stays, z == at.z)))
        def _():
            arrived(v5, w_send.at[z])

        return carry

    lax.fori_loop(0, 8, worker_sent, 0)
    exchange_sent(at, outbox, m_send)


def dma(*shape):
    return pltpu.SemaphoreType.DMA(shape)


def vmem(count):
    return [pl.BlockSpec(memory_space=pltpu.VMEM)] * count


def shards(
    pair_act, cotangent, ln_gain, ln_shift, w_proj, gate_bias, w_bias, w_out, residue_mask, valid_length
):
    any_space = pl.BlockSpec(memory_space=pl.ANY)
    positions = lax.axis_index("col") * WIDTH + lax.iota(jnp.int32, WIDTH)
    flags = jnp.where(positions < valid_length[0], residue_mask, 0).astype(BF16)
    msg = jnp.concatenate(
        [
            pair_act.reshape(COLS, PART, C),
            cotangent.reshape(COLS, PART, C),
            jnp.broadcast_to(flags[None, :, None], (COLS, WIDTH, C)),
            jnp.zeros((COLS, INBOX - 2 * PART - WIDTH, C), BF16),
        ],
        axis=1,
    )
    gain = ln_gain.reshape(1, C)
    w_bias_t = w_bias.T
    natural = jax.ShapeDtypeStruct((OWN, N, C), F32)
    natural_b = jax.ShapeDtypeStruct((OWN, N, C), BF16)
    turned_b = jax.ShapeDtypeStruct((OWN, C, N), BF16)
    (bias, normed, standard, rstd, q, k, v, d, q_t, k_t, v_t, d_t, gate, dgate, mask) = pl.pallas_call(
        gather_kernel,
        out_shape=[
            jax.ShapeDtypeStruct((4, 2, COLS, OWN, H, N), F32),
            natural_b,
            natural,
            natural,
            natural_b,
            natural_b,
            natural_b,
            natural_b,
            turned_b,
            turned_b,
            turned_b,
            turned_b,
            natural,
            natural,
            jax.ShapeDtypeStruct((N, C), F32),
        ],
        in_specs=[any_space] + vmem(7),
        out_specs=vmem(15),
        scratch_shapes=[
            pltpu.VMEM((COLS, INBOX, C), BF16),
            dma(COLS),
            dma(COLS),
            dma(3),
            dma(3),
            dma(3),
            dma(3),
            dma(4, 3),
            dma(4, 3),
            dma(4, 4),
            dma(4, 4),
        ],
        compiler_params=pltpu.CompilerParams(
            collective_id=0, has_side_effects=True, vmem_limit_bytes=VMEM_LIMIT
        ),
        name="gather",
    )(
        msg,
        gain,
        ln_shift.reshape(1, C),
        w_proj,
        w_proj[:, : 3 * HD].T,
        gate_bias.reshape(1, HD),
        jnp.concatenate([w_bias_t, jnp.zeros((12, C), BF16)], axis=0),
        w_out,
    )
    update, d_normed, proj, d_bias = pl.pallas_call(
        attend_kernel,
        out_shape=[
            natural,
            natural,
            jax.ShapeDtypeStruct((C, 4 * HD), F32),
            jax.ShapeDtypeStruct((N, H, N), F32),
        ],
        in_specs=vmem(15),
        out_specs=vmem(4),
        scratch_shapes=[
            pltpu.VMEM((H, N, N), F32),
            pltpu.VMEM((H, N, N), F32),
            pltpu.VMEM((OWN, HD, N), F32),
            pltpu.VMEM((OWN, HD, N), F32),
            pltpu.VMEM((OWN, N, HD), F32),
            pltpu.VMEM((OWN, N, HD), F32),
        ],
        compiler_params=pltpu.CompilerParams(vmem_limit_bytes=VMEM_LIMIT),
        name="attend",
    )(bias.reshape(N, H, N), mask, q, k, v, d, q_t, k_t, v_t, d_t, gate, dgate, normed, w_out, w_proj)
    block = (4, OWN, H, N)
    out, proj_out = pl.pallas_call(
        reduce_kernel,
        out_shape=[
            jax.ShapeDtypeStruct((COLS, 2 * PART, C), BF16),
            jax.ShapeDtypeStruct((C, 4 * HD), F32),
        ],
        in_specs=vmem(8),
        out_specs=[any_space, any_space],
        scratch_shapes=[
            pltpu.VMEM((4, 4) + block, F32),
            pltpu.VMEM((3, 4) + block, F32),
            pltpu.VMEM((4,) + block, F32),
            pltpu.VMEM((3,) + block, F32),
            pltpu.VMEM(block, F32),
            pltpu.VMEM((3,) + block[1:], F32),
            pltpu.VMEM((COLS, 8, 4 * HD), F32),
            pltpu.VMEM((8, 4 * HD), F32),
            pltpu.VMEM((8, 8, 4 * HD), F32),
            pltpu.VMEM((8, 4 * HD), F32),
            pltpu.VMEM((COLS, 2 * PART, C), F32),
            pltpu.VMEM((COLS, 2 * PART, C), BF16),
            dma(4, 4),
            dma(4, 4),
            dma(3),
            dma(3),
            dma(3),
            dma(3),
            dma(3),
            dma(3),
            dma(COLS),
            dma(COLS),
            dma(8),
            dma(8),
            dma(COLS),
            dma(COLS),
            dma(COLS),
            dma(COLS),
        ],
        compiler_params=pltpu.CompilerParams(
            collective_id=1, has_side_effects=True, vmem_limit_bytes=VMEM_LIMIT
        ),
        name="reduce",
    )(
        d_bias.reshape((4, 2, COLS, OWN, H, N)),
        proj,
        d_normed,
        update,
        standard,
        rstd,
        gain,
        w_bias_t.astype(F32),
    )
    shape = pair_act.shape
    return (out[:, :PART].reshape(shape), out[:, PART:].reshape(shape), proj_out)


def solution(mesh):
    return jax.shard_map(
        shards,
        mesh=mesh,
        in_specs=(
            P(("complex", "row"), "col", None),
            P(("complex", "row"), "col", None),
            P(),
            P(),
            P(),
            P(),
            P(),
            P(),
            P(("complex", "col")),
            P("complex"),
        ),
        out_specs=(
            P(("complex", "row"), "col", None),
            P(("complex", "row"), "col", None),
            P("complex", None),
        ),
        check_vma=False,
    )
```

```python
import jax
import jax.numpy as jnp
from jax import lax
from jax.experimental import pallas as pl
from jax.experimental.pallas import tpu as pltpu
from jax.sharding import PartitionSpec as P

MESH = pl.DeviceIdType.MESH
F32 = jnp.float32
BF16 = jnp.bfloat16
N = 384
C = 128
H = 4
DH = 32
HD = H * DH
COLS = 16
ROWS = 8
WIDTH = N // COLS
TALL = N // ROWS
OWN = 3
PART = OWN * WIDTH
PADDED = 80
SLOT = 64
PAIR = 2 * SLOT
SCALE = DH ** (-0.5)
VMEM_LIMIT = 60 * 1024 * 1024
NT = (((1,), (1,)), ((), ()))


class Place:
    def __init__(self):
        self.e = lax.axis_index("complex")
        self.z = lax.axis_index("row")
        self.c = lax.axis_index("col")
        self.part = lax.rem(self.z, 2)
        self.zz = lax.div(self.z, 2)
        self.stays = self.part == self.e
        self.row0 = (self.zz * 2 + self.e) * TALL + self.c * OWN

    def swapped(self, c):
        return (self.part, self.zz * 2 + self.e, c)

    def plane(self, n):
        return (self.e, self.z, lax.rem(self.c + n, COLS))

    def partner(self):
        return (1 - self.e, self.z, self.c)

    def worker(self, core, zz):
        return (core, zz * 2 + self.e, self.c)

    def home(self, z):
        return (self.part, z, self.c)

    def is_worker(self, core, zz):
        return jnp.logical_and(self.stays, jnp.logical_and(core == self.e, zz == self.zz))

    def is_home(self, z):
        return jnp.logical_and(self.stays, z == self.z)


def remote(src, dst, send, recv, device):
    return pltpu.make_async_remote_copy(
        src_ref=src, dst_ref=dst, send_sem=send, recv_sem=recv, device_id=device, device_id_type=MESH
    )


def arrived(ref, sem):
    pltpu.make_async_copy(ref, ref, sem).wait()


def send_or_copy(here, src, dst, send, recv, device):
    @pl.when(here)
    def _():
        pltpu.make_async_copy(src, dst, recv).start()

    @pl.when(jnp.logical_not(here))
    def _():
        remote(src, dst, send, recv, device).start()


def greet(device):
    pl.semaphore_signal(pltpu.get_barrier_semaphore(), inc=1, device_id=device, device_id_type=MESH)


def greet_all(at):
    def plane(n, carry):
        greet(at.plane(n))
        return carry

    lax.fori_loop(1, COLS, plane, 0)

    def worker(n, carry):
        core, zz = lax.div(n, 4), lax.rem(n, 4)

        @pl.when(jnp.logical_not(at.is_worker(core, zz)))
        def _():
            greet(at.worker(core, zz))

        return carry

    lax.fori_loop(0, 8, worker, 0)

    def home(n, carry):
        greet(at.home(n * 2 + 1 - at.e))
        return carry

    lax.fori_loop(0, 4, home, 0)

    @pl.when(jnp.logical_not(at.stays))
    def _():
        def column(n, carry):
            greet(at.swapped(n))
            return carry

        lax.fori_loop(0, COLS, column, 0)

    return jnp.where(at.stays, COLS - 1 + 7 + 4, COLS - 1 + 8 + 4 + COLS)


def exchange_start(at, source, landing, send, recv):
    def column(n, carry):
        t = lax.rem(at.c + n, COLS)
        here = jnp.logical_and(n == 0, at.stays)
        send_or_copy(here, source.at[t], landing.at[at.c], send.at[t], recv.at[at.c], at.swapped(t))
        return carry

    lax.fori_loop(0, COLS, column, 0)


def exchange_arrived(landing, recv):
    def column(n, carry):
        arrived(landing.at[n], recv.at[n])
        return carry

    lax.fori_loop(0, COLS, column, 0)


def exchange_sent(at, source, send):
    def column(n, carry):
        t = lax.rem(at.c + n, COLS)

        @pl.when(jnp.logical_or(n > 0, jnp.logical_not(at.stays)))
        def _():
            arrived(source.at[t], send.at[t])

        return carry

    lax.fori_loop(0, COLS, column, 0)


def repeat_heads(w_bias):
    wide = w_bias[...].astype(F32)
    lane = lax.div(lax.broadcasted_iota(jnp.int32, (C, H * SLOT), 1), SLOT)
    total = jnp.zeros((C, H * SLOT), F32)
    for h in range(H):
        total = jnp.where(lane == h, wide[:, h : h + 1], total)
    return total.astype(BF16)


def only_row(repeated, i):
    lane = lax.rem(lax.broadcasted_iota(jnp.int32, (C, H * SLOT), 1), SLOT)
    return repeated * (lane == i).astype(F32).astype(BF16)


def standardize(values):
    centre = values - jnp.mean(values, axis=-1, keepdims=True)
    inverse = lax.rsqrt(jnp.mean(centre * centre, axis=-1, keepdims=True) + 1e-5)
    return centre * inverse, jnp.broadcast_to(inverse, values.shape)


def norm_backward(grad, unit, inverse):
    mean_grad = jnp.mean(grad, axis=-1, keepdims=True)
    mean_cross = jnp.mean(grad * unit, axis=-1, keepdims=True)
    return inverse * (grad - mean_grad - unit * mean_cross)


MAIN_SCRATCH = dict(
    m1=((COLS, PADDED, C), BF16),
    m2=((COLS, PART + WIDTH, C), BF16),
    in1=((COLS, PADDED, C), BF16),
    in2=((COLS, PART + WIDTH, C), BF16),
    w_proj_t=((3 * HD, C), BF16),
    w_rep=((C, H * SLOT), BF16),
    home_rows=((TALL, WIDTH, C), F32),
    zpack=((2, WIDTH, PAIR), F32),
    zin=((ROWS, WIDTH, PAIR), F32),
    bias=((H, COLS, WIDTH, N), F32),
    d_bias=((H, COLS, WIDTH, N), F32),
    d_other=((2, COLS, WIDTH, N), F32),
    d_plane=((2, COLS, WIDTH, N), F32),
    zout=((ROWS, WIDTH, PAIR), F32),
    hin=((2, 4, WIDTH, PAIR), F32),
    mask=((N, C), F32),
    normed=((OWN, N, C), BF16),
    unit=((OWN, N, C), F32),
    rstd=((OWN, N, C), F32),
    q=((OWN, N, C), BF16),
    k=((OWN, N, C), BF16),
    v=((OWN, N, C), BF16),
    d=((OWN, N, C), BF16),
    q_t=((OWN, C, N), BF16),
    k_t=((OWN, C, N), BF16),
    v_t=((OWN, C, N), BF16),
    d_t=((OWN, C, N), BF16),
    gate=((OWN, N, C), F32),
    dgate=((OWN, N, C), F32),
    att_t=((OWN, HD, N), F32),
    dq_t=((OWN, HD, N), F32),
    dk=((OWN, N, HD), F32),
    dv=((OWN, N, HD), F32),
    proj=((C, 4 * HD), F32),
    r5=((COLS, 8, 4 * HD), F32),
    v5=((8, 4 * HD), F32),
    r6=((8, 8, 4 * HD), F32),
    v6=((8, 4 * HD), F32),
    stage_u=((COLS, PADDED, C), F32),
    stage_a=((COLS, PADDED, C), F32),
    out_u=((COLS, PADDED, C), BF16),
    out_a=((COLS, PADDED, C), BF16),
)
MAIN_SEMS = dict(
    in1=(COLS,),
    in2=(COLS,),
    z=(8,),
    plane=(2, COLS),
    partner=(2,),
    back=(2,),
    d_plane=(2, COLS),
    dz=(8,),
    p1=(COLS,),
    p2=(8,),
    p3=(COLS,),
    u=(COLS,),
    a=(COLS,),
)
MAIN_IN = 9
MAIN_OUT = 6


class Names:
    pass


def main_kernel(*refs):
    (pair, cot, flags, gain, shift, w_proj, gate_bias, w_bias, w_out) = refs[:MAIN_IN]
    (land_u, land_a, proj_out, h_sum, home_unit, home_rstd) = refs[MAIN_IN : MAIN_IN + MAIN_OUT]
    rest = refs[MAIN_IN + MAIN_OUT :]
    m, send, recv = Names(), Names(), Names()
    for name, ref in zip(MAIN_SCRATCH, rest):
        setattr(m, name, ref)
    rest = rest[len(MAIN_SCRATCH) :]
    for name, ref in zip(MAIN_SEMS, rest):
        setattr(send, name, ref)
    for name, ref in zip(MAIN_SEMS, rest[len(MAIN_SEMS) :]):
        setattr(recv, name, ref)
    at = Place()
    e = at.e
    count = greet_all(at)

    m.m1[...] = jnp.concatenate(
        [pair[...].astype(F32).reshape(COLS, PART, C), jnp.zeros((COLS, PADDED - PART, C), F32)], axis=1
    ).astype(BF16)
    m.m2[...] = jnp.concatenate(
        [
            cot[...].astype(F32).reshape(COLS, PART, C),
            jnp.broadcast_to(flags[...][None], (COLS, WIDTH, C)),
        ],
        axis=1,
    ).astype(BF16)
    pl.semaphore_wait(pltpu.get_barrier_semaphore(), count)
    exchange_start(at, m.m1, m.in1, send.in1, recv.in1)
    exchange_start(at, m.m2, m.in2, send.in2, recv.in2)

    m.w_rep[...] = repeat_heads(w_bias)
    unit, inverse = standardize(pair[...].astype(F32).reshape(TALL * WIDTH, C))
    home_unit[...] = unit.reshape(TALL, WIDTH, C)
    home_rstd[...] = inverse.reshape(TALL, WIDTH, C)
    m.home_rows[...] = (unit * gain[...] + shift[...]).reshape(TALL, WIDTH, C)

    def home_bias(n, total):
        for i in range(8):
            rows = m.home_rows[n * 8 + i].astype(BF16)
            total = total + jnp.dot(rows, only_row(m.w_rep[...], n * 8 + i), preferred_element_type=F32)
        return total

    packed = lax.fori_loop(0, TALL // 8, home_bias, jnp.zeros((WIDTH, H * SLOT), F32))
    negative = (flags[...] - 1.0) * 1e9
    m.zpack[0] = packed[:, :PAIR] + negative
    m.zpack[1] = packed[:, PAIR:] + negative

    def to_workers(n, carry):
        core, zz = lax.div(n, 4), lax.rem(n, 4)
        send_or_copy(
            at.is_worker(core, zz),
            m.zpack.at[core],
            m.zin.at[at.z],
            send.z.at[n],
            recv.z.at[at.z],
            at.worker(core, zz),
        )
        return carry

    lax.fori_loop(0, 8, to_workers, 0)

    m.w_proj_t[...] = w_proj[:, : 3 * HD].astype(F32).T.astype(BF16)
    m.d_bias[...] = jnp.zeros_like(m.d_bias)
    m.dk[...] = jnp.zeros_like(m.dk)
    m.dv[...] = jnp.zeros_like(m.dv)
    exchange_arrived(m.in1, recv.in1)

    for s in range(OWN):
        values = m.in1[:, s * WIDTH : (s + 1) * WIDTH, :].astype(F32).reshape(N, C)
        unit, inverse = standardize(values)
        m.unit[s] = unit
        m.rstd[s] = inverse
        m.normed[s] = (unit * gain[...] + shift[...]).astype(BF16)

    for z in range(ROWS):
        arrived(m.zin.at[z], recv.z.at[z])
    for hh in range(2):
        head = e * 2 + hh
        m.bias[head, at.c] = jnp.concatenate(
            [m.zin[z][:, hh * SLOT : hh * SLOT + TALL] for z in range(ROWS)], axis=1
        )
        mine = m.bias.at[head, at.c]

        def to_plane(n, carry):
            remote(mine, mine, send.plane.at[hh, n], recv.plane.at[hh, n], at.plane(n)).start()
            return carry

        lax.fori_loop(1, COLS, to_plane, 0)

    for s in range(OWN):
        rows = m.normed[s]
        flat = jnp.dot(rows, w_proj[...], preferred_element_type=F32)
        m.q[s] = (flat[:, :HD] * SCALE).astype(BF16)
        m.k[s] = flat[:, HD : 2 * HD].astype(BF16)
        m.v[s] = flat[:, 2 * HD : 3 * HD].astype(BF16)
        m.gate[s] = jax.nn.sigmoid(flat[:, 3 * HD :] + gate_bias[...])
        flat_t = lax.dot_general(m.w_proj_t[...], rows, NT, preferred_element_type=F32)
        m.q_t[s] = (flat_t[:HD] * SCALE).astype(BF16)
        m.k_t[s] = flat_t[HD : 2 * HD].astype(BF16)
        m.v_t[s] = flat_t[2 * HD : 3 * HD].astype(BF16)

    exchange_arrived(m.in2, recv.in2)
    m.mask[...] = m.in2[:, PART : PART + WIDTH, :].astype(F32).reshape(N, C)
    for s in range(OWN):
        values = m.in2[:, s * WIDTH : (s + 1) * WIDTH, :].astype(F32).reshape(N, C)
        pair_mask = m.mask[...] * m.mask[pl.ds(at.row0 + s, 1), :]
        d_out = jnp.where(pair_mask > 0, values, 0.0).astype(BF16)
        d_gated = lax.dot_general(d_out, w_out[...], NT, preferred_element_type=F32)
        gates = m.gate[s]
        d_attn = d_gated * gates
        m.d[s] = d_attn.astype(BF16)
        m.d_t[s] = d_attn.T.astype(BF16)
        m.dgate[s] = d_attn * (1.0 - gates)

    def own_bias_arrived(hh):
        head = e * 2 + hh

        def from_plane(n, carry):
            arrived(m.bias.at[head, lax.rem(at.c - n + COLS, COLS)], recv.plane.at[hh, n])
            return carry

        lax.fori_loop(1, COLS, from_plane, 0)
        whole = m.bias.at[head]
        remote(whole, whole, send.partner.at[hh], recv.partner.at[hh], at.partner()).start()

    def other_bias_arrived(hh):
        arrived(m.bias.at[(1 - e) * 2 + hh], recv.partner.at[hh])

    def attend(h):
        here = pl.ds(pl.multiple_of(h * DH, DH), DH)
        lane = lax.div(lax.broadcasted_iota(jnp.int32, (C, C), 1), DH)
        row = lax.div(lax.broadcasted_iota(jnp.int32, (C, C), 0), DH)
        by_lane = (lane == h).astype(F32).astype(BF16)
        by_row = (row == h).astype(F32).astype(BF16)

        def one_row(s, carry):
            keys, values = m.k[s], m.v[s]
            keys_t, values_t = m.k_t[s, here, :], m.v_t[s, here, :]
            dk_sum = dv_sum = None
            for n in range(3):
                lanes = slice(n * C, (n + 1) * C)
                scores = jnp.dot(keys, m.q_t[s, :, lanes] * by_row, preferred_element_type=F32)
                scores = scores + m.bias[h, :, :, lanes].reshape(N, C)
                exponent = jnp.exp(scores - jnp.max(scores, axis=0, keepdims=True))
                weights = exponent * (1.0 / jnp.sum(exponent, axis=0, keepdims=True))
                weights_b = weights.astype(BF16)
                attended = jnp.dot(values_t, weights_b, preferred_element_type=F32)
                m.att_t[s, here, lanes] = attended
                delta = jnp.sum(attended * m.d_t[s, here, lanes].astype(F32), axis=0, keepdims=True)
                d_prob = jnp.dot(values, m.d_t[s, :, lanes] * by_row, preferred_element_type=F32)
                d_score = weights * (d_prob - delta)
                d_score_b = d_score.astype(BF16)
                m.d_bias[h, :, :, lanes] += d_score.reshape(COLS, WIDTH, C)
                m.dq_t[s, here, lanes] = jnp.dot(keys_t, d_score_b, preferred_element_type=F32)
                dv_part = jnp.dot(weights_b, m.d[s, lanes, :] * by_lane, preferred_element_type=F32)
                dk_part = jnp.dot(d_score_b, m.q[s, lanes, :] * by_lane, preferred_element_type=F32)
                dv_sum = dv_part if dv_sum is None else dv_sum + dv_part
                dk_sum = dk_part if dk_sum is None else dk_sum + dk_part
            m.dk[s] += dk_sum
            m.dv[s] += dv_sum
            return carry

        lax.fori_loop(0, OWN, one_row, 0)

    def to_other(hh):
        head = (1 - e) * 2 + hh
        remote(m.d_bias.at[head], m.d_other.at[hh], send.back.at[hh], recv.back.at[hh], at.partner()).start()

    def scatter_plane(hh):
        head = e * 2 + hh
        arrived(m.d_other.at[hh], recv.back.at[hh])
        m.d_bias[head] += m.d_other[hh]

        def to_plane(n, carry):
            remote(
                m.d_bias.at[head, lax.rem(at.c + n, COLS)],
                m.d_plane.at[hh, n],
                send.d_plane.at[hh, n],
                recv.d_plane.at[hh, n],
                at.plane(n),
            ).start()
            return carry

        lax.fori_loop(1, COLS, to_plane, 0)

    def plane_sum(hh):
        def from_plane(n, total):
            arrived(m.d_plane.at[hh, n], recv.d_plane.at[hh, n])
            return total + m.d_plane[hh, n]

        return lax.fori_loop(1, COLS, from_plane, m.d_bias[e * 2 + hh, at.c])

    own_bias_arrived(0)
    attend(e * 2)
    own_bias_arrived(1)
    other_bias_arrived(0)
    attend(2 - e * 2)
    to_other(0)
    other_bias_arrived(1)
    attend(3 - e * 2)
    to_other(1)
    scatter_plane(0)
    attend(e * 2 + 1)
    scatter_plane(1)

    for s in range(OWN):
        attended = m.att_t[s].T
        gated = (m.gate[s] * attended).astype(BF16)
        pair_mask = m.mask[...] * m.mask[pl.ds(at.row0 + s, 1), :]
        update = jnp.dot(gated, w_out[...], preferred_element_type=F32) * pair_mask
        d_proj = jnp.concatenate(
            [m.dq_t[s].T * SCALE, m.dk[s], m.dv[s], m.dgate[s] * attended], axis=1
        ).astype(BF16)
        d_normed = lax.dot_general(d_proj, w_proj[...], NT, preferred_element_type=F32)
        result = norm_backward(d_normed * gain[...], m.unit[s], m.rstd[s])
        m.stage_u[:, s * WIDTH : (s + 1) * WIDTH, :] = update.reshape(COLS, WIDTH, C)
        m.stage_a[:, s * WIDTH : (s + 1) * WIDTH, :] = result.reshape(COLS, WIDTH, C)
        normed_t = m.normed[s].astype(F32).T.astype(BF16)
        share = jnp.dot(normed_t, d_proj, preferred_element_type=F32)
        if s == 0:
            m.proj[...] = share
        else:
            m.proj[...] += share
    pad = jnp.zeros((COLS, PADDED - PART, C), F32)
    m.stage_u[:, PART:, :] = pad
    m.stage_a[:, PART:, :] = pad
    m.out_u[...] = m.stage_u[...].astype(BF16)
    m.out_a[...] = m.stage_a[...].astype(BF16)

    def rows_of(ref, c):
        return ref.at[pl.ds(pl.multiple_of(c * 8, 8), 8), :]

    def scatter_proj(n, carry):
        t = lax.rem(at.c + n, COLS)
        remote(rows_of(m.proj, t), m.r5.at[n], send.p1.at[n], recv.p1.at[n], at.plane(n)).start()
        return carry

    lax.fori_loop(1, COLS, scatter_proj, 0)
    exchange_start(at, m.out_u, land_u, send.u, recv.u)
    exchange_start(at, m.out_a, land_a, send.a, recv.a)

    halves = [plane_sum(0), plane_sum(1)]
    blank = jnp.zeros((WIDTH, SLOT - TALL), F32)
    for z in range(ROWS):
        mine = slice(z * TALL, (z + 1) * TALL)
        m.zout[z] = jnp.concatenate([halves[0][:, mine], blank, halves[1][:, mine], blank], axis=1)

    def to_homes(z, carry):
        send_or_copy(
            at.is_home(z),
            m.zout.at[z],
            m.hin.at[e, at.zz],
            send.dz.at[z],
            recv.dz.at[e * 4 + at.zz],
            at.home(z),
        )
        return carry

    lax.fori_loop(0, ROWS, to_homes, 0)

    def proj_arrived(n, total):
        arrived(m.r5.at[n], recv.p1.at[n])
        return total + m.r5[n]

    m.v5[...] = lax.fori_loop(1, COLS, proj_arrived, m.proj[pl.ds(pl.multiple_of(at.c * 8, 8), 8), :])

    def proj_to_homes(z, carry):
        slot = e * 4 + at.zz
        send_or_copy(at.is_home(z), m.v5, m.r6.at[slot], send.p2.at[z], recv.p2.at[slot], at.home(z))
        return carry

    lax.fori_loop(0, ROWS, proj_to_homes, 0)

    def share_arrived(n, total):
        arrived(m.r6.at[n], recv.p2.at[n])
        return total + m.r6[n]

    m.v6[...] = lax.fori_loop(0, 8, share_arrived, jnp.zeros((8, 4 * HD), F32))
    own_rows = rows_of(proj_out, at.c)
    pltpu.make_async_copy(m.v6, own_rows, recv.p3.at[0]).start()

    def spread(n, carry):
        remote(m.v6, own_rows, send.p3.at[n], recv.p3.at[n], at.plane(n)).start()
        return carry

    lax.fori_loop(1, COLS, spread, 0)

    for core in range(2):
        for zz in range(4):
            arrived(m.hin.at[core, zz], recv.dz.at[core * 4 + zz])
        lanes = slice(core * PAIR, (core + 1) * PAIR)
        h_sum[:, lanes] = (m.hin[core, 0] + m.hin[core, 1]) + (m.hin[core, 2] + m.hin[core, 3])
    exchange_arrived(land_u, recv.u)
    exchange_arrived(land_a, recv.a)

    def out_arrived(n, carry):
        arrived(rows_of(proj_out, lax.rem(at.c - n + COLS, COLS)), recv.p3.at[n])
        return carry

    lax.fori_loop(0, COLS, out_arrived, 0)

    def column_sent(n, carry):
        for hh in range(2):
            arrived(m.bias.at[0, 0], send.plane.at[hh, n])
            arrived(m.d_bias.at[0, 0], send.d_plane.at[hh, n])
        arrived(m.v5, send.p1.at[n])
        arrived(m.v6, send.p3.at[n])
        return carry

    lax.fori_loop(1, COLS, column_sent, 0)

    def column_group_sent(n, carry):
        @pl.when(jnp.logical_not(at.is_worker(lax.div(n, 4), lax.rem(n, 4))))
        def _():
            arrived(m.zpack.at[0], send.z.at[n])

        @pl.when(jnp.logical_not(at.is_home(n)))
        def _():
            arrived(m.zout.at[0], send.dz.at[n])
            arrived(m.v5, send.p2.at[n])

        return carry

    lax.fori_loop(0, 8, column_group_sent, 0)
    for hh in range(2):
        arrived(m.bias.at[0], send.partner.at[hh])
        arrived(m.d_bias.at[0], send.back.at[hh])
    exchange_sent(at, m.m1, send.in1)
    exchange_sent(at, m.m2, send.in2)
    exchange_sent(at, m.out_u, send.u)
    exchange_sent(at, m.out_a, send.a)


def finish_kernel(
    land_u, land_a, proj_in, h_sum, unit, rstd, gain, w_bias, update, pair_grad, proj_out, w_rep, split, share
):
    proj_out[...] = proj_in[...]
    update[...] = land_u[:, :PART, :].astype(F32).reshape(TALL, WIDTH, C).astype(BF16)
    share[...] = land_a[:, :PART, :].astype(F32).reshape(TALL, WIDTH, C)
    w_rep[...] = repeat_heads(w_bias)
    total = h_sum[...]
    for n in range(3):
        term = total.astype(BF16).astype(F32)
        split[n * WIDTH : (n + 1) * WIDTH, :] = term
        total = total - term

    def rows(n, carry):
        terms = split[...].astype(BF16)
        for inner in range(8):
            i = n * 8 + inner
            parts = lax.dot_general(terms, only_row(w_rep[...], i), NT, preferred_element_type=F32)
            grad = (parts[2 * WIDTH :] + parts[WIDTH : 2 * WIDTH]) + parts[:WIDTH]
            result = norm_backward(grad * gain[...], unit[i], rstd[i])
            pair_grad[i] = (share[i] + result).astype(BF16)
        return carry

    lax.fori_loop(0, TALL // 8, rows, 0)


def vmem(count):
    return [pl.BlockSpec(memory_space=pltpu.VMEM)] * count


def shards(
    pair_act, cotangent, ln_gain, ln_shift, w_proj, gate_bias, w_bias, w_out, residue_mask, valid_length
):
    any_space = pl.BlockSpec(memory_space=pl.ANY)
    positions = lax.axis_index("col") * WIDTH + lax.iota(jnp.int32, WIDTH)
    flags = jnp.where(positions < valid_length[0], residue_mask, 0).astype(F32)
    gain = ln_gain.reshape(1, C)
    sems = [pltpu.SemaphoreType.DMA(shape) for shape in MAIN_SEMS.values()]
    landing = jax.ShapeDtypeStruct((COLS, PADDED, C), BF16)
    block = jax.ShapeDtypeStruct(pair_act.shape, F32)
    proj_shape = jax.ShapeDtypeStruct((C, 4 * HD), F32)
    land_u, land_a, proj, h_sum, unit, rstd = pl.pallas_call(
        main_kernel,
        out_shape=[
            landing,
            landing,
            proj_shape,
            jax.ShapeDtypeStruct((WIDTH, H * SLOT), F32),
            block,
            block,
        ],
        in_specs=vmem(MAIN_IN),
        out_specs=[any_space] * 3 + vmem(3),
        scratch_shapes=[pltpu.VMEM(shape, dtype) for shape, dtype in MAIN_SCRATCH.values()] + sems + sems,
        compiler_params=pltpu.CompilerParams(
            collective_id=0, has_side_effects=True, vmem_limit_bytes=VMEM_LIMIT
        ),
        name="main",
    )(
        pair_act,
        cotangent,
        jnp.broadcast_to(flags[:, None], (WIDTH, C)),
        gain,
        ln_shift.reshape(1, C),
        w_proj,
        gate_bias.reshape(1, HD),
        w_bias,
        w_out,
    )
    result = jax.ShapeDtypeStruct(pair_act.shape, BF16)
    return pl.pallas_call(
        finish_kernel,
        out_shape=[result, result, proj_shape],
        in_specs=vmem(8),
        out_specs=vmem(3),
        scratch_shapes=[
            pltpu.VMEM((C, H * SLOT), BF16),
            pltpu.VMEM((3 * WIDTH, H * SLOT), F32),
            pltpu.VMEM(pair_act.shape, F32),
        ],
        compiler_params=pltpu.CompilerParams(vmem_limit_bytes=VMEM_LIMIT),
        name="finish",
    )(land_u, land_a, proj, h_sum, unit, rstd, gain, w_bias)


def solution(mesh):
    return jax.shard_map(
        shards,
        mesh=mesh,
        in_specs=(
            P(("complex", "row"), "col", None),
            P(("complex", "row"), "col", None),
            P(),
            P(),
            P(),
            P(),
            P(),
            P(),
            P(("complex", "col")),
            P("complex"),
        ),
        out_specs=(
            P(("complex", "row"), "col", None),
            P(("complex", "row"), "col", None),
            P("complex", None),
        ),
        check_vma=False,
    )
```

```python
import jax
import jax.numpy as jnp
from jax import lax
from jax.experimental import pallas as pl
from jax.experimental.pallas import tpu as pltpu
from jax.sharding import PartitionSpec as P

MESH = pl.DeviceIdType.MESH
F32 = jnp.float32
BF16 = jnp.bfloat16
N = 384
C = 128
H = 4
DH = 32
HD = H * DH
COLS = 16
ROWS = 8
WIDTH = N // COLS
TALL = N // ROWS
OWN = 3
PART = OWN * WIDTH
PADDED = 80
SLOT = 64
PAIR = 2 * SLOT
SCALE = DH ** (-0.5)
VMEM_LIMIT = 48 * 1024 * 1024
NT = (((1,), (1,)), ((), ()))


class Place:
    def __init__(self):
        self.e = lax.axis_index("complex")
        self.z = lax.axis_index("row")
        self.c = lax.axis_index("col")
        self.part = lax.rem(self.z, 2)
        self.zz = lax.div(self.z, 2)
        self.stays = self.part == self.e
        self.y = lax.div(self.c, 4)
        self.x = lax.rem(self.c, 4)
        self.f = self.x * (1 - self.e) + self.y * self.e
        self.g = self.y * (1 - self.e) + self.x * self.e
        self.row0 = (self.zz * 2 + self.e) * TALL + self.c * OWN

    def swapped(self, c):
        return (self.part, self.zz * 2 + self.e, c)

    def col(self, f, g):
        return lax.rem(f, 4) * (1 + 3 * self.e) + lax.rem(g, 4) * (4 - 3 * self.e)

    def fpeer(self, n):
        return (self.e, self.z, self.col(self.f + n, self.g))

    def gpeer(self, n):
        return (self.e, self.z, self.col(self.f, self.g + n))

    def plane(self, n):
        return (self.e, self.z, lax.rem(self.c + n, COLS))

    def partner(self):
        return (1 - self.e, self.z, self.c)

    def worker(self, core, zz):
        return (core, zz * 2 + self.e, self.c)

    def home(self, z):
        return (self.part, z, self.c)

    def is_worker(self, core, zz):
        return jnp.logical_and(self.stays, jnp.logical_and(core == self.e, zz == self.zz))

    def is_home(self, z):
        return jnp.logical_and(self.stays, z == self.z)


def remote(src, dst, send, recv, device):
    return pltpu.make_async_remote_copy(
        src_ref=src, dst_ref=dst, send_sem=send, recv_sem=recv, device_id=device, device_id_type=MESH
    )


def arrived(ref, sem):
    pltpu.make_async_copy(ref, ref, sem).wait()


def send_or_copy(here, src, dst, send, recv, device):
    @pl.when(here)
    def _():
        pltpu.make_async_copy(src, dst, recv).start()

    @pl.when(jnp.logical_not(here))
    def _():
        remote(src, dst, send, recv, device).start()


def greet(device):
    pl.semaphore_signal(pltpu.get_barrier_semaphore(), inc=1, device_id=device, device_id_type=MESH)


def greet_all(at):
    def plane(n, carry):
        greet(at.plane(n))
        return carry

    lax.fori_loop(1, COLS, plane, 0)

    def worker(n, carry):
        core, zz = lax.div(n, 4), lax.rem(n, 4)

        @pl.when(jnp.logical_not(at.is_worker(core, zz)))
        def _():
            greet(at.worker(core, zz))

        return carry

    lax.fori_loop(0, 8, worker, 0)

    def home(n, carry):
        greet(at.home(n * 2 + 1 - at.e))
        return carry

    lax.fori_loop(0, 4, home, 0)

    @pl.when(jnp.logical_not(at.stays))
    def _():
        def column(n, carry):
            greet(at.swapped(n))
            return carry

        lax.fori_loop(0, COLS, column, 0)

    return jnp.where(at.stays, COLS - 1 + 7 + 4, COLS - 1 + 8 + 4 + COLS)


def exchange_start(at, source, landing, send, recv):
    def column(n, carry):
        t = lax.rem(at.c + n, COLS)
        here = jnp.logical_and(n == 0, at.stays)
        send_or_copy(here, source.at[t], landing.at[at.c], send.at[t], recv.at[at.c], at.swapped(t))
        return carry

    lax.fori_loop(0, COLS, column, 0)


def exchange_arrived(landing, recv):
    def column(n, carry):
        arrived(landing.at[n], recv.at[n])
        return carry

    lax.fori_loop(0, COLS, column, 0)


def exchange_sent(at, source, send):
    def column(n, carry):
        t = lax.rem(at.c + n, COLS)

        @pl.when(jnp.logical_or(n > 0, jnp.logical_not(at.stays)))
        def _():
            arrived(source.at[t], send.at[t])

        return carry

    lax.fori_loop(0, COLS, column, 0)


def repeat_heads(w_bias_t):
    wide = jnp.concatenate([w_bias_t[...].astype(F32), jnp.zeros((C - H, C), F32)], axis=0).T
    lane = lax.div(lax.broadcasted_iota(jnp.int32, (C, H * SLOT), 1), SLOT)
    total = jnp.zeros((C, H * SLOT), F32)
    for h in range(H):
        total = jnp.where(lane == h, wide[:, h : h + 1], total)
    return total.astype(BF16)


def only_row(repeated, i):
    lane = lax.rem(lax.broadcasted_iota(jnp.int32, (C, H * SLOT), 1), SLOT)
    return repeated * (lane == i).astype(F32).astype(BF16)


def standardize(values):
    centre = values - jnp.mean(values, axis=-1, keepdims=True)
    inverse = lax.rsqrt(jnp.mean(centre * centre, axis=-1, keepdims=True) + 1e-5)
    return centre * inverse, jnp.broadcast_to(inverse, values.shape)


def norm_backward(grad, unit, inverse):
    mean_grad = jnp.mean(grad, axis=-1, keepdims=True)
    mean_cross = jnp.mean(grad * unit, axis=-1, keepdims=True)
    return inverse * (grad - mean_grad - unit * mean_cross)


MAIN_SCRATCH = dict(
    m1=((COLS, PADDED, C), BF16),
    m2=((COLS, PADDED, C), BF16),
    in1=((COLS, PADDED, C), BF16),
    in2=((COLS, PADDED, C), BF16),
    flags=((WIDTH, C), F32),
    w_proj_t=((3 * HD, C), BF16),
    w_rep=((C, H * SLOT), BF16),
    home_rows=((TALL, WIDTH, C), F32),
    zpack=((2, WIDTH, PAIR), F32),
    zin=((ROWS, WIDTH, PAIR), F32),
    bias=((H, COLS, WIDTH, N), F32),
    d_bias=((H, COLS, WIDTH, N), F32),
    d_other=((2, COLS, WIDTH, N), F32),
    stage_far=((4, WIDTH, N), F32),
    d_far=((2, 3, 4 * WIDTH, N), BF16),
    d_far_in=((2, 3, 4 * WIDTH, N), BF16),
    d_near=((2, 4, WIDTH, N), F32),
    d_near_in=((2, 3, WIDTH, N), F32),
    zout=((ROWS, WIDTH, PAIR), F32),
    hin=((2, 4, WIDTH, PAIR), F32),
    mask=((COLS, WIDTH, C), F32),
    row_mask=((OWN, 1, C), F32),
    normed=((OWN, N, C), BF16),
    unit=((OWN, N, C), F32),
    rstd=((OWN, N, C), F32),
    q=((OWN, N, C), BF16),
    k=((OWN, N, C), BF16),
    v=((OWN, N, C), BF16),
    d=((OWN, N, C), BF16),
    q_t=((OWN, C, N), BF16),
    k_t=((OWN, C, N), BF16),
    v_t=((OWN, C, N), BF16),
    d_t=((OWN, C, N), BF16),
    gate=((OWN, N, C), F32),
    dgate=((OWN, N, C), F32),
    att_t=((OWN, HD, N), F32),
    att=((OWN, N, HD), F32),
    d_proj=((OWN, N, 4 * HD), BF16),
    dq_t=((OWN, HD, N), F32),
    dk=((OWN, N, HD), F32),
    dv=((OWN, N, HD), F32),
    proj=((C, 4 * HD), F32),
    r5=((COLS, 8, 4 * HD), F32),
    v5=((8, 4 * HD), F32),
    r6=((8, 8, 4 * HD), F32),
    v6=((8, 4 * HD), F32),
    stage_u=((COLS, PADDED, C), F32),
    stage_a=((COLS, PADDED, C), F32),
    out_u=((COLS, PADDED, C), BF16),
    out_a=((COLS, PADDED, C), BF16),
)
MAIN_SEMS = dict(
    in1=(COLS,),
    in2=(COLS,),
    z=(8,),
    near=(2, 3),
    far=(2, 4, 3),
    partner=(2,),
    back=(2,),
    d_far=(2, 3),
    d_near=(2, 3),
    dz=(8,),
    p1=(COLS,),
    p2=(8,),
    p3=(COLS,),
    u=(COLS,),
    a=(COLS,),
)
MAIN_IN = 10
MAIN_OUT = 6


class Names:
    pass


def main_kernel(*refs):
    (pair, cot, residues, length, gain, shift, w_proj, gate_bias, w_bias_t, w_out) = refs[:MAIN_IN]
    (land_u, land_a, proj_out, h_sum, home_unit, home_rstd) = refs[MAIN_IN : MAIN_IN + MAIN_OUT]
    rest = refs[MAIN_IN + MAIN_OUT :]
    m, send, recv = Names(), Names(), Names()
    for name, ref in zip(MAIN_SCRATCH, rest):
        setattr(m, name, ref)
    rest = rest[len(MAIN_SCRATCH) :]
    for name, ref in zip(MAIN_SEMS, rest):
        setattr(send, name, ref)
    for name, ref in zip(MAIN_SEMS, rest[len(MAIN_SEMS) :]):
        setattr(recv, name, ref)
    at = Place()
    e = at.e
    count = greet_all(at)

    sublane = lax.broadcasted_iota(jnp.int32, (WIDTH, WIDTH), 0)
    lane = lax.broadcasted_iota(jnp.int32, (WIDTH, WIDTH), 1)
    valid = jnp.where(lane + at.c * WIDTH < length[0], residues[...], 0).astype(F32)
    valid = jnp.sum(jnp.where(lane == sublane, valid, 0.0), axis=1, keepdims=True)
    m.flags[...] = jnp.broadcast_to(valid, (WIDTH, C))
    lane = lax.broadcasted_iota(jnp.int32, (8, C), 1)
    packed_flags = jnp.where(
        lane == 0, m.flags[0:8, :], jnp.where(lane == 1, m.flags[8:16, :], m.flags[16:24, :])
    )
    pad = jnp.zeros((COLS, PADDED - PART, C), F32)
    m.m1[...] = jnp.concatenate(
        [
            pair[...].astype(F32).reshape(COLS, PART, C),
            jnp.broadcast_to(packed_flags[None], (COLS, PADDED - PART, C)),
        ],
        axis=1,
    ).astype(BF16)
    m.m2[...] = jnp.concatenate([cot[...].astype(F32).reshape(COLS, PART, C), pad], axis=1).astype(BF16)

    m.w_rep[...] = repeat_heads(w_bias_t)
    unit, inverse = standardize(pair[...].astype(F32).reshape(TALL * WIDTH, C))
    home_unit[...] = unit.reshape(TALL, WIDTH, C)
    home_rstd[...] = inverse.reshape(TALL, WIDTH, C)
    m.home_rows[...] = (unit * gain[...] + shift[...]).reshape(TALL, WIDTH, C)

    def home_bias(n, total):
        for i in range(8):
            rows = m.home_rows[n * 8 + i].astype(BF16)
            total = total + jnp.dot(rows, only_row(m.w_rep[...], n * 8 + i), preferred_element_type=F32)
        return total

    packed = lax.fori_loop(0, TALL // 8, home_bias, jnp.zeros((WIDTH, H * SLOT), F32))
    negative = (m.flags[...] - 1.0) * 1e9
    m.zpack[0] = packed[:, :PAIR] + negative
    m.zpack[1] = packed[:, PAIR:] + negative

    pl.semaphore_wait(pltpu.get_barrier_semaphore(), count)

    def to_workers(n, carry):
        core, zz = lax.div(n, 4), lax.rem(n, 4)
        send_or_copy(
            at.is_worker(core, zz),
            m.zpack.at[core],
            m.zin.at[at.z],
            send.z.at[n],
            recv.z.at[at.z],
            at.worker(core, zz),
        )
        return carry

    lax.fori_loop(0, 8, to_workers, 0)
    exchange_start(at, m.m1, m.in1, send.in1, recv.in1)
    exchange_start(at, m.m2, m.in2, send.in2, recv.in2)

    m.w_proj_t[...] = w_proj[:, : 3 * HD].astype(F32).T.astype(BF16)
    m.d_bias[...] = jnp.zeros_like(m.d_bias)
    m.dk[...] = jnp.zeros_like(m.dk)
    m.dv[...] = jnp.zeros_like(m.dv)
    exchange_arrived(m.in1, recv.in1)

    for s in range(OWN):
        values = m.in1[:, s * WIDTH : (s + 1) * WIDTH, :].astype(F32).reshape(N, C)
        unit, inverse = standardize(values)
        m.unit[s] = unit
        m.rstd[s] = inverse
        m.normed[s] = (unit * gain[...] + shift[...]).astype(BF16)

    def bias_block(hh, a, b):
        return m.bias.at[e * 2 + hh, at.col(at.f - a + 4, at.g - b + 4)]

    def to_far(hh, a):
        block = bias_block(hh, a, 0)
        for n in (1, 2, 3):
            remote(block, block, send.far.at[hh, a, n - 1], recv.far.at[hh, a, n - 1], at.gpeer(n)).start()

    def forward(hh):
        for n in (1, 2, 3):
            arrived(bias_block(hh, n, 0), recv.near.at[hh, n - 1])
            to_far(hh, n)

    for z in range(ROWS):
        arrived(m.zin.at[z], recv.z.at[z])
    for hh in range(2):
        head = e * 2 + hh
        m.bias[head, at.c] = jnp.concatenate(
            [m.zin[z][:, hh * SLOT : hh * SLOT + TALL] for z in range(ROWS)], axis=1
        )
        mine = m.bias.at[head, at.c]
        for n in (1, 2, 3):
            remote(mine, mine, send.near.at[hh, n - 1], recv.near.at[hh, n - 1], at.fpeer(n)).start()
        to_far(hh, 0)

    for s in range(OWN):
        rows = m.normed[s]
        flat = jnp.dot(rows, w_proj[...], preferred_element_type=F32)
        m.q[s] = (flat[:, :HD] * SCALE).astype(BF16)
        m.k[s] = flat[:, HD : 2 * HD].astype(BF16)
        m.v[s] = flat[:, 2 * HD : 3 * HD].astype(BF16)
        m.gate[s] = jax.nn.sigmoid(flat[:, 3 * HD :] + gate_bias[...])
        flat_t = lax.dot_general(m.w_proj_t[...], rows, NT, preferred_element_type=F32)
        m.q_t[s] = (flat_t[:HD] * SCALE).astype(BF16)
        m.k_t[s] = flat_t[HD : 2 * HD].astype(BF16)
        m.v_t[s] = flat_t[2 * HD : 3 * HD].astype(BF16)

    forward(0)
    forward(1)
    exchange_arrived(m.in2, recv.in2)
    tiles = m.in1[:, PART:, :].astype(F32)
    for t in range(3):
        rows = jnp.broadcast_to(tiles[:, :, t : t + 1], (COLS, 8, C))
        m.mask[:, t * 8 : (t + 1) * 8, :] = rows
    for s in range(OWN):
        values = m.in2[:, s * WIDTH : (s + 1) * WIDTH, :].astype(F32).reshape(N, C)
        row = at.row0 + s
        own_mask = m.mask[lax.div(row, WIDTH), pl.ds(lax.rem(row, WIDTH), 1), :]
        m.row_mask[s] = own_mask
        pair_mask = m.mask[...].reshape(N, C) * own_mask
        d_out = jnp.where(pair_mask > 0, values, 0.0).astype(BF16)
        d_gated = lax.dot_general(d_out, w_out[...], NT, preferred_element_type=F32)
        gates = m.gate[s]
        d_attn = d_gated * gates
        m.d[s] = d_attn.astype(BF16)
        m.d_t[s] = d_attn.T.astype(BF16)
        m.dgate[s] = d_attn * (1.0 - gates)

    def own_bias_arrived(hh):
        for a in range(4):
            for n in (1, 2, 3):
                arrived(bias_block(hh, a, n), recv.far.at[hh, a, n - 1])
        whole = m.bias.at[e * 2 + hh]
        remote(whole, whole, send.partner.at[hh], recv.partner.at[hh], at.partner()).start()

    def other_bias_arrived(hh):
        arrived(m.bias.at[(1 - e) * 2 + hh], recv.partner.at[hh])

    def attend(h):
        here = pl.ds(pl.multiple_of(h * DH, DH), DH)
        lane = lax.div(lax.broadcasted_iota(jnp.int32, (C, C), 1), DH)
        row = lax.div(lax.broadcasted_iota(jnp.int32, (C, C), 0), DH)
        by_lane = (lane == h).astype(F32).astype(BF16)
        by_row = (row == h).astype(F32).astype(BF16)

        def one_row(s, carry):
            keys, values = m.k[s], m.v[s]
            keys_t, values_t = m.k_t[s, here, :], m.v_t[s, here, :]
            dk_sum = dv_sum = None
            for n in range(3):
                lanes = slice(n * C, (n + 1) * C)
                scores = jnp.dot(keys, m.q_t[s, :, lanes] * by_row, preferred_element_type=F32)
                scores = scores + m.bias[h, :, :, lanes].reshape(N, C)
                exponent = jnp.exp(scores - jnp.max(scores, axis=0, keepdims=True))
                weights = exponent * (1.0 / jnp.sum(exponent, axis=0, keepdims=True))
                weights_b = weights.astype(BF16)
                attended = jnp.dot(values_t, weights_b, preferred_element_type=F32)
                m.att_t[s, here, lanes] = attended
                delta = jnp.sum(attended * m.d_t[s, here, lanes].astype(F32), axis=0, keepdims=True)
                d_prob = jnp.dot(values, m.d_t[s, :, lanes] * by_row, preferred_element_type=F32)
                d_score = weights * (d_prob - delta)
                d_score_b = d_score.astype(BF16)
                m.d_bias[h, :, :, lanes] += d_score.reshape(COLS, WIDTH, C)
                m.dq_t[s, here, lanes] = jnp.dot(keys_t, d_score_b, preferred_element_type=F32)
                dv_part = jnp.dot(weights_b, m.d[s, lanes, :] * by_lane, preferred_element_type=F32)
                dk_part = jnp.dot(d_score_b, m.q[s, lanes, :] * by_lane, preferred_element_type=F32)
                dv_sum = dv_part if dv_sum is None else dv_sum + dv_part
                dk_sum = dk_part if dk_sum is None else dk_sum + dk_part
            m.dk[s] += dk_sum
            m.dv[s] += dv_sum
            return carry

        lax.fori_loop(0, OWN, one_row, 0)

    def to_other(hh):
        head = (1 - e) * 2 + hh
        remote(m.d_bias.at[head], m.d_other.at[hh], send.back.at[hh], recv.back.at[hh], at.partner()).start()

    def scatter_far(hh):
        head = e * 2 + hh
        arrived(m.d_other.at[hh], recv.back.at[hh])
        for n in (1, 2, 3, 0):
            for f in range(4):
                column = at.col(f, at.g + n)
                both = m.d_bias[head, column] + m.d_other[hh, column]
                if n == 0:
                    m.d_near[hh, f] = both
                else:
                    m.stage_far[f] = both
            if n > 0:
                m.d_far[hh, n - 1] = m.stage_far[...].reshape(4 * WIDTH, N).astype(BF16)
                remote(
                    m.d_far.at[hh, n - 1],
                    m.d_far_in.at[hh, n - 1],
                    send.d_far.at[hh, n - 1],
                    recv.d_far.at[hh, n - 1],
                    at.gpeer(n),
                ).start()

    def scatter_near(hh):
        for n in range(3):
            arrived(m.d_far_in.at[hh, n], recv.d_far.at[hh, n])
        far = (m.d_far_in[hh, 0].astype(F32) + m.d_far_in[hh, 1].astype(F32)) + m.d_far_in[hh, 2].astype(F32)
        m.d_near[hh] += far.reshape(4, WIDTH, N)
        for n in (1, 2, 3):
            remote(
                m.d_near.at[hh, lax.rem(at.f + n, 4)],
                m.d_near_in.at[hh, n - 1],
                send.d_near.at[hh, n - 1],
                recv.d_near.at[hh, n - 1],
                at.fpeer(n),
            ).start()

    def plane_sum(hh):
        for n in range(3):
            arrived(m.d_near_in.at[hh, n], recv.d_near.at[hh, n])
        return (m.d_near[hh, at.f] + m.d_near_in[hh, 0]) + (m.d_near_in[hh, 1] + m.d_near_in[hh, 2])

    own_bias_arrived(0)
    attend(e * 2)
    own_bias_arrived(1)
    other_bias_arrived(0)
    attend(2 - e * 2)
    to_other(0)
    other_bias_arrived(1)
    attend(3 - e * 2)
    to_other(1)
    scatter_far(0)
    attend(e * 2 + 1)
    scatter_far(1)
    scatter_near(0)

    for s in range(OWN):
        attended = m.att_t[s].T
        m.att[s] = attended
        d_proj = jnp.concatenate(
            [m.dq_t[s].T * SCALE, m.dk[s], m.dv[s], m.dgate[s] * attended], axis=1
        ).astype(BF16)
        m.d_proj[s] = d_proj
        normed_t = m.normed[s].astype(F32).T.astype(BF16)
        share = jnp.dot(normed_t, d_proj, preferred_element_type=F32)
        if s == 0:
            m.proj[...] = share
        else:
            m.proj[...] += share

    def rows_of(ref, c):
        return ref.at[pl.ds(pl.multiple_of(c * 8, 8), 8), :]

    def scatter_proj(n, carry):
        t = lax.rem(at.c + n, COLS)
        remote(rows_of(m.proj, t), m.r5.at[n], send.p1.at[n], recv.p1.at[n], at.plane(n)).start()
        return carry

    lax.fori_loop(1, COLS, scatter_proj, 0)
    scatter_near(1)

    for s in range(OWN):
        gated = (m.gate[s] * m.att[s]).astype(BF16)
        pair_mask = m.mask[...].reshape(N, C) * m.row_mask[s]
        update = jnp.dot(gated, w_out[...], preferred_element_type=F32) * pair_mask
        m.stage_u[:, s * WIDTH : (s + 1) * WIDTH, :] = update.reshape(COLS, WIDTH, C)
    m.stage_u[:, PART:, :] = pad
    m.out_u[...] = m.stage_u[...].astype(BF16)
    exchange_start(at, m.out_u, land_u, send.u, recv.u)

    halves = [plane_sum(0), plane_sum(1)]
    blank = jnp.zeros((WIDTH, SLOT - TALL), F32)
    for z in range(ROWS):
        mine = slice(z * TALL, (z + 1) * TALL)
        m.zout[z] = jnp.concatenate([halves[0][:, mine], blank, halves[1][:, mine], blank], axis=1)

    def to_homes(z, carry):
        send_or_copy(
            at.is_home(z),
            m.zout.at[z],
            m.hin.at[e, at.zz],
            send.dz.at[z],
            recv.dz.at[e * 4 + at.zz],
            at.home(z),
        )
        return carry

    lax.fori_loop(0, ROWS, to_homes, 0)

    for s in range(OWN):
        d_normed = lax.dot_general(m.d_proj[s], w_proj[...], NT, preferred_element_type=F32)
        result = norm_backward(d_normed * gain[...], m.unit[s], m.rstd[s])
        m.stage_a[:, s * WIDTH : (s + 1) * WIDTH, :] = result.reshape(COLS, WIDTH, C)
    m.stage_a[:, PART:, :] = pad
    m.out_a[...] = m.stage_a[...].astype(BF16)
    exchange_start(at, m.out_a, land_a, send.a, recv.a)

    def proj_arrived(n, total):
        arrived(m.r5.at[n], recv.p1.at[n])
        return total + m.r5[n]

    m.v5[...] = lax.fori_loop(1, COLS, proj_arrived, m.proj[pl.ds(pl.multiple_of(at.c * 8, 8), 8), :])

    def proj_to_homes(z, carry):
        slot = e * 4 + at.zz
        send_or_copy(at.is_home(z), m.v5, m.r6.at[slot], send.p2.at[z], recv.p2.at[slot], at.home(z))
        return carry

    lax.fori_loop(0, ROWS, proj_to_homes, 0)

    def share_arrived(n, total):
        arrived(m.r6.at[n], recv.p2.at[n])
        return total + m.r6[n]

    m.v6[...] = lax.fori_loop(0, 8, share_arrived, jnp.zeros((8, 4 * HD), F32))
    own_rows = rows_of(proj_out, at.c)
    pltpu.make_async_copy(m.v6, own_rows, recv.p3.at[0]).start()

    def spread(n, carry):
        remote(m.v6, own_rows, send.p3.at[n], recv.p3.at[n], at.plane(n)).start()
        return carry

    lax.fori_loop(1, COLS, spread, 0)

    for core in range(2):
        for zz in range(4):
            arrived(m.hin.at[core, zz], recv.dz.at[core * 4 + zz])
        lanes = slice(core * PAIR, (core + 1) * PAIR)
        h_sum[:, lanes] = (m.hin[core, 0] + m.hin[core, 1]) + (m.hin[core, 2] + m.hin[core, 3])
    exchange_arrived(land_u, recv.u)
    exchange_arrived(land_a, recv.a)

    def out_arrived(n, carry):
        arrived(rows_of(proj_out, lax.rem(at.c - n + COLS, COLS)), recv.p3.at[n])
        return carry

    lax.fori_loop(0, COLS, out_arrived, 0)

    def column_sent(n, carry):
        arrived(m.v5, send.p1.at[n])
        arrived(m.v6, send.p3.at[n])
        return carry

    lax.fori_loop(1, COLS, column_sent, 0)

    def column_group_sent(n, carry):
        @pl.when(jnp.logical_not(at.is_worker(lax.div(n, 4), lax.rem(n, 4))))
        def _():
            arrived(m.zpack.at[0], send.z.at[n])

        @pl.when(jnp.logical_not(at.is_home(n)))
        def _():
            arrived(m.zout.at[0], send.dz.at[n])
            arrived(m.v5, send.p2.at[n])

        return carry

    lax.fori_loop(0, 8, column_group_sent, 0)
    for hh in range(2):
        for n in range(3):
            arrived(m.bias.at[0, 0], send.near.at[hh, n])
            for a in range(4):
                arrived(m.bias.at[0, 0], send.far.at[hh, a, n])
            arrived(m.d_far.at[0, 0], send.d_far.at[hh, n])
            arrived(m.d_near.at[0, 0], send.d_near.at[hh, n])
        arrived(m.bias.at[0], send.partner.at[hh])
        arrived(m.d_bias.at[0], send.back.at[hh])
    exchange_sent(at, m.m1, send.in1)
    exchange_sent(at, m.m2, send.in2)
    exchange_sent(at, m.out_u, send.u)
    exchange_sent(at, m.out_a, send.a)


def finish_kernel(
    land_u, land_a, proj_in, h_sum, unit, rstd, gain, w_bias_t, update, pair_grad, proj_out, w_rep, split, share
):
    proj_out[...] = proj_in[...]
    update[...] = land_u[:, :PART, :].astype(F32).reshape(TALL, WIDTH, C).astype(BF16)
    share[...] = land_a[:, :PART, :].astype(F32).reshape(TALL, WIDTH, C)
    w_rep[...] = repeat_heads(w_bias_t)
    total = h_sum[...]
    for n in range(3):
        term = total.astype(BF16).astype(F32)
        split[n * WIDTH : (n + 1) * WIDTH, :] = term
        total = total - term

    def rows(n, carry):
        terms = split[...].astype(BF16)
        for inner in range(8):
            i = n * 8 + inner
            parts = lax.dot_general(terms, only_row(w_rep[...], i), NT, preferred_element_type=F32)
            grad = (parts[2 * WIDTH :] + parts[WIDTH : 2 * WIDTH]) + parts[:WIDTH]
            result = norm_backward(grad * gain[...], unit[i], rstd[i])
            pair_grad[i] = (share[i] + result).astype(BF16)
        return carry

    lax.fori_loop(0, TALL // 8, rows, 0)


def vmem(count):
    return [pl.BlockSpec(memory_space=pltpu.VMEM)] * count


def shards(
    pair_act, cotangent, ln_gain, ln_shift, w_proj, gate_bias, w_bias, w_out, residue_mask, valid_length
):
    any_space = pl.BlockSpec(memory_space=pl.ANY)
    gain = ln_gain.reshape(1, C)
    sems = [pltpu.SemaphoreType.DMA(shape) for shape in MAIN_SEMS.values()]
    landing = jax.ShapeDtypeStruct((COLS, PADDED, C), BF16)
    block = jax.ShapeDtypeStruct(pair_act.shape, F32)
    proj_shape = jax.ShapeDtypeStruct((C, 4 * HD), F32)
    land_u, land_a, proj, h_sum, unit, rstd = pl.pallas_call(
        main_kernel,
        out_shape=[
            landing,
            landing,
            proj_shape,
            jax.ShapeDtypeStruct((WIDTH, H * SLOT), F32),
            block,
            block,
        ],
        in_specs=vmem(3) + [pl.BlockSpec(memory_space=pltpu.SMEM)] + vmem(MAIN_IN - 4),
        out_specs=[any_space] * 3 + vmem(3),
        scratch_shapes=[pltpu.VMEM(shape, dtype) for shape, dtype in MAIN_SCRATCH.values()] + sems + sems,
        compiler_params=pltpu.CompilerParams(
            collective_id=0, has_side_effects=True, vmem_limit_bytes=VMEM_LIMIT
        ),
        name="main",
    )(
        pair_act,
        cotangent,
        residue_mask.reshape(1, WIDTH),
        valid_length,
        gain,
        ln_shift.reshape(1, C),
        w_proj,
        gate_bias.reshape(1, HD),
        w_bias.T,
        w_out,
    )
    result = jax.ShapeDtypeStruct(pair_act.shape, BF16)
    return pl.pallas_call(
        finish_kernel,
        out_shape=[result, result, proj_shape],
        in_specs=vmem(8),
        out_specs=vmem(3),
        scratch_shapes=[
            pltpu.VMEM((C, H * SLOT), BF16),
            pltpu.VMEM((3 * WIDTH, H * SLOT), F32),
            pltpu.VMEM(pair_act.shape, F32),
        ],
        compiler_params=pltpu.CompilerParams(vmem_limit_bytes=VMEM_LIMIT),
        name="finish",
    )(land_u, land_a, proj, h_sum, unit, rstd, gain, w_bias.T)


def solution(mesh):
    return jax.shard_map(
        shards,
        mesh=mesh,
        in_specs=(
            P(("complex", "row"), "col", None),
            P(("complex", "row"), "col", None),
            P(),
            P(),
            P(),
            P(),
            P(),
            P(),
            P(("complex", "col")),
            P("complex"),
        ),
        out_specs=(
            P(("complex", "row"), "col", None),
            P(("complex", "row"), "col", None),
            P("complex", None),
        ),
        check_vma=False,
    )
```

```python
import jax
import jax.numpy as jnp
from jax import lax
from jax.experimental import pallas as pl
from jax.experimental.pallas import tpu as pltpu
from jax.sharding import PartitionSpec as P

MESH = pl.DeviceIdType.MESH
F32 = jnp.float32
BF16 = jnp.bfloat16
N = 384
C = 128
H = 4
DH = 32
HD = H * DH
COLS = 16
ROWS = 8
WIDTH = N // COLS
TALL = N // ROWS
OWN = 3
PART = OWN * WIDTH
PADDED = 80
SLOT = 64
PAIR = 2 * SLOT
SCALE = DH ** (-0.5)
VMEM_LIMIT = 60 * 1024 * 1024
NT = (((1,), (1,)), ((), ()))


class Place:
    def __init__(self):
        self.e = lax.axis_index("complex")
        self.z = lax.axis_index("row")
        self.c = lax.axis_index("col")
        self.part = lax.rem(self.z, 2)
        self.zz = lax.div(self.z, 2)
        self.stays = self.part == self.e
        self.y = lax.div(self.c, 4)
        self.x = lax.rem(self.c, 4)
        self.f = self.x * (1 - self.e) + self.y * self.e
        self.g = self.y * (1 - self.e) + self.x * self.e
        self.row0 = (self.zz * 2 + self.e) * TALL + self.c * OWN

    def swapped(self, c):
        return (self.part, self.zz * 2 + self.e, c)

    def col(self, f, g):
        return lax.rem(f, 4) * (1 + 3 * self.e) + lax.rem(g, 4) * (4 - 3 * self.e)

    def fpeer(self, n):
        return (self.e, self.z, self.col(self.f + n, self.g))

    def gpeer(self, n):
        return (self.e, self.z, self.col(self.f, self.g + n))

    def plane(self, n):
        return (self.e, self.z, lax.rem(self.c + n, COLS))

    def partner(self):
        return (1 - self.e, self.z, self.c)

    def worker(self, core, zz):
        return (core, zz * 2 + self.e, self.c)

    def home(self, z):
        return (self.part, z, self.c)

    def is_worker(self, core, zz):
        return jnp.logical_and(self.stays, jnp.logical_and(core == self.e, zz == self.zz))

    def is_home(self, z):
        return jnp.logical_and(self.stays, z == self.z)


def remote(src, dst, send, recv, device):
    return pltpu.make_async_remote_copy(
        src_ref=src, dst_ref=dst, send_sem=send, recv_sem=recv, device_id=device, device_id_type=MESH
    )


def arrived(ref, sem):
    pltpu.make_async_copy(ref, ref, sem).wait()


def send_or_copy(here, src, dst, send, recv, device):
    @pl.when(here)
    def _():
        pltpu.make_async_copy(src, dst, recv).start()

    @pl.when(jnp.logical_not(here))
    def _():
        remote(src, dst, send, recv, device).start()


def greet(device):
    pl.semaphore_signal(pltpu.get_barrier_semaphore(), inc=1, device_id=device, device_id_type=MESH)


def greet_all(at):
    def plane(n, carry):
        greet(at.plane(n))
        return carry

    lax.fori_loop(1, COLS, plane, 0)

    def worker(n, carry):
        core, zz = lax.div(n, 4), lax.rem(n, 4)

        @pl.when(jnp.logical_not(at.is_worker(core, zz)))
        def _():
            greet(at.worker(core, zz))

        return carry

    lax.fori_loop(0, 8, worker, 0)

    def home(n, carry):
        greet(at.home(n * 2 + 1 - at.e))
        return carry

    lax.fori_loop(0, 4, home, 0)

    @pl.when(jnp.logical_not(at.stays))
    def _():
        def column(n, carry):
            greet(at.swapped(n))
            return carry

        lax.fori_loop(0, COLS, column, 0)

    return jnp.where(at.stays, COLS - 1 + 7 + 4, COLS - 1 + 8 + 4 + COLS)


def exchange_start(at, source, landing, send, recv):
    def column(n, carry):
        t = lax.rem(at.c + n, COLS)
        here = jnp.logical_and(n == 0, at.stays)
        send_or_copy(here, source.at[t], landing.at[at.c], send.at[t], recv.at[at.c], at.swapped(t))
        return carry

    lax.fori_loop(0, COLS, column, 0)


def exchange_arrived(landing, recv):
    def column(n, carry):
        arrived(landing.at[n], recv.at[n])
        return carry

    lax.fori_loop(0, COLS, column, 0)


def exchange_sent(at, source, send):
    def column(n, carry):
        t = lax.rem(at.c + n, COLS)

        @pl.when(jnp.logical_or(n > 0, jnp.logical_not(at.stays)))
        def _():
            arrived(source.at[t], send.at[t])

        return carry

    lax.fori_loop(0, COLS, column, 0)


def repeat_heads(w_bias_t):
    wide = jnp.concatenate([w_bias_t[...].astype(F32), jnp.zeros((C - H, C), F32)], axis=0).T
    lane = lax.div(lax.broadcasted_iota(jnp.int32, (C, H * SLOT), 1), SLOT)
    total = jnp.zeros((C, H * SLOT), F32)
    for h in range(H):
        total = jnp.where(lane == h, wide[:, h : h + 1], total)
    return total.astype(BF16)


def only_row(repeated, i):
    lane = lax.rem(lax.broadcasted_iota(jnp.int32, (C, H * SLOT), 1), SLOT)
    return repeated * (lane == i).astype(F32).astype(BF16)


def standardize(values):
    centre = values - jnp.mean(values, axis=-1, keepdims=True)
    inverse = lax.rsqrt(jnp.mean(centre * centre, axis=-1, keepdims=True) + 1e-5)
    return centre * inverse, jnp.broadcast_to(inverse, values.shape)


def norm_backward(grad, unit, inverse):
    mean_grad = jnp.mean(grad, axis=-1, keepdims=True)
    mean_cross = jnp.mean(grad * unit, axis=-1, keepdims=True)
    return inverse * (grad - mean_grad - unit * mean_cross)


MAIN_SCRATCH = dict(
    pair=((TALL, WIDTH, C), BF16),
    cot=((TALL, WIDTH, C), BF16),
    residues=((1, WIDTH), jnp.int32),
    gain=((1, C), F32),
    shift=((1, C), F32),
    w_proj=((C, 4 * HD), BF16),
    gate_bias=((1, HD), F32),
    w_bias_t=((H, C), BF16),
    w_out=((HD, C), BF16),
    home_unit=((TALL, WIDTH, C), F32),
    home_rstd=((TALL, WIDTH, C), F32),
    scores=((H, OWN, N, N), F32),
    d_prob=((H, OWN, N, N), F32),
    m1=((COLS, PADDED, C), BF16),
    m2=((COLS, PADDED, C), BF16),
    in1=((COLS, PADDED, C), BF16),
    in2=((COLS, PADDED, C), BF16),
    flags=((WIDTH, C), F32),
    w_proj_t=((3 * HD, C), BF16),
    w_rep=((C, H * SLOT), BF16),
    home_rows=((TALL, WIDTH, C), F32),
    zpack=((2, WIDTH, PAIR), F32),
    zin=((ROWS, WIDTH, PAIR), F32),
    bias=((H, COLS, WIDTH, N), F32),
    d_bias=((H, COLS, WIDTH, N), F32),
    d_other=((2, COLS, WIDTH, N), F32),
    stage_far=((4, WIDTH, N), F32),
    d_far=((2, 3, 4 * WIDTH, N), BF16),
    d_far_in=((2, 3, 4 * WIDTH, N), BF16),
    d_near=((2, 4, WIDTH, N), F32),
    d_near_in=((2, 3, WIDTH, N), F32),
    zout=((ROWS, WIDTH, PAIR), F32),
    hin=((2, 4, WIDTH, PAIR), F32),
    mask=((COLS, WIDTH, C), F32),
    row_mask=((OWN, 1, C), F32),
    normed=((OWN, N, C), BF16),
    unit=((OWN, N, C), F32),
    rstd=((OWN, N, C), F32),
    q=((OWN, N, C), BF16),
    k=((OWN, N, C), BF16),
    v=((OWN, N, C), BF16),
    d=((OWN, N, C), BF16),
    q_t=((OWN, C, N), BF16),
    k_t=((OWN, C, N), BF16),
    v_t=((OWN, C, N), BF16),
    d_t=((OWN, C, N), BF16),
    gate=((OWN, N, C), F32),
    dgate=((OWN, N, C), F32),
    att_t=((OWN, HD, N), F32),
    att=((OWN, N, HD), F32),
    d_proj=((OWN, N, 4 * HD), BF16),
    dq_t=((OWN, HD, N), F32),
    dk=((OWN, N, HD), F32),
    dv=((OWN, N, HD), F32),
    proj=((C, 4 * HD), F32),
    r5=((COLS, 8, 4 * HD), F32),
    v5=((8, 4 * HD), F32),
    r6=((8, 8, 4 * HD), F32),
    v6=((8, 4 * HD), F32),
    stage_u=((COLS, PADDED, C), F32),
    stage_a=((COLS, PADDED, C), F32),
    out_u=((COLS, PADDED, C), BF16),
    out_a=((COLS, PADDED, C), BF16),
)
MAIN_SEMS = dict(
    operand=(9,),
    norm=(2,),
    in1=(COLS,),
    in2=(COLS,),
    z=(8,),
    near=(2, 3),
    far=(2, 4, 3),
    partner=(2,),
    back=(2,),
    d_far=(2, 3),
    d_near=(2, 3),
    dz=(8,),
    p1=(COLS,),
    p2=(8,),
    p3=(COLS,),
    u=(COLS,),
    a=(COLS,),
)
MAIN_IN = 10
MAIN_OUT = 6


class Names:
    pass


def main_kernel(*refs):
    length, operands = refs[0], refs[1:MAIN_IN]
    (land_u, land_a, proj_out, h_sum, unit_out, rstd_out) = refs[MAIN_IN : MAIN_IN + MAIN_OUT]
    rest = refs[MAIN_IN + MAIN_OUT :]
    m, send, recv = Names(), Names(), Names()
    for name, ref in zip(MAIN_SCRATCH, rest):
        setattr(m, name, ref)
    rest = rest[len(MAIN_SCRATCH) :]
    for name, ref in zip(MAIN_SEMS, rest):
        setattr(send, name, ref)
    for name, ref in zip(MAIN_SEMS, rest[len(MAIN_SEMS) :]):
        setattr(recv, name, ref)
    held = (m.pair, m.cot, m.residues, m.gain, m.shift, m.w_proj, m.gate_bias, m.w_bias_t, m.w_out)
    pair, cot, residues, gain, shift, w_proj, gate_bias, w_bias_t, w_out = held
    for n in range(MAIN_IN - 1):
        pltpu.make_async_copy(operands[n], held[n], recv.operand.at[n]).start()
    at = Place()
    e = at.e
    count = greet_all(at)
    for n in range(MAIN_IN - 1):
        arrived(held[n], recv.operand.at[n])

    sublane = lax.broadcasted_iota(jnp.int32, (WIDTH, WIDTH), 0)
    lane = lax.broadcasted_iota(jnp.int32, (WIDTH, WIDTH), 1)
    valid = jnp.where(lane + at.c * WIDTH < length[0], residues[...], 0).astype(F32)
    valid = jnp.sum(jnp.where(lane == sublane, valid, 0.0), axis=1, keepdims=True)
    m.flags[...] = jnp.broadcast_to(valid, (WIDTH, C))
    lane = lax.broadcasted_iota(jnp.int32, (8, C), 1)
    packed_flags = jnp.where(
        lane == 0, m.flags[0:8, :], jnp.where(lane == 1, m.flags[8:16, :], m.flags[16:24, :])
    )
    pad = jnp.zeros((COLS, PADDED - PART, C), F32)
    m.m1[...] = jnp.concatenate(
        [
            pair[...].astype(F32).reshape(COLS, PART, C),
            jnp.broadcast_to(packed_flags[None], (COLS, PADDED - PART, C)),
        ],
        axis=1,
    ).astype(BF16)
    m.m2[...] = jnp.concatenate([cot[...].astype(F32).reshape(COLS, PART, C), pad], axis=1).astype(BF16)

    m.w_rep[...] = repeat_heads(w_bias_t)
    unit, inverse = standardize(pair[...].astype(F32).reshape(TALL * WIDTH, C))
    m.home_unit[...] = unit.reshape(TALL, WIDTH, C)
    m.home_rstd[...] = inverse.reshape(TALL, WIDTH, C)
    m.home_rows[...] = (unit * gain[...] + shift[...]).reshape(TALL, WIDTH, C)

    def home_bias(n, total):
        for i in range(8):
            rows = m.home_rows[n * 8 + i].astype(BF16)
            total = total + jnp.dot(rows, only_row(m.w_rep[...], n * 8 + i), preferred_element_type=F32)
        return total

    packed = lax.fori_loop(0, TALL // 8, home_bias, jnp.zeros((WIDTH, H * SLOT), F32))
    negative = (m.flags[...] - 1.0) * 1e9
    m.zpack[0] = packed[:, :PAIR] + negative
    m.zpack[1] = packed[:, PAIR:] + negative

    pl.semaphore_wait(pltpu.get_barrier_semaphore(), count)

    def to_workers(n, carry):
        core, zz = lax.div(n, 4), lax.rem(n, 4)
        send_or_copy(
            at.is_worker(core, zz),
            m.zpack.at[core],
            m.zin.at[at.z],
            send.z.at[n],
            recv.z.at[at.z],
            at.worker(core, zz),
        )
        return carry

    lax.fori_loop(0, 8, to_workers, 0)
    exchange_start(at, m.m1, m.in1, send.in1, recv.in1)
    exchange_start(at, m.m2, m.in2, send.in2, recv.in2)
    pltpu.make_async_copy(m.home_unit, unit_out, recv.norm.at[0]).start()
    pltpu.make_async_copy(m.home_rstd, rstd_out, recv.norm.at[1]).start()

    m.w_proj_t[...] = w_proj[:, : 3 * HD].astype(F32).T.astype(BF16)
    m.d_bias[...] = jnp.zeros_like(m.d_bias)
    m.dk[...] = jnp.zeros_like(m.dk)
    m.dv[...] = jnp.zeros_like(m.dv)
    exchange_arrived(m.in1, recv.in1)

    for s in range(OWN):
        values = m.in1[:, s * WIDTH : (s + 1) * WIDTH, :].astype(F32).reshape(N, C)
        unit, inverse = standardize(values)
        m.unit[s] = unit
        m.rstd[s] = inverse
        m.normed[s] = (unit * gain[...] + shift[...]).astype(BF16)

    def bias_block(hh, a, b):
        return m.bias.at[e * 2 + hh, at.col(at.f - a + 4, at.g - b + 4)]

    def to_far(hh, a):
        block = bias_block(hh, a, 0)
        for n in (1, 2, 3):
            remote(block, block, send.far.at[hh, a, n - 1], recv.far.at[hh, a, n - 1], at.gpeer(n)).start()

    def forward(hh):
        for n in (1, 2, 3):
            arrived(bias_block(hh, n, 0), recv.near.at[hh, n - 1])
            to_far(hh, n)

    for z in range(ROWS):
        arrived(m.zin.at[z], recv.z.at[z])
    for hh in range(2):
        head = e * 2 + hh
        m.bias[head, at.c] = jnp.concatenate(
            [m.zin[z][:, hh * SLOT : hh * SLOT + TALL] for z in range(ROWS)], axis=1
        )
        mine = m.bias.at[head, at.c]
        for n in (1, 2, 3):
            remote(mine, mine, send.near.at[hh, n - 1], recv.near.at[hh, n - 1], at.fpeer(n)).start()
        to_far(hh, 0)

    for s in range(OWN):
        rows = m.normed[s]
        flat = jnp.dot(rows, w_proj[...], preferred_element_type=F32)
        m.q[s] = (flat[:, :HD] * SCALE).astype(BF16)
        m.k[s] = flat[:, HD : 2 * HD].astype(BF16)
        m.v[s] = flat[:, 2 * HD : 3 * HD].astype(BF16)
        m.gate[s] = jax.nn.sigmoid(flat[:, 3 * HD :] + gate_bias[...])
        flat_t = lax.dot_general(m.w_proj_t[...], rows, NT, preferred_element_type=F32)
        m.q_t[s] = (flat_t[:HD] * SCALE).astype(BF16)
        m.k_t[s] = flat_t[HD : 2 * HD].astype(BF16)
        m.v_t[s] = flat_t[2 * HD : 3 * HD].astype(BF16)

    forward(0)
    forward(1)
    exchange_arrived(m.in2, recv.in2)
    tiles = m.in1[:, PART:, :].astype(F32)
    for t in range(3):
        rows = jnp.broadcast_to(tiles[:, :, t : t + 1], (COLS, 8, C))
        m.mask[:, t * 8 : (t + 1) * 8, :] = rows
    for s in range(OWN):
        values = m.in2[:, s * WIDTH : (s + 1) * WIDTH, :].astype(F32).reshape(N, C)
        row = at.row0 + s
        own_mask = m.mask[lax.div(row, WIDTH), pl.ds(lax.rem(row, WIDTH), 1), :]
        m.row_mask[s] = own_mask
        pair_mask = m.mask[...].reshape(N, C) * own_mask
        d_out = jnp.where(pair_mask > 0, values, 0.0).astype(BF16)
        d_gated = lax.dot_general(d_out, w_out[...], NT, preferred_element_type=F32)
        gates = m.gate[s]
        d_attn = d_gated * gates
        m.d[s] = d_attn.astype(BF16)
        m.d_t[s] = d_attn.T.astype(BF16)
        m.dgate[s] = d_attn * (1.0 - gates)

    def products(h, carry):
        row = lax.div(lax.broadcasted_iota(jnp.int32, (C, N), 0), DH)
        by_row = (row == h).astype(F32).astype(BF16)
        for s in range(OWN):
            m.scores[h, s] = jnp.dot(m.k[s], m.q_t[s] * by_row, preferred_element_type=F32)
            m.d_prob[h, s] = jnp.dot(m.v[s], m.d_t[s] * by_row, preferred_element_type=F32)
        return carry

    lax.fori_loop(0, H, products, 0)

    def own_bias_arrived(hh):
        for a in range(4):
            for n in (1, 2, 3):
                arrived(bias_block(hh, a, n), recv.far.at[hh, a, n - 1])
        whole = m.bias.at[e * 2 + hh]
        remote(whole, whole, send.partner.at[hh], recv.partner.at[hh], at.partner()).start()

    def other_bias_arrived(hh):
        arrived(m.bias.at[(1 - e) * 2 + hh], recv.partner.at[hh])

    def attend(h):
        here = pl.ds(pl.multiple_of(h * DH, DH), DH)
        lane = lax.div(lax.broadcasted_iota(jnp.int32, (C, C), 1), DH)
        by_lane = (lane == h).astype(F32).astype(BF16)

        def one_row(s, carry):
            keys_t, values_t = m.k_t[s, here, :], m.v_t[s, here, :]
            dk_sum = dv_sum = None
            for n in range(3):
                lanes = slice(n * C, (n + 1) * C)
                scores = m.scores[h, s, :, lanes] + m.bias[h, :, :, lanes].reshape(N, C)
                exponent = jnp.exp(scores - jnp.max(scores, axis=0, keepdims=True))
                weights = exponent * (1.0 / jnp.sum(exponent, axis=0, keepdims=True))
                weights_b = weights.astype(BF16)
                attended = jnp.dot(values_t, weights_b, preferred_element_type=F32)
                m.att_t[s, here, lanes] = attended
                delta = jnp.sum(attended * m.d_t[s, here, lanes].astype(F32), axis=0, keepdims=True)
                d_score = weights * (m.d_prob[h, s, :, lanes] - delta)
                d_score_b = d_score.astype(BF16)
                m.d_bias[h, :, :, lanes] += d_score.reshape(COLS, WIDTH, C)
                m.dq_t[s, here, lanes] = jnp.dot(keys_t, d_score_b, preferred_element_type=F32)
                dv_part = jnp.dot(weights_b, m.d[s, lanes, :] * by_lane, preferred_element_type=F32)
                dk_part = jnp.dot(d_score_b, m.q[s, lanes, :] * by_lane, preferred_element_type=F32)
                dv_sum = dv_part if dv_sum is None else dv_sum + dv_part
                dk_sum = dk_part if dk_sum is None else dk_sum + dk_part
            m.dk[s] += dk_sum
            m.dv[s] += dv_sum
            return carry

        lax.fori_loop(0, OWN, one_row, 0)

    def to_other(hh):
        head = (1 - e) * 2 + hh
        remote(m.d_bias.at[head], m.d_other.at[hh], send.back.at[hh], recv.back.at[hh], at.partner()).start()

    def scatter_far(hh):
        head = e * 2 + hh
        arrived(m.d_other.at[hh], recv.back.at[hh])
        for n in (1, 2, 3, 0):
            for f in range(4):
                column = at.col(f, at.g + n)
                both = m.d_bias[head, column] + m.d_other[hh, column]
                if n == 0:
                    m.d_near[hh, f] = both
                else:
                    m.stage_far[f] = both
            if n > 0:
                m.d_far[hh, n - 1] = m.stage_far[...].reshape(4 * WIDTH, N).astype(BF16)
                remote(
                    m.d_far.at[hh, n - 1],
                    m.d_far_in.at[hh, n - 1],
                    send.d_far.at[hh, n - 1],
                    recv.d_far.at[hh, n - 1],
                    at.gpeer(n),
                ).start()

    def scatter_near(hh):
        for n in range(3):
            arrived(m.d_far_in.at[hh, n], recv.d_far.at[hh, n])
        far = (m.d_far_in[hh, 0].astype(F32) + m.d_far_in[hh, 1].astype(F32)) + m.d_far_in[hh, 2].astype(F32)
        m.d_near[hh] += far.reshape(4, WIDTH, N)
        for n in (1, 2, 3):
            remote(
                m.d_near.at[hh, lax.rem(at.f + n, 4)],
                m.d_near_in.at[hh, n - 1],
                send.d_near.at[hh, n - 1],
                recv.d_near.at[hh, n - 1],
                at.fpeer(n),
            ).start()

    def plane_sum(hh):
        for n in range(3):
            arrived(m.d_near_in.at[hh, n], recv.d_near.at[hh, n])
        return (m.d_near[hh, at.f] + m.d_near_in[hh, 0]) + (m.d_near_in[hh, 1] + m.d_near_in[hh, 2])

    own_bias_arrived(0)
    attend(e * 2)
    own_bias_arrived(1)
    other_bias_arrived(0)
    attend(2 - e * 2)
    to_other(0)
    other_bias_arrived(1)
    attend(3 - e * 2)
    to_other(1)
    scatter_far(0)
    attend(e * 2 + 1)
    scatter_far(1)

    for s in range(OWN):
        attended = m.att_t[s].T
        m.att[s] = attended
        d_proj = jnp.concatenate(
            [m.dq_t[s].T * SCALE, m.dk[s], m.dv[s], m.dgate[s] * attended], axis=1
        ).astype(BF16)
        m.d_proj[s] = d_proj
        normed_t = m.normed[s].astype(F32).T.astype(BF16)
        share = jnp.dot(normed_t, d_proj, preferred_element_type=F32)
        if s == 0:
            m.proj[...] = share
        else:
            m.proj[...] += share

    def rows_of(ref, c):
        return ref.at[pl.ds(pl.multiple_of(c * 8, 8), 8), :]

    def scatter_proj(n, carry):
        t = lax.rem(at.c + n, COLS)
        remote(rows_of(m.proj, t), m.r5.at[n], send.p1.at[n], recv.p1.at[n], at.plane(n)).start()
        return carry

    lax.fori_loop(1, COLS, scatter_proj, 0)
    scatter_near(0)

    for s in range(OWN):
        gated = (m.gate[s] * m.att[s]).astype(BF16)
        pair_mask = m.mask[...].reshape(N, C) * m.row_mask[s]
        update = jnp.dot(gated, w_out[...], preferred_element_type=F32) * pair_mask
        m.stage_u[:, s * WIDTH : (s + 1) * WIDTH, :] = update.reshape(COLS, WIDTH, C)
    m.stage_u[:, PART:, :] = pad
    m.out_u[...] = m.stage_u[...].astype(BF16)
    exchange_start(at, m.out_u, land_u, send.u, recv.u)
    scatter_near(1)

    for s in range(OWN):
        d_normed = lax.dot_general(m.d_proj[s], w_proj[...], NT, preferred_element_type=F32)
        result = norm_backward(d_normed * gain[...], m.unit[s], m.rstd[s])
        m.stage_a[:, s * WIDTH : (s + 1) * WIDTH, :] = result.reshape(COLS, WIDTH, C)
    m.stage_a[:, PART:, :] = pad
    m.out_a[...] = m.stage_a[...].astype(BF16)
    exchange_start(at, m.out_a, land_a, send.a, recv.a)

    halves = [plane_sum(0), plane_sum(1)]
    blank = jnp.zeros((WIDTH, SLOT - TALL), F32)
    for z in range(ROWS):
        mine = slice(z * TALL, (z + 1) * TALL)
        m.zout[z] = jnp.concatenate([halves[0][:, mine], blank, halves[1][:, mine], blank], axis=1)

    def to_homes(z, carry):
        send_or_copy(
            at.is_home(z),
            m.zout.at[z],
            m.hin.at[e, at.zz],
            send.dz.at[z],
            recv.dz.at[e * 4 + at.zz],
            at.home(z),
        )
        return carry

    lax.fori_loop(0, ROWS, to_homes, 0)


    def proj_arrived(n, total):
        arrived(m.r5.at[n], recv.p1.at[n])
        return total + m.r5[n]

    m.v5[...] = lax.fori_loop(1, COLS, proj_arrived, m.proj[pl.ds(pl.multiple_of(at.c * 8, 8), 8), :])

    def proj_to_homes(z, carry):
        slot = e * 4 + at.zz
        send_or_copy(at.is_home(z), m.v5, m.r6.at[slot], send.p2.at[z], recv.p2.at[slot], at.home(z))
        return carry

    lax.fori_loop(0, ROWS, proj_to_homes, 0)

    def share_arrived(n, total):
        arrived(m.r6.at[n], recv.p2.at[n])
        return total + m.r6[n]

    m.v6[...] = lax.fori_loop(0, 8, share_arrived, jnp.zeros((8, 4 * HD), F32))
    own_rows = rows_of(proj_out, at.c)
    pltpu.make_async_copy(m.v6, own_rows, recv.p3.at[0]).start()

    def spread(n, carry):
        remote(m.v6, own_rows, send.p3.at[n], recv.p3.at[n], at.plane(n)).start()
        return carry

    lax.fori_loop(1, COLS, spread, 0)

    for core in range(2):
        for zz in range(4):
            arrived(m.hin.at[core, zz], recv.dz.at[core * 4 + zz])
        lanes = slice(core * PAIR, (core + 1) * PAIR)
        h_sum[:, lanes] = (m.hin[core, 0] + m.hin[core, 1]) + (m.hin[core, 2] + m.hin[core, 3])
    exchange_arrived(land_u, recv.u)
    exchange_arrived(land_a, recv.a)

    def out_arrived(n, carry):
        arrived(rows_of(proj_out, lax.rem(at.c - n + COLS, COLS)), recv.p3.at[n])
        return carry

    lax.fori_loop(0, COLS, out_arrived, 0)

    arrived(unit_out, recv.norm.at[0])
    arrived(rstd_out, recv.norm.at[1])

    def column_sent(n, carry):
        arrived(m.v5, send.p1.at[n])
        arrived(m.v6, send.p3.at[n])
        return carry

    lax.fori_loop(1, COLS, column_sent, 0)

    def column_group_sent(n, carry):
        @pl.when(jnp.logical_not(at.is_worker(lax.div(n, 4), lax.rem(n, 4))))
        def _():
            arrived(m.zpack.at[0], send.z.at[n])

        @pl.when(jnp.logical_not(at.is_home(n)))
        def _():
            arrived(m.zout.at[0], send.dz.at[n])
            arrived(m.v5, send.p2.at[n])

        return carry

    lax.fori_loop(0, 8, column_group_sent, 0)
    for hh in range(2):
        for n in range(3):
            arrived(m.bias.at[0, 0], send.near.at[hh, n])
            for a in range(4):
                arrived(m.bias.at[0, 0], send.far.at[hh, a, n])
            arrived(m.d_far.at[0, 0], send.d_far.at[hh, n])
            arrived(m.d_near.at[0, 0], send.d_near.at[hh, n])
        arrived(m.bias.at[0], send.partner.at[hh])
        arrived(m.d_bias.at[0], send.back.at[hh])
    exchange_sent(at, m.m1, send.in1)
    exchange_sent(at, m.m2, send.in2)
    exchange_sent(at, m.out_u, send.u)
    exchange_sent(at, m.out_a, send.a)


STEPS = 4


def finish_kernel(
    land_u, land_a, proj_in, h_sum, unit, rstd, gain, w_bias_t, update, pair_grad, proj_out, w_rep, split, share
):
    tall = TALL // STEPS
    step = pl.program_id(0)

    @pl.when(step == 0)
    def _():
        proj_out[...] = proj_in[...]
        w_rep[...] = repeat_heads(w_bias_t)
        total = h_sum[...]
        for n in range(3):
            term = total.astype(BF16).astype(F32)
            split[n * WIDTH : (n + 1) * WIDTH, :] = term
            total = total - term

    update[...] = land_u[:, :PART, :].astype(F32).reshape(tall, WIDTH, C).astype(BF16)
    share[...] = land_a[:, :PART, :].astype(F32).reshape(tall, WIDTH, C)
    terms = split[...].astype(BF16)
    for i in range(tall):
        parts = lax.dot_general(
            terms, only_row(w_rep[...], step * tall + i), NT, preferred_element_type=F32
        )
        grad = (parts[2 * WIDTH :] + parts[WIDTH : 2 * WIDTH]) + parts[:WIDTH]
        result = norm_backward(grad * gain[...], unit[i], rstd[i])
        pair_grad[i] = (share[i] + result).astype(BF16)


def vmem(count):
    return [pl.BlockSpec(memory_space=pltpu.VMEM)] * count


def shards(
    pair_act, cotangent, ln_gain, ln_shift, w_proj, gate_bias, w_bias, w_out, residue_mask, valid_length
):
    any_space = pl.BlockSpec(memory_space=pl.ANY)
    gain = ln_gain.reshape(1, C)
    sems = [pltpu.SemaphoreType.DMA(shape) for shape in MAIN_SEMS.values()]
    landing = jax.ShapeDtypeStruct((COLS, PADDED, C), BF16)
    block = jax.ShapeDtypeStruct(pair_act.shape, F32)
    proj_shape = jax.ShapeDtypeStruct((C, 4 * HD), F32)
    land_u, land_a, proj, h_sum, unit, rstd = pl.pallas_call(
        main_kernel,
        out_shape=[
            landing,
            landing,
            proj_shape,
            jax.ShapeDtypeStruct((WIDTH, H * SLOT), F32),
            block,
            block,
        ],
        in_specs=[pl.BlockSpec(memory_space=pltpu.SMEM)] + [any_space] * (MAIN_IN - 1),
        out_specs=[any_space] * 3 + vmem(1) + [any_space] * 2,
        scratch_shapes=[pltpu.VMEM(shape, dtype) for shape, dtype in MAIN_SCRATCH.values()] + sems + sems,
        compiler_params=pltpu.CompilerParams(
            collective_id=0, has_side_effects=True, vmem_limit_bytes=VMEM_LIMIT
        ),
        name="main",
    )(
        valid_length,
        pair_act,
        cotangent,
        residue_mask.reshape(1, WIDTH),
        gain,
        ln_shift.reshape(1, C),
        w_proj,
        gate_bias.reshape(1, HD),
        w_bias.T,
        w_out,
    )
    result = jax.ShapeDtypeStruct(pair_act.shape, BF16)
    tall = TALL // STEPS
    rows = pl.BlockSpec((tall, WIDTH, C), lambda n: (n, 0, 0))
    landed = pl.BlockSpec((COLS // STEPS, PADDED, C), lambda n: (n, 0, 0))

    def whole(*shape):
        return pl.BlockSpec(shape, lambda n: (0,) * len(shape))

    return pl.pallas_call(
        finish_kernel,
        out_shape=[result, result, proj_shape],
        grid=(STEPS,),
        in_specs=[
            landed,
            landed,
            whole(C, 4 * HD),
            whole(WIDTH, H * SLOT),
            rows,
            rows,
            whole(1, C),
            whole(H, C),
        ],
        out_specs=[rows, rows, whole(C, 4 * HD)],
        scratch_shapes=[
            pltpu.VMEM((C, H * SLOT), BF16),
            pltpu.VMEM((3 * WIDTH, H * SLOT), F32),
            pltpu.VMEM((tall, WIDTH, C), F32),
        ],
        compiler_params=pltpu.CompilerParams(vmem_limit_bytes=VMEM_LIMIT),
        name="finish",
    )(land_u, land_a, proj, h_sum, unit, rstd, gain, w_bias.T)


def solution(mesh):
    return jax.shard_map(
        shards,
        mesh=mesh,
        in_specs=(
            P(("complex", "row"), "col", None),
            P(("complex", "row"), "col", None),
            P(),
            P(),
            P(),
            P(),
            P(),
            P(),
            P(("complex", "col")),
            P("complex"),
        ),
        out_specs=(
            P(("complex", "row"), "col", None),
            P(("complex", "row"), "col", None),
            P("complex", None),
        ),
        check_vma=False,
    )
```

```python
import jax
import jax.numpy as jnp
from jax import lax
from jax.experimental import pallas as pl
from jax.experimental.pallas import tpu as pltpu
from jax.sharding import PartitionSpec as P

MESH = pl.DeviceIdType.MESH
F32 = jnp.float32
BF16 = jnp.bfloat16
N = 384
C = 128
H = 4
DH = 32
HD = H * DH
COLS = 16
ROWS = 8
WIDTH = N // COLS
TALL = N // ROWS
OWN = 3
PART = OWN * WIDTH
PADDED = 80
SLOT = 64
PAIR = 2 * SLOT
SCALE = DH ** (-0.5)
VMEM_LIMIT = 60 * 1024 * 1024
NT = (((1,), (1,)), ((), ()))


class Place:
    def __init__(self):
        self.e = lax.axis_index("complex")
        self.z = lax.axis_index("row")
        self.c = lax.axis_index("col")
        self.part = lax.rem(self.z, 2)
        self.zz = lax.div(self.z, 2)
        self.stays = self.part == self.e
        self.y = lax.div(self.c, 4)
        self.x = lax.rem(self.c, 4)
        self.f = self.x * (1 - self.e) + self.y * self.e
        self.g = self.y * (1 - self.e) + self.x * self.e
        self.row0 = (self.zz * 2 + self.e) * TALL + self.c * OWN

    def swapped(self, c):
        return (self.part, self.zz * 2 + self.e, c)

    def col(self, f, g):
        return lax.rem(f, 4) * (1 + 3 * self.e) + lax.rem(g, 4) * (4 - 3 * self.e)

    def fpeer(self, n):
        return (self.e, self.z, self.col(self.f + n, self.g))

    def gpeer(self, n):
        return (self.e, self.z, self.col(self.f, self.g + n))

    def plane(self, n):
        return (self.e, self.z, lax.rem(self.c + n, COLS))

    def partner(self):
        return (1 - self.e, self.z, self.c)

    def worker(self, core, zz):
        return (core, zz * 2 + self.e, self.c)

    def home(self, z):
        return (self.part, z, self.c)

    def is_worker(self, core, zz):
        return jnp.logical_and(self.stays, jnp.logical_and(core == self.e, zz == self.zz))

    def is_home(self, z):
        return jnp.logical_and(self.stays, z == self.z)


def remote(src, dst, send, recv, device):
    return pltpu.make_async_remote_copy(
        src_ref=src, dst_ref=dst, send_sem=send, recv_sem=recv, device_id=device, device_id_type=MESH
    )


def arrived(ref, sem):
    pltpu.make_async_copy(ref, ref, sem).wait()


def send_or_copy(here, src, dst, send, recv, device):
    @pl.when(here)
    def _():
        pltpu.make_async_copy(src, dst, recv).start()

    @pl.when(jnp.logical_not(here))
    def _():
        remote(src, dst, send, recv, device).start()


def greet(device):
    pl.semaphore_signal(pltpu.get_barrier_semaphore(), inc=1, device_id=device, device_id_type=MESH)


def greet_all(at):
    def plane(n, carry):
        greet(at.plane(n))
        return carry

    lax.fori_loop(1, COLS, plane, 0)

    def worker(n, carry):
        core, zz = lax.div(n, 4), lax.rem(n, 4)

        @pl.when(jnp.logical_not(at.is_worker(core, zz)))
        def _():
            greet(at.worker(core, zz))

        return carry

    lax.fori_loop(0, 8, worker, 0)

    def home(n, carry):
        greet(at.home(n * 2 + 1 - at.e))
        return carry

    lax.fori_loop(0, 4, home, 0)

    @pl.when(jnp.logical_not(at.stays))
    def _():
        def column(n, carry):
            greet(at.swapped(n))
            return carry

        lax.fori_loop(0, COLS, column, 0)

    return jnp.where(at.stays, COLS - 1 + 7 + 4, COLS - 1 + 8 + 4 + COLS)


def exchange_start(at, source, slot, send, recv):
    def column(n, carry):
        t = lax.rem(at.c + n, COLS)
        here = jnp.logical_and(n == 0, at.stays)
        send_or_copy(here, source.at[t], slot, send.at[t], recv.at[at.c], at.swapped(t))
        return carry

    lax.fori_loop(0, COLS, column, 0)


def exchange_arrived(landing, recv):
    def column(n, carry):
        arrived(landing.at[n], recv.at[n])
        return carry

    lax.fori_loop(0, COLS, column, 0)


def exchange_sent(at, source, send):
    def column(n, carry):
        t = lax.rem(at.c + n, COLS)

        @pl.when(jnp.logical_or(n > 0, jnp.logical_not(at.stays)))
        def _():
            arrived(source.at[t], send.at[t])

        return carry

    lax.fori_loop(0, COLS, column, 0)


def repeat_heads(w_bias_t):
    wide = jnp.concatenate([w_bias_t[...].astype(F32), jnp.zeros((C - H, C), F32)], axis=0).T
    lane = lax.div(lax.broadcasted_iota(jnp.int32, (C, H * SLOT), 1), SLOT)
    total = jnp.zeros((C, H * SLOT), F32)
    for h in range(H):
        total = jnp.where(lane == h, wide[:, h : h + 1], total)
    return total.astype(BF16)


def only_row(repeated, i):
    lane = lax.rem(lax.broadcasted_iota(jnp.int32, (1, H * SLOT), 1), SLOT)
    return repeated * (lane == i).astype(F32).astype(BF16)


def standardize(values):
    centre = values - jnp.mean(values, axis=-1, keepdims=True)
    inverse = lax.rsqrt(jnp.mean(centre * centre, axis=-1, keepdims=True) + 1e-5)
    return centre * inverse, jnp.broadcast_to(inverse, values.shape)


def norm_backward(grad, unit, inverse):
    mean_grad = jnp.mean(grad, axis=-1, keepdims=True)
    mean_cross = jnp.mean(grad * unit, axis=-1, keepdims=True)
    return inverse * (grad - mean_grad - unit * mean_cross)


MAIN_SCRATCH = dict(
    pair=((TALL, WIDTH, C), BF16),
    cot=((TALL, WIDTH, C), BF16),
    residues=((1, WIDTH), jnp.int32),
    gain=((1, C), F32),
    shift=((1, C), F32),
    w_proj=((C, 4 * HD), BF16),
    gate_bias=((1, HD), F32),
    w_bias_t=((H, C), BF16),
    w_out=((HD, C), BF16),
    home_unit=((TALL, WIDTH, C), F32),
    home_rstd=((TALL, WIDTH, C), F32),
    scores=((H, OWN, N, N), F32),
    d_prob=((H, OWN, N, N), F32),
    m1=((COLS, PADDED, C), BF16),
    m2=((COLS, PADDED, C), BF16),
    in1=((COLS, PADDED, C), BF16),
    in2=((COLS, PADDED, C), BF16),
    flags=((WIDTH, C), F32),
    w_proj_t=((3 * HD, C), BF16),
    w_rep=((C, H * SLOT), BF16),
    home_rows=((TALL, WIDTH, C), F32),
    zpack=((2, WIDTH, PAIR), F32),
    zin=((ROWS, WIDTH, PAIR), F32),
    bias=((H, COLS, WIDTH, N), F32),
    d_bias=((H, COLS, WIDTH, N), F32),
    d_other=((2, COLS, WIDTH, N), F32),
    stage_far=((4, WIDTH, N), F32),
    d_far=((2, 3, 4 * WIDTH, N), BF16),
    d_far_in=((2, 3, 4 * WIDTH, N), BF16),
    d_near=((2, 4, WIDTH, N), F32),
    d_near_in=((2, 3, WIDTH, N), F32),
    zout=((ROWS, WIDTH, PAIR), F32),
    hin=((2, 4, WIDTH, PAIR), F32),
    mask=((COLS, WIDTH, C), F32),
    row_mask=((OWN, 1, C), F32),
    normed=((OWN, N, C), BF16),
    unit=((OWN, N, C), F32),
    rstd=((OWN, N, C), F32),
    q=((OWN, N, C), BF16),
    k=((OWN, N, C), BF16),
    v=((OWN, N, C), BF16),
    d=((OWN, N, C), BF16),
    q_t=((OWN, C, N), BF16),
    k_t=((OWN, C, N), BF16),
    v_t=((OWN, C, N), BF16),
    d_t=((OWN, C, N), BF16),
    gate=((OWN, N, C), F32),
    dgate=((OWN, N, C), F32),
    att_t=((OWN, HD, N), F32),

    dq_t=((OWN, HD, N), F32),
    dk=((OWN, N, HD), F32),
    dv=((OWN, N, HD), F32),
    proj=((C, 4 * HD), F32),
    proj_b=((C, 4 * HD), BF16),
    r5=((COLS, 16, 2 * HD), BF16),
    v5=((16, 2 * HD), F32),
    r6=((8, 16, 2 * HD), F32),
    v6=((16, 2 * HD), BF16),
    out=((OWN, COLS, 2 * WIDTH, C), BF16),
)
MAIN_SEMS = dict(
    operand=(9,),
    norm=(2,),
    in1=(COLS,),
    in2=(COLS,),
    z=(8,),
    near=(2, 3),
    far=(2, 4, 3),
    partner=(2,),
    back=(2,),
    d_far=(2, 3),
    d_near=(2, 3),
    dz=(8,),
    p1=(COLS,),
    p2=(8,),
    p3=(COLS,),
    out=(OWN, COLS),
)
MAIN_IN = 10
MAIN_OUT = 5


class Names:
    pass


def main_kernel(*refs):
    length, operands = refs[0], refs[1:MAIN_IN]
    (land, proj_out, h_sum, unit_out, rstd_out) = refs[MAIN_IN : MAIN_IN + MAIN_OUT]
    rest = refs[MAIN_IN + MAIN_OUT :]
    m, send, recv = Names(), Names(), Names()
    for name, ref in zip(MAIN_SCRATCH, rest):
        setattr(m, name, ref)
    rest = rest[len(MAIN_SCRATCH) :]
    for name, ref in zip(MAIN_SEMS, rest):
        setattr(send, name, ref)
    for name, ref in zip(MAIN_SEMS, rest[len(MAIN_SEMS) :]):
        setattr(recv, name, ref)
    held = (m.pair, m.cot, m.residues, m.gain, m.shift, m.w_proj, m.gate_bias, m.w_bias_t, m.w_out)
    pair, cot, residues, gain, shift, w_proj, gate_bias, w_bias_t, w_out = held
    for n in range(MAIN_IN - 1):
        pltpu.make_async_copy(operands[n], held[n], recv.operand.at[n]).start()
    at = Place()
    e = at.e
    count = greet_all(at)
    for n in range(MAIN_IN - 1):
        arrived(held[n], recv.operand.at[n])

    sublane = lax.broadcasted_iota(jnp.int32, (WIDTH, WIDTH), 0)
    lane = lax.broadcasted_iota(jnp.int32, (WIDTH, WIDTH), 1)
    valid = jnp.where(lane + at.c * WIDTH < length[0], residues[...], 0).astype(F32)
    valid = jnp.sum(jnp.where(lane == sublane, valid, 0.0), axis=1, keepdims=True)
    m.flags[...] = jnp.broadcast_to(valid, (WIDTH, C))
    lane = lax.broadcasted_iota(jnp.int32, (8, C), 1)
    packed_flags = jnp.where(
        lane == 0, m.flags[0:8, :], jnp.where(lane == 1, m.flags[8:16, :], m.flags[16:24, :])
    )
    pad = jnp.zeros((COLS, PADDED - PART, C), F32)
    m.m1[...] = jnp.concatenate(
        [
            pair[...].astype(F32).reshape(COLS, PART, C),
            jnp.broadcast_to(packed_flags[None], (COLS, PADDED - PART, C)),
        ],
        axis=1,
    ).astype(BF16)
    m.m2[...] = jnp.concatenate([cot[...].astype(F32).reshape(COLS, PART, C), pad], axis=1).astype(BF16)

    m.w_rep[...] = repeat_heads(w_bias_t)
    unit, inverse = standardize(pair[...].astype(F32).reshape(TALL * WIDTH, C))
    m.home_unit[...] = unit.reshape(TALL, WIDTH, C)
    m.home_rstd[...] = inverse.reshape(TALL, WIDTH, C)
    m.home_rows[...] = (unit * gain[...] + shift[...]).reshape(TALL, WIDTH, C)

    def home_bias(n, total):
        for i in range(8):
            rows = m.home_rows[n * 8 + i].astype(BF16)
            total = total + jnp.dot(rows, only_row(m.w_rep[...], n * 8 + i), preferred_element_type=F32)
        return total

    packed = lax.fori_loop(0, TALL // 8, home_bias, jnp.zeros((WIDTH, H * SLOT), F32))
    negative = (m.flags[...] - 1.0) * 1e9
    m.zpack[0] = packed[:, :PAIR] + negative
    m.zpack[1] = packed[:, PAIR:] + negative

    pl.semaphore_wait(pltpu.get_barrier_semaphore(), count)

    def to_workers(n, carry):
        core, zz = lax.div(n, 4), lax.rem(n, 4)
        send_or_copy(
            at.is_worker(core, zz),
            m.zpack.at[core],
            m.zin.at[at.z],
            send.z.at[n],
            recv.z.at[at.z],
            at.worker(core, zz),
        )
        return carry

    lax.fori_loop(0, 8, to_workers, 0)
    exchange_start(at, m.m1, m.in1.at[at.c], send.in1, recv.in1)
    exchange_start(at, m.m2, m.in2.at[at.c], send.in2, recv.in2)
    pltpu.make_async_copy(m.home_unit, unit_out, recv.norm.at[0]).start()
    pltpu.make_async_copy(m.home_rstd, rstd_out, recv.norm.at[1]).start()

    m.w_proj_t[...] = w_proj[:, : 3 * HD].astype(F32).T.astype(BF16)
    m.d_bias[...] = jnp.zeros_like(m.d_bias)
    m.dk[...] = jnp.zeros_like(m.dk)
    m.dv[...] = jnp.zeros_like(m.dv)
    m.proj[...] = jnp.zeros_like(m.proj)
    exchange_arrived(m.in1, recv.in1)

    for s in range(OWN):
        values = m.in1[:, s * WIDTH : (s + 1) * WIDTH, :].astype(F32).reshape(N, C)
        unit, inverse = standardize(values)
        m.unit[s] = unit
        m.rstd[s] = inverse
        m.normed[s] = (unit * gain[...] + shift[...]).astype(BF16)

    def bias_block(hh, a, b):
        return m.bias.at[e * 2 + hh, at.col(at.f - a + 4, at.g - b + 4)]

    def to_far(hh, a):
        block = bias_block(hh, a, 0)
        for n in (1, 2, 3):
            remote(block, block, send.far.at[hh, a, n - 1], recv.far.at[hh, a, n - 1], at.gpeer(n)).start()

    def forward(hh):
        for n in (1, 2, 3):
            arrived(bias_block(hh, n, 0), recv.near.at[hh, n - 1])
            to_far(hh, n)

    for z in range(ROWS):
        arrived(m.zin.at[z], recv.z.at[z])
    for hh in range(2):
        head = e * 2 + hh
        m.bias[head, at.c] = jnp.concatenate(
            [m.zin[z][:, hh * SLOT : hh * SLOT + TALL] for z in range(ROWS)], axis=1
        )
        mine = m.bias.at[head, at.c]
        for n in (1, 2, 3):
            remote(mine, mine, send.near.at[hh, n - 1], recv.near.at[hh, n - 1], at.fpeer(n)).start()
        to_far(hh, 0)

    for s in range(OWN):
        rows = m.normed[s]
        flat = jnp.dot(rows, w_proj[...], preferred_element_type=F32)
        m.q[s] = (flat[:, :HD] * SCALE).astype(BF16)
        m.k[s] = flat[:, HD : 2 * HD].astype(BF16)
        m.v[s] = flat[:, 2 * HD : 3 * HD].astype(BF16)
        m.gate[s] = jax.nn.sigmoid(flat[:, 3 * HD :] + gate_bias[...])
        flat_t = lax.dot_general(m.w_proj_t[...], rows, NT, preferred_element_type=F32)
        m.q_t[s] = (flat_t[:HD] * SCALE).astype(BF16)
        m.k_t[s] = flat_t[HD : 2 * HD].astype(BF16)
        m.v_t[s] = flat_t[2 * HD : 3 * HD].astype(BF16)

    forward(0)
    forward(1)
    exchange_arrived(m.in2, recv.in2)
    tiles = m.in1[:, PART:, :].astype(F32)
    for t in range(3):
        rows = jnp.broadcast_to(tiles[:, :, t : t + 1], (COLS, 8, C))
        m.mask[:, t * 8 : (t + 1) * 8, :] = rows
    for s in range(OWN):
        values = m.in2[:, s * WIDTH : (s + 1) * WIDTH, :].astype(F32).reshape(N, C)
        row = at.row0 + s
        own_mask = m.mask[lax.div(row, WIDTH), pl.ds(lax.rem(row, WIDTH), 1), :]
        m.row_mask[s] = own_mask
        pair_mask = m.mask[...].reshape(N, C) * own_mask
        d_out = jnp.where(pair_mask > 0, values, 0.0).astype(BF16)
        d_gated = lax.dot_general(d_out, w_out[...], NT, preferred_element_type=F32)
        gates = m.gate[s]
        d_attn = d_gated * gates
        m.d[s] = d_attn.astype(BF16)
        m.d_t[s] = d_attn.T.astype(BF16)
        m.dgate[s] = d_attn * (1.0 - gates)

    def products(h, carry):
        row = lax.div(lax.broadcasted_iota(jnp.int32, (C, N), 0), DH)
        by_row = (row == h).astype(F32).astype(BF16)
        for s in range(OWN):
            m.scores[h, s] = jnp.dot(m.k[s], m.q_t[s] * by_row, preferred_element_type=F32)
            m.d_prob[h, s] = jnp.dot(m.v[s], m.d_t[s] * by_row, preferred_element_type=F32)
        return carry

    lax.fori_loop(0, H, products, 0)

    def own_bias_arrived(hh):
        for a in range(4):
            for n in (1, 2, 3):
                arrived(bias_block(hh, a, n), recv.far.at[hh, a, n - 1])
        whole = m.bias.at[e * 2 + hh]
        remote(whole, whole, send.partner.at[hh], recv.partner.at[hh], at.partner()).start()

    def other_bias_arrived(hh):
        arrived(m.bias.at[(1 - e) * 2 + hh], recv.partner.at[hh])

    def attend(h, then=None):
        here = pl.ds(pl.multiple_of(h * DH, DH), DH)
        lane = lax.div(lax.broadcasted_iota(jnp.int32, (C, C), 1), DH)
        by_lane = (lane == h).astype(F32).astype(BF16)

        def one_row(s, carry):
            keys_t, values_t = m.k_t[s, here, :], m.v_t[s, here, :]
            dk_sum = dv_sum = None
            for n in range(3):
                lanes = slice(n * C, (n + 1) * C)
                scores = m.scores[h, s, :, lanes] + m.bias[h, :, :, lanes].reshape(N, C)
                exponent = jnp.exp(scores - jnp.max(scores, axis=0, keepdims=True))
                weights = exponent * (1.0 / jnp.sum(exponent, axis=0, keepdims=True))
                weights_b = weights.astype(BF16)
                attended = jnp.dot(values_t, weights_b, preferred_element_type=F32)
                m.att_t[s, here, lanes] = attended
                delta = jnp.sum(attended * m.d_t[s, here, lanes].astype(F32), axis=0, keepdims=True)
                d_score = weights * (m.d_prob[h, s, :, lanes] - delta)
                d_score_b = d_score.astype(BF16)
                m.d_bias[h, :, :, lanes] += d_score.reshape(COLS, WIDTH, C)
                m.dq_t[s, here, lanes] = jnp.dot(keys_t, d_score_b, preferred_element_type=F32)
                dv_part = jnp.dot(weights_b, m.d[s, lanes, :] * by_lane, preferred_element_type=F32)
                dk_part = jnp.dot(d_score_b, m.q[s, lanes, :] * by_lane, preferred_element_type=F32)
                dv_sum = dv_part if dv_sum is None else dv_sum + dv_part
                dk_sum = dk_part if dk_sum is None else dk_sum + dk_part
            m.dk[s] += dk_sum
            m.dv[s] += dv_sum
            if then is not None:
                then(s)
            return carry

        lax.fori_loop(0, OWN, one_row, 0)

    def to_other(hh):
        head = (1 - e) * 2 + hh
        remote(m.d_bias.at[head], m.d_other.at[hh], send.back.at[hh], recv.back.at[hh], at.partner()).start()

    def scatter_far(hh):
        head = e * 2 + hh
        arrived(m.d_other.at[hh], recv.back.at[hh])
        for n in (1, 2, 3, 0):
            for f in range(4):
                column = at.col(f, at.g + n)
                both = m.d_bias[head, column] + m.d_other[hh, column]
                if n == 0:
                    m.d_near[hh, f] = both
                else:
                    m.stage_far[f] = both
            if n > 0:
                m.d_far[hh, n - 1] = m.stage_far[...].reshape(4 * WIDTH, N).astype(BF16)
                remote(
                    m.d_far.at[hh, n - 1],
                    m.d_far_in.at[hh, n - 1],
                    send.d_far.at[hh, n - 1],
                    recv.d_far.at[hh, n - 1],
                    at.gpeer(n),
                ).start()

    def scatter_near(hh):
        for n in range(3):
            arrived(m.d_far_in.at[hh, n], recv.d_far.at[hh, n])
        far = (m.d_far_in[hh, 0].astype(F32) + m.d_far_in[hh, 1].astype(F32)) + m.d_far_in[hh, 2].astype(F32)
        m.d_near[hh] += far.reshape(4, WIDTH, N)
        for n in (1, 2, 3):
            remote(
                m.d_near.at[hh, lax.rem(at.f + n, 4)],
                m.d_near_in.at[hh, n - 1],
                send.d_near.at[hh, n - 1],
                recv.d_near.at[hh, n - 1],
                at.fpeer(n),
            ).start()

    def plane_sum(hh):
        for n in range(3):
            arrived(m.d_near_in.at[hh, n], recv.d_near.at[hh, n])
        return (m.d_near[hh, at.f] + m.d_near_in[hh, 0]) + (m.d_near_in[hh, 1] + m.d_near_in[hh, 2])

    def finish_row(s):
        attended = m.att_t[s].T
        gated = (m.gate[s] * attended).astype(BF16)
        pair_mask = m.mask[...].reshape(N, C) * m.row_mask[s]
        update = jnp.dot(gated, w_out[...], preferred_element_type=F32) * pair_mask
        d_proj = jnp.concatenate(
            [m.dq_t[s].T * SCALE, m.dk[s], m.dv[s], m.dgate[s] * attended], axis=1
        ).astype(BF16)
        d_normed = lax.dot_general(d_proj, w_proj[...], NT, preferred_element_type=F32)
        result = norm_backward(d_normed * gain[...], m.unit[s], m.rstd[s])
        m.out[s] = jnp.concatenate(
            [update.reshape(COLS, WIDTH, C), result.reshape(COLS, WIDTH, C)], axis=1
        ).astype(BF16)
        exchange_start(at, m.out.at[s], land.at[at.c, s], send.out.at[s], recv.out.at[s])
        normed_t = m.normed[s].astype(F32).T.astype(BF16)
        m.proj[...] += jnp.dot(normed_t, d_proj, preferred_element_type=F32)

    own_bias_arrived(0)
    attend(e * 2)
    own_bias_arrived(1)
    other_bias_arrived(0)
    attend(2 - e * 2)
    to_other(0)
    other_bias_arrived(1)
    attend(3 - e * 2)
    to_other(1)
    scatter_far(0)
    attend(e * 2 + 1, finish_row)
    scatter_far(1)

    def piece(ref, c):
        rows = pl.ds(pl.multiple_of(lax.div(c, 2) * 16, 16), 16)
        return ref.at[rows, pl.ds(pl.multiple_of(lax.rem(c, 2) * 2 * HD, 2 * HD), 2 * HD)]

    m.proj_b[...] = m.proj[...].astype(BF16)

    def scatter_proj(n, carry):
        t = lax.rem(at.c + n, COLS)
        remote(piece(m.proj_b, t), m.r5.at[n], send.p1.at[n], recv.p1.at[n], at.plane(n)).start()
        return carry

    lax.fori_loop(1, COLS, scatter_proj, 0)
    scatter_near(0)
    scatter_near(1)

    halves = [plane_sum(0), plane_sum(1)]
    blank = jnp.zeros((WIDTH, SLOT - TALL), F32)
    for z in range(ROWS):
        mine = slice(z * TALL, (z + 1) * TALL)
        m.zout[z] = jnp.concatenate([halves[0][:, mine], blank, halves[1][:, mine], blank], axis=1)

    def to_homes(z, carry):
        send_or_copy(
            at.is_home(z),
            m.zout.at[z],
            m.hin.at[e, at.zz],
            send.dz.at[z],
            recv.dz.at[e * 4 + at.zz],
            at.home(z),
        )
        return carry

    lax.fori_loop(0, ROWS, to_homes, 0)


    def proj_arrived(n, total):
        arrived(m.r5.at[n], recv.p1.at[n])
        return total + m.r5[n].astype(F32)

    m.v5[...] = lax.fori_loop(1, COLS, proj_arrived, piece(m.proj, at.c)[...])

    def proj_to_homes(z, carry):
        slot = e * 4 + at.zz
        send_or_copy(at.is_home(z), m.v5, m.r6.at[slot], send.p2.at[z], recv.p2.at[slot], at.home(z))
        return carry

    lax.fori_loop(0, ROWS, proj_to_homes, 0)

    def share_arrived(n, total):
        arrived(m.r6.at[n], recv.p2.at[n])
        return total + m.r6[n]

    m.v6[...] = lax.fori_loop(0, 8, share_arrived, jnp.zeros((16, 2 * HD), F32)).astype(BF16)
    own_piece = piece(proj_out, at.c)
    pltpu.make_async_copy(m.v6, own_piece, recv.p3.at[0]).start()

    def spread(n, carry):
        remote(m.v6, own_piece, send.p3.at[n], recv.p3.at[n], at.plane(n)).start()
        return carry

    lax.fori_loop(1, COLS, spread, 0)

    for core in range(2):
        for zz in range(4):
            arrived(m.hin.at[core, zz], recv.dz.at[core * 4 + zz])
        lanes = slice(core * PAIR, (core + 1) * PAIR)
        h_sum[:, lanes] = (m.hin[core, 0] + m.hin[core, 1]) + (m.hin[core, 2] + m.hin[core, 3])
    for s in range(OWN):
        exchange_arrived(land.at[:, s], recv.out.at[s])

    def out_arrived(n, carry):
        arrived(piece(proj_out, lax.rem(at.c - n + COLS, COLS)), recv.p3.at[n])
        return carry

    lax.fori_loop(0, COLS, out_arrived, 0)

    arrived(unit_out, recv.norm.at[0])
    arrived(rstd_out, recv.norm.at[1])

    def column_sent(n, carry):
        arrived(m.v6, send.p1.at[n])
        arrived(m.v6, send.p3.at[n])
        return carry

    lax.fori_loop(1, COLS, column_sent, 0)

    def column_group_sent(n, carry):
        @pl.when(jnp.logical_not(at.is_worker(lax.div(n, 4), lax.rem(n, 4))))
        def _():
            arrived(m.zpack.at[0], send.z.at[n])

        @pl.when(jnp.logical_not(at.is_home(n)))
        def _():
            arrived(m.zout.at[0], send.dz.at[n])
            arrived(m.v5, send.p2.at[n])

        return carry

    lax.fori_loop(0, 8, column_group_sent, 0)
    for hh in range(2):
        for n in range(3):
            arrived(m.bias.at[0, 0], send.near.at[hh, n])
            for a in range(4):
                arrived(m.bias.at[0, 0], send.far.at[hh, a, n])
            arrived(m.d_far.at[0, 0], send.d_far.at[hh, n])
            arrived(m.d_near.at[0, 0], send.d_near.at[hh, n])
        arrived(m.bias.at[0], send.partner.at[hh])
        arrived(m.d_bias.at[0], send.back.at[hh])
    exchange_sent(at, m.m1, send.in1)
    exchange_sent(at, m.m2, send.in2)
    for s in range(OWN):
        exchange_sent(at, m.out.at[s], send.out.at[s])


STEPS = 4


def finish_kernel(
    land, proj_in, h_sum, unit, rstd, gain, w_bias_t, update, pair_grad, proj_out, w_rep, split, share
):
    tall = TALL // STEPS
    step = pl.program_id(0)

    @pl.when(step == 0)
    def _():
        proj_out[...] = proj_in[...].astype(F32)
        w_rep[...] = repeat_heads(w_bias_t)
        total = h_sum[...]
        for n in range(3):
            term = total.astype(BF16).astype(F32)
            split[n * WIDTH : (n + 1) * WIDTH, :] = term
            total = total - term

    landed = land[...].astype(F32)
    update[...] = landed[:, :, :WIDTH, :].reshape(tall, WIDTH, C).astype(BF16)
    share[...] = landed[:, :, WIDTH:, :].reshape(tall, WIDTH, C)
    terms = split[...].astype(BF16)
    for i in range(tall):
        parts = lax.dot_general(
            terms, only_row(w_rep[...], step * tall + i), NT, preferred_element_type=F32
        )
        grad = (parts[2 * WIDTH :] + parts[WIDTH : 2 * WIDTH]) + parts[:WIDTH]
        result = norm_backward(grad * gain[...], unit[i], rstd[i])
        pair_grad[i] = (share[i] + result).astype(BF16)


def vmem(count):
    return [pl.BlockSpec(memory_space=pltpu.VMEM)] * count


def shards(
    pair_act, cotangent, ln_gain, ln_shift, w_proj, gate_bias, w_bias, w_out, residue_mask, valid_length
):
    any_space = pl.BlockSpec(memory_space=pl.ANY)
    gain = ln_gain.reshape(1, C)
    sems = [pltpu.SemaphoreType.DMA(shape) for shape in MAIN_SEMS.values()]
    landing = jax.ShapeDtypeStruct((COLS, OWN, 2 * WIDTH, C), BF16)
    block = jax.ShapeDtypeStruct(pair_act.shape, F32)
    proj_shape = jax.ShapeDtypeStruct((C, 4 * HD), F32)
    land, proj, h_sum, unit, rstd = pl.pallas_call(
        main_kernel,
        out_shape=[
            landing,
            jax.ShapeDtypeStruct((C, 4 * HD), BF16),
            jax.ShapeDtypeStruct((WIDTH, H * SLOT), F32),
            block,
            block,
        ],
        in_specs=[pl.BlockSpec(memory_space=pltpu.SMEM)] + [any_space] * (MAIN_IN - 1),
        out_specs=[any_space] * 2 + vmem(1) + [any_space] * 2,
        scratch_shapes=[pltpu.VMEM(shape, dtype) for shape, dtype in MAIN_SCRATCH.values()] + sems + sems,
        compiler_params=pltpu.CompilerParams(
            collective_id=0, has_side_effects=True, vmem_limit_bytes=VMEM_LIMIT
        ),
        name="main",
    )(
        valid_length,
        pair_act,
        cotangent,
        residue_mask.reshape(1, WIDTH),
        gain,
        ln_shift.reshape(1, C),
        w_proj,
        gate_bias.reshape(1, HD),
        w_bias.T,
        w_out,
    )
    result = jax.ShapeDtypeStruct(pair_act.shape, BF16)
    tall = TALL // STEPS
    rows = pl.BlockSpec((tall, WIDTH, C), lambda n: (n, 0, 0))
    landed = pl.BlockSpec((COLS // STEPS, OWN, 2 * WIDTH, C), lambda n: (n, 0, 0, 0))

    def whole(*shape):
        return pl.BlockSpec(shape, lambda n: (0,) * len(shape))

    return pl.pallas_call(
        finish_kernel,
        out_shape=[result, result, proj_shape],
        grid=(STEPS,),
        in_specs=[
            landed,
            whole(C, 4 * HD),
            whole(WIDTH, H * SLOT),
            rows,
            rows,
            whole(1, C),
            whole(H, C),
        ],
        out_specs=[rows, rows, whole(C, 4 * HD)],
        scratch_shapes=[
            pltpu.VMEM((C, H * SLOT), BF16),
            pltpu.VMEM((3 * WIDTH, H * SLOT), F32),
            pltpu.VMEM((tall, WIDTH, C), F32),
        ],
        compiler_params=pltpu.CompilerParams(vmem_limit_bytes=VMEM_LIMIT),
        name="finish",
    )(land, proj, h_sum, unit, rstd, gain, w_bias.T)


def solution(mesh):
    return jax.shard_map(
        shards,
        mesh=mesh,
        in_specs=(
            P(("complex", "row"), "col", None),
            P(("complex", "row"), "col", None),
            P(),
            P(),
            P(),
            P(),
            P(),
            P(),
            P(("complex", "col")),
            P("complex"),
        ),
        out_specs=(
            P(("complex", "row"), "col", None),
            P(("complex", "row"), "col", None),
            P("complex", None),
        ),
        check_vma=False,
    )
```

```python
import jax
import jax.numpy as jnp
from jax import lax
from jax.experimental import pallas as pl
from jax.experimental.pallas import tpu as pltpu
from jax.sharding import PartitionSpec as P

MESH = pl.DeviceIdType.MESH
F32 = jnp.float32
BF16 = jnp.bfloat16
N = 384
C = 128
H = 4
DH = 32
HD = H * DH
COLS = 16
ROWS = 8
WIDTH = N // COLS
TALL = N // ROWS
OWN = 3
PART = OWN * WIDTH
PADDED = 80
SLOT = 64
PAIR = 2 * SLOT
SCALE = DH ** (-0.5)
VMEM_LIMIT = 60 * 1024 * 1024
NT = (((1,), (1,)), ((), ()))


class Place:
    def __init__(self):
        self.e = lax.axis_index("complex")
        self.z = lax.axis_index("row")
        self.c = lax.axis_index("col")
        self.part = lax.rem(self.z, 2)
        self.zz = lax.div(self.z, 2)
        self.stays = self.part == self.e
        self.y = lax.div(self.c, 4)
        self.x = lax.rem(self.c, 4)
        self.f = self.x * (1 - self.e) + self.y * self.e
        self.g = self.y * (1 - self.e) + self.x * self.e
        self.row0 = (self.zz * 2 + self.e) * TALL + self.c * OWN

    def swapped(self, c):
        return (self.part, self.zz * 2 + self.e, c)

    def col(self, f, g):
        return lax.rem(f, 4) * (1 + 3 * self.e) + lax.rem(g, 4) * (4 - 3 * self.e)

    def fpeer(self, n):
        return (self.e, self.z, self.col(self.f + n, self.g))

    def gpeer(self, n):
        return (self.e, self.z, self.col(self.f, self.g + n))

    def plane(self, n):
        return (self.e, self.z, lax.rem(self.c + n, COLS))

    def partner(self):
        return (1 - self.e, self.z, self.c)

    def worker(self, core, zz):
        return (core, zz * 2 + self.e, self.c)

    def home(self, z):
        return (self.part, z, self.c)

    def is_worker(self, core, zz):
        return jnp.logical_and(self.stays, jnp.logical_and(core == self.e, zz == self.zz))

    def is_home(self, z):
        return jnp.logical_and(self.stays, z == self.z)


def remote(src, dst, send, recv, device):
    return pltpu.make_async_remote_copy(
        src_ref=src, dst_ref=dst, send_sem=send, recv_sem=recv, device_id=device, device_id_type=MESH
    )


def arrived(ref, sem):
    pltpu.make_async_copy(ref, ref, sem).wait()


def send_or_copy(here, src, dst, send, recv, device):
    @pl.when(here)
    def _():
        pltpu.make_async_copy(src, dst, recv).start()

    @pl.when(jnp.logical_not(here))
    def _():
        remote(src, dst, send, recv, device).start()


def greet(device):
    pl.semaphore_signal(pltpu.get_barrier_semaphore(), inc=1, device_id=device, device_id_type=MESH)


def greet_all(at):
    def plane(n, carry):
        greet(at.plane(n))
        return carry

    lax.fori_loop(1, COLS, plane, 0)

    def worker(n, carry):
        core, zz = lax.div(n, 4), lax.rem(n, 4)

        @pl.when(jnp.logical_not(at.is_worker(core, zz)))
        def _():
            greet(at.worker(core, zz))

        return carry

    lax.fori_loop(0, 8, worker, 0)

    def home(n, carry):
        greet(at.home(n * 2 + 1 - at.e))
        return carry

    lax.fori_loop(0, 4, home, 0)

    @pl.when(jnp.logical_not(at.stays))
    def _():
        def column(n, carry):
            greet(at.swapped(n))
            return carry

        lax.fori_loop(0, COLS, column, 0)

    return jnp.where(at.stays, COLS - 1 + 7 + 4, COLS - 1 + 8 + 4 + COLS)


def exchange_start(at, source, slot, send, recv):
    def column(n, carry):
        t = lax.rem(at.c + n, COLS)
        here = jnp.logical_and(n == 0, at.stays)
        send_or_copy(here, source.at[t], slot, send.at[t], recv.at[at.c], at.swapped(t))
        return carry

    lax.fori_loop(0, COLS, column, 0)


def exchange_arrived(landing, recv):
    def column(n, carry):
        arrived(landing.at[n], recv.at[n])
        return carry

    lax.fori_loop(0, COLS, column, 0)


def exchange_sent(at, source, send):
    def column(n, carry):
        t = lax.rem(at.c + n, COLS)

        @pl.when(jnp.logical_or(n > 0, jnp.logical_not(at.stays)))
        def _():
            arrived(source.at[t], send.at[t])

        return carry

    lax.fori_loop(0, COLS, column, 0)


def repeat_heads(w_bias_t):
    wide = jnp.concatenate([w_bias_t[...].astype(F32), jnp.zeros((C - H, C), F32)], axis=0).T
    lane = lax.div(lax.broadcasted_iota(jnp.int32, (C, H * SLOT), 1), SLOT)
    total = jnp.zeros((C, H * SLOT), F32)
    for h in range(H):
        total = jnp.where(lane == h, wide[:, h : h + 1], total)
    return total.astype(BF16)


def only_row(repeated, i):
    lane = lax.rem(lax.broadcasted_iota(jnp.int32, (1, H * SLOT), 1), SLOT)
    return repeated * (lane == i).astype(F32).astype(BF16)


def standardize(values):
    centre = values - jnp.mean(values, axis=-1, keepdims=True)
    inverse = lax.rsqrt(jnp.mean(centre * centre, axis=-1, keepdims=True) + 1e-5)
    return centre * inverse, jnp.broadcast_to(inverse, values.shape)


def norm_backward(grad, unit, inverse):
    mean_grad = jnp.mean(grad, axis=-1, keepdims=True)
    mean_cross = jnp.mean(grad * unit, axis=-1, keepdims=True)
    return inverse * (grad - mean_grad - unit * mean_cross)


MAIN_SCRATCH = dict(
    pair=((TALL, WIDTH, C), BF16),
    cot=((TALL, WIDTH, C), BF16),
    residues=((1, WIDTH), jnp.int32),
    gain=((1, C), F32),
    shift=((1, C), F32),
    w_proj=((C, 4 * HD), BF16),
    gate_bias=((1, HD), F32),
    w_bias_t=((H, C), BF16),
    w_out=((HD, C), BF16),
    home_unit=((TALL, WIDTH, C), F32),
    home_rstd=((TALL, WIDTH, C), F32),
    scores=((H, OWN, N, N), F32),
    d_prob=((H, OWN, N, N), F32),
    m1=((COLS, PADDED, C), BF16),
    m2=((COLS, PADDED, C), BF16),
    in1=((COLS, PADDED, C), BF16),
    in2=((COLS, PADDED, C), BF16),
    flags=((WIDTH, C), F32),
    w_proj_t=((3 * HD, C), BF16),
    w_rep=((C, H * SLOT), BF16),
    home_rows=((TALL, WIDTH, C), F32),
    zpack=((2, WIDTH, PAIR), F32),
    zin=((ROWS, WIDTH, PAIR), F32),
    bias=((H, COLS, WIDTH, N), F32),
    d_bias=((H, COLS, WIDTH, N), F32),
    d_other=((2, COLS, WIDTH, N), F32),
    stage_far=((4, WIDTH, N), F32),
    d_far=((2, 3, 4 * WIDTH, N), BF16),
    d_far_in=((2, 3, 4 * WIDTH, N), BF16),
    d_near=((2, 4, WIDTH, N), F32),
    d_near_in=((2, 3, WIDTH, N), F32),
    zout=((ROWS, WIDTH, PAIR), F32),
    hin=((2, 4, WIDTH, PAIR), F32),
    mask=((COLS, WIDTH, C), F32),
    row_mask=((OWN, 1, C), F32),
    normed=((OWN, N, C), BF16),
    unit=((OWN, N, C), F32),
    rstd=((OWN, N, C), F32),
    q=((OWN, N, C), BF16),
    k=((OWN, N, C), BF16),
    v=((OWN, N, C), BF16),
    d=((OWN, N, C), BF16),
    q_t=((OWN, C, N), BF16),
    k_t=((OWN, C, N), BF16),
    v_t=((OWN, C, N), BF16),
    d_t=((OWN, C, N), BF16),
    gate=((OWN, N, C), F32),
    dgate=((OWN, N, C), F32),
    att_t=((OWN, HD, N), F32),

    dq_t=((OWN, HD, N), F32),
    dk=((OWN, N, HD), F32),
    dv=((OWN, N, HD), F32),
    proj=((C, 4 * HD), F32),
    proj_b=((C, 4 * HD), BF16),
    r5=((COLS, 16, 2 * HD), BF16),
    v5=((16, 2 * HD), F32),
    r6=((8, 16, 2 * HD), F32),
    v6=((16, 2 * HD), BF16),
    out=((OWN, COLS, 2 * WIDTH, C), BF16),
)
MAIN_SEMS = dict(
    operand=(9,),
    norm=(2,),
    in1=(COLS,),
    in2=(COLS,),
    z=(8,),
    near=(2, 3),
    far=(2, 4, 3),
    partner=(2,),
    back=(2,),
    d_far=(2, 3),
    d_near=(2, 3),
    dz=(8,),
    p1=(COLS,),
    p2=(8,),
    p3=(COLS,),
    out=(OWN, COLS),
)
MAIN_IN = 10
MAIN_OUT = 5


class Names:
    pass


def main_kernel(*refs):
    length, operands = refs[0], refs[1:MAIN_IN]
    (land, proj_out, h_sum, unit_out, rstd_out) = refs[MAIN_IN : MAIN_IN + MAIN_OUT]
    rest = refs[MAIN_IN + MAIN_OUT :]
    m, send, recv = Names(), Names(), Names()
    for name, ref in zip(MAIN_SCRATCH, rest):
        setattr(m, name, ref)
    rest = rest[len(MAIN_SCRATCH) :]
    for name, ref in zip(MAIN_SEMS, rest):
        setattr(send, name, ref)
    for name, ref in zip(MAIN_SEMS, rest[len(MAIN_SEMS) :]):
        setattr(recv, name, ref)
    held = (m.pair, m.cot, m.residues, m.gain, m.shift, m.w_proj, m.gate_bias, m.w_bias_t, m.w_out)
    pair, cot, residues, gain, shift, w_proj, gate_bias, w_bias_t, w_out = held
    for n in range(MAIN_IN - 1):
        pltpu.make_async_copy(operands[n], held[n], recv.operand.at[n]).start()
    at = Place()
    e = at.e
    count = greet_all(at)
    for n in range(MAIN_IN - 1):
        arrived(held[n], recv.operand.at[n])

    sublane = lax.broadcasted_iota(jnp.int32, (WIDTH, WIDTH), 0)
    lane = lax.broadcasted_iota(jnp.int32, (WIDTH, WIDTH), 1)
    valid = jnp.where(lane + at.c * WIDTH < length[0], residues[...], 0).astype(F32)
    valid = jnp.sum(jnp.where(lane == sublane, valid, 0.0), axis=1, keepdims=True)
    m.flags[...] = jnp.broadcast_to(valid, (WIDTH, C))
    lane = lax.broadcasted_iota(jnp.int32, (8, C), 1)
    packed_flags = jnp.where(
        lane == 0, m.flags[0:8, :], jnp.where(lane == 1, m.flags[8:16, :], m.flags[16:24, :])
    )
    pad = jnp.zeros((COLS, PADDED - PART, C), F32)
    m.m1[...] = jnp.concatenate(
        [
            pair[...].astype(F32).reshape(COLS, PART, C),
            jnp.broadcast_to(packed_flags[None], (COLS, PADDED - PART, C)),
        ],
        axis=1,
    ).astype(BF16)
    m.m2[...] = jnp.concatenate([cot[...].astype(F32).reshape(COLS, PART, C), pad], axis=1).astype(BF16)

    m.w_rep[...] = repeat_heads(w_bias_t)
    unit, inverse = standardize(pair[...].astype(F32).reshape(TALL * WIDTH, C))
    m.home_unit[...] = unit.reshape(TALL, WIDTH, C)
    m.home_rstd[...] = inverse.reshape(TALL, WIDTH, C)
    m.home_rows[...] = (unit * gain[...] + shift[...]).reshape(TALL, WIDTH, C)

    def home_bias(n, total):
        for i in range(8):
            rows = m.home_rows[n * 8 + i].astype(BF16)
            total = total + jnp.dot(rows, only_row(m.w_rep[...], n * 8 + i), preferred_element_type=F32)
        return total

    packed = lax.fori_loop(0, TALL // 8, home_bias, jnp.zeros((WIDTH, H * SLOT), F32))
    negative = (m.flags[...] - 1.0) * 1e9
    m.zpack[0] = packed[:, :PAIR] + negative
    m.zpack[1] = packed[:, PAIR:] + negative

    pl.semaphore_wait(pltpu.get_barrier_semaphore(), count)

    def to_workers(n, carry):
        core, zz = lax.div(n, 4), lax.rem(n, 4)
        send_or_copy(
            at.is_worker(core, zz),
            m.zpack.at[core],
            m.zin.at[at.z],
            send.z.at[n],
            recv.z.at[at.z],
            at.worker(core, zz),
        )
        return carry

    lax.fori_loop(0, 8, to_workers, 0)
    exchange_start(at, m.m1, m.in1.at[at.c], send.in1, recv.in1)
    exchange_start(at, m.m2, m.in2.at[at.c], send.in2, recv.in2)
    pltpu.make_async_copy(m.home_unit, unit_out, recv.norm.at[0]).start()
    pltpu.make_async_copy(m.home_rstd, rstd_out, recv.norm.at[1]).start()

    m.w_proj_t[...] = w_proj[:, : 3 * HD].astype(F32).T.astype(BF16)
    m.d_bias[...] = jnp.zeros_like(m.d_bias)
    m.dk[...] = jnp.zeros_like(m.dk)
    m.dv[...] = jnp.zeros_like(m.dv)
    m.proj[...] = jnp.zeros_like(m.proj)
    exchange_arrived(m.in1, recv.in1)

    for s in range(OWN):
        values = m.in1[:, s * WIDTH : (s + 1) * WIDTH, :].astype(F32).reshape(N, C)
        unit, inverse = standardize(values)
        m.unit[s] = unit
        m.rstd[s] = inverse
        m.normed[s] = (unit * gain[...] + shift[...]).astype(BF16)

    def bias_block(hh, a, b):
        return m.bias.at[e * 2 + hh, at.col(at.f - a + 4, at.g - b + 4)]

    def to_far(hh, a):
        block = bias_block(hh, a, 0)
        for n in (1, 2, 3):
            remote(block, block, send.far.at[hh, a, n - 1], recv.far.at[hh, a, n - 1], at.gpeer(n)).start()

    def forward(hh):
        for n in (1, 2, 3):
            arrived(bias_block(hh, n, 0), recv.near.at[hh, n - 1])
            to_far(hh, n)

    for z in range(ROWS):
        arrived(m.zin.at[z], recv.z.at[z])
    for hh in range(2):
        head = e * 2 + hh
        m.bias[head, at.c] = jnp.concatenate(
            [m.zin[z][:, hh * SLOT : hh * SLOT + TALL] for z in range(ROWS)], axis=1
        )
        mine = m.bias.at[head, at.c]
        for n in (1, 2, 3):
            remote(mine, mine, send.near.at[hh, n - 1], recv.near.at[hh, n - 1], at.fpeer(n)).start()
        to_far(hh, 0)

    for s in range(OWN):
        rows = m.normed[s]
        flat = jnp.dot(rows, w_proj[...], preferred_element_type=F32)
        m.q[s] = (flat[:, :HD] * SCALE).astype(BF16)
        m.k[s] = flat[:, HD : 2 * HD].astype(BF16)
        m.v[s] = flat[:, 2 * HD : 3 * HD].astype(BF16)
        m.gate[s] = jax.nn.sigmoid(flat[:, 3 * HD :] + gate_bias[...])
        flat_t = lax.dot_general(m.w_proj_t[...], rows, NT, preferred_element_type=F32)
        m.q_t[s] = (flat_t[:HD] * SCALE).astype(BF16)
        m.k_t[s] = flat_t[HD : 2 * HD].astype(BF16)
        m.v_t[s] = flat_t[2 * HD : 3 * HD].astype(BF16)

    forward(0)
    forward(1)
    exchange_arrived(m.in2, recv.in2)
    tiles = m.in1[:, PART:, :].astype(F32)
    for t in range(3):
        rows = jnp.broadcast_to(tiles[:, :, t : t + 1], (COLS, 8, C))
        m.mask[:, t * 8 : (t + 1) * 8, :] = rows
    for s in range(OWN):
        values = m.in2[:, s * WIDTH : (s + 1) * WIDTH, :].astype(F32).reshape(N, C)
        row = at.row0 + s
        own_mask = m.mask[lax.div(row, WIDTH), pl.ds(lax.rem(row, WIDTH), 1), :]
        m.row_mask[s] = own_mask
        pair_mask = m.mask[...].reshape(N, C) * own_mask
        d_out = jnp.where(pair_mask > 0, values, 0.0).astype(BF16)
        d_gated = lax.dot_general(d_out, w_out[...], NT, preferred_element_type=F32)
        gates = m.gate[s]
        d_attn = d_gated * gates
        m.d[s] = d_attn.astype(BF16)
        m.d_t[s] = d_attn.T.astype(BF16)
        m.dgate[s] = d_attn * (1.0 - gates)

    def products(h, carry):
        row = lax.div(lax.broadcasted_iota(jnp.int32, (C, N), 0), DH)
        by_row = (row == h).astype(F32).astype(BF16)
        for s in range(OWN):
            m.scores[h, s] = jnp.dot(m.k[s], m.q_t[s] * by_row, preferred_element_type=F32)
            m.d_prob[h, s] = jnp.dot(m.v[s], m.d_t[s] * by_row, preferred_element_type=F32)
        return carry

    lax.fori_loop(0, H, products, 0)

    def own_bias_arrived(hh):
        for a in range(4):
            for n in (1, 2, 3):
                arrived(bias_block(hh, a, n), recv.far.at[hh, a, n - 1])
        whole = m.bias.at[e * 2 + hh]
        remote(whole, whole, send.partner.at[hh], recv.partner.at[hh], at.partner()).start()

    def other_bias_arrived(hh):
        arrived(m.bias.at[(1 - e) * 2 + hh], recv.partner.at[hh])

    def attend(h, then=None):
        here = pl.ds(pl.multiple_of(h * DH, DH), DH)
        lane = lax.div(lax.broadcasted_iota(jnp.int32, (C, C), 1), DH)
        by_lane = (lane == h).astype(F32).astype(BF16)

        def one_row(s, carry):
            keys_t, values_t = m.k_t[s, here, :], m.v_t[s, here, :]
            dk_sum = dv_sum = None
            for n in range(3):
                lanes = slice(n * C, (n + 1) * C)
                scores = m.scores[h, s, :, lanes] + m.bias[h, :, :, lanes].reshape(N, C)
                exponent = jnp.exp(scores - jnp.max(scores, axis=0, keepdims=True))
                weights = exponent * (1.0 / jnp.sum(exponent, axis=0, keepdims=True))
                weights_b = weights.astype(BF16)
                attended = jnp.dot(values_t, weights_b, preferred_element_type=F32)
                m.att_t[s, here, lanes] = attended
                delta = jnp.sum(attended * m.d_t[s, here, lanes].astype(F32), axis=0, keepdims=True)
                d_score = weights * (m.d_prob[h, s, :, lanes] - delta)
                d_score_b = d_score.astype(BF16)
                m.d_bias[h, :, :, lanes] += d_score.reshape(COLS, WIDTH, C)
                m.dq_t[s, here, lanes] = jnp.dot(keys_t, d_score_b, preferred_element_type=F32)
                dv_part = jnp.dot(weights_b, m.d[s, lanes, :] * by_lane, preferred_element_type=F32)
                dk_part = jnp.dot(d_score_b, m.q[s, lanes, :] * by_lane, preferred_element_type=F32)
                dv_sum = dv_part if dv_sum is None else dv_sum + dv_part
                dk_sum = dk_part if dk_sum is None else dk_sum + dk_part
            m.dk[s] += dk_sum
            m.dv[s] += dv_sum
            if then is not None:
                then(s)
            return carry

        lax.fori_loop(0, OWN, one_row, 0)

    def to_other(hh):
        head = (1 - e) * 2 + hh
        remote(m.d_bias.at[head], m.d_other.at[hh], send.back.at[hh], recv.back.at[hh], at.partner()).start()

    def scatter_far(hh):
        head = e * 2 + hh
        arrived(m.d_other.at[hh], recv.back.at[hh])
        for n in (1, 2, 3, 0):
            for f in range(4):
                column = at.col(f, at.g + n)
                both = m.d_bias[head, column] + m.d_other[hh, column]
                if n == 0:
                    m.d_near[hh, f] = both
                else:
                    m.stage_far[f] = both
            if n > 0:
                m.d_far[hh, n - 1] = m.stage_far[...].reshape(4 * WIDTH, N).astype(BF16)
                remote(
                    m.d_far.at[hh, n - 1],
                    m.d_far_in.at[hh, n - 1],
                    send.d_far.at[hh, n - 1],
                    recv.d_far.at[hh, n - 1],
                    at.gpeer(n),
                ).start()

    def scatter_near(hh):
        for n in range(3):
            arrived(m.d_far_in.at[hh, n], recv.d_far.at[hh, n])
        far = (m.d_far_in[hh, 0].astype(F32) + m.d_far_in[hh, 1].astype(F32)) + m.d_far_in[hh, 2].astype(F32)
        m.d_near[hh] += far.reshape(4, WIDTH, N)
        for n in (1, 2, 3):
            remote(
                m.d_near.at[hh, lax.rem(at.f + n, 4)],
                m.d_near_in.at[hh, n - 1],
                send.d_near.at[hh, n - 1],
                recv.d_near.at[hh, n - 1],
                at.fpeer(n),
            ).start()

    def plane_sum(hh):
        for n in range(3):
            arrived(m.d_near_in.at[hh, n], recv.d_near.at[hh, n])
        return (m.d_near[hh, at.f] + m.d_near_in[hh, 0]) + (m.d_near_in[hh, 1] + m.d_near_in[hh, 2])

    def finish_row(s):
        attended = m.att_t[s].T
        gated = (m.gate[s] * attended).astype(BF16)
        pair_mask = m.mask[...].reshape(N, C) * m.row_mask[s]
        update = jnp.dot(gated, w_out[...], preferred_element_type=F32) * pair_mask
        d_proj = jnp.concatenate(
            [m.dq_t[s].T * SCALE, m.dk[s], m.dv[s], m.dgate[s] * attended], axis=1
        ).astype(BF16)
        d_normed = lax.dot_general(d_proj, w_proj[...], NT, preferred_element_type=F32)
        result = norm_backward(d_normed * gain[...], m.unit[s], m.rstd[s])
        m.out[s] = jnp.concatenate(
            [update.reshape(COLS, WIDTH, C), result.reshape(COLS, WIDTH, C)], axis=1
        ).astype(BF16)
        normed_t = m.normed[s].astype(F32).T.astype(BF16)
        m.proj[...] += jnp.dot(normed_t, d_proj, preferred_element_type=F32)

    own_bias_arrived(0)
    attend(e * 2)
    own_bias_arrived(1)
    other_bias_arrived(0)
    attend(2 - e * 2)
    to_other(0)
    other_bias_arrived(1)
    attend(3 - e * 2)
    to_other(1)
    scatter_far(0)
    attend(e * 2 + 1, finish_row)
    scatter_far(1)

    def piece(ref, c):
        rows = pl.ds(pl.multiple_of(lax.div(c, 2) * 16, 16), 16)
        return ref.at[rows, pl.ds(pl.multiple_of(lax.rem(c, 2) * 2 * HD, 2 * HD), 2 * HD)]

    m.proj_b[...] = m.proj[...].astype(BF16)

    def scatter_proj(n, carry):
        t = lax.rem(at.c + n, COLS)
        remote(piece(m.proj_b, t), m.r5.at[n], send.p1.at[n], recv.p1.at[n], at.plane(n)).start()
        return carry

    lax.fori_loop(1, COLS, scatter_proj, 0)
    scatter_near(0)
    scatter_near(1)

    def proj_arrived(n, total):
        arrived(m.r5.at[n], recv.p1.at[n])
        return total + m.r5[n].astype(F32)

    m.v5[...] = lax.fori_loop(1, COLS, proj_arrived, piece(m.proj, at.c)[...])

    def proj_to_homes(z, carry):
        slot = e * 4 + at.zz
        send_or_copy(at.is_home(z), m.v5, m.r6.at[slot], send.p2.at[z], recv.p2.at[slot], at.home(z))
        return carry

    lax.fori_loop(0, ROWS, proj_to_homes, 0)

    for s in range(OWN):
        exchange_start(at, m.out.at[s], land.at[at.c, s], send.out.at[s], recv.out.at[s])
    halves = [plane_sum(0), plane_sum(1)]
    blank = jnp.zeros((WIDTH, SLOT - TALL), F32)
    for z in range(ROWS):
        mine = slice(z * TALL, (z + 1) * TALL)
        m.zout[z] = jnp.concatenate([halves[0][:, mine], blank, halves[1][:, mine], blank], axis=1)

    def to_homes(z, carry):
        send_or_copy(
            at.is_home(z),
            m.zout.at[z],
            m.hin.at[e, at.zz],
            send.dz.at[z],
            recv.dz.at[e * 4 + at.zz],
            at.home(z),
        )
        return carry

    lax.fori_loop(0, ROWS, to_homes, 0)


    def share_arrived(n, total):
        arrived(m.r6.at[n], recv.p2.at[n])
        return total + m.r6[n]

    m.v6[...] = lax.fori_loop(0, 8, share_arrived, jnp.zeros((16, 2 * HD), F32)).astype(BF16)
    own_piece = piece(proj_out, at.c)
    pltpu.make_async_copy(m.v6, own_piece, recv.p3.at[0]).start()

    def spread(n, carry):
        remote(m.v6, own_piece, send.p3.at[n], recv.p3.at[n], at.plane(n)).start()
        return carry

    lax.fori_loop(1, COLS, spread, 0)

    for core in range(2):
        for zz in range(4):
            arrived(m.hin.at[core, zz], recv.dz.at[core * 4 + zz])
        lanes = slice(core * PAIR, (core + 1) * PAIR)
        h_sum[:, lanes] = (m.hin[core, 0] + m.hin[core, 1]) + (m.hin[core, 2] + m.hin[core, 3])
    for s in range(OWN):
        exchange_arrived(land.at[:, s], recv.out.at[s])

    def out_arrived(n, carry):
        arrived(piece(proj_out, lax.rem(at.c - n + COLS, COLS)), recv.p3.at[n])
        return carry

    lax.fori_loop(0, COLS, out_arrived, 0)

    arrived(unit_out, recv.norm.at[0])
    arrived(rstd_out, recv.norm.at[1])

    def column_sent(n, carry):
        arrived(m.v6, send.p1.at[n])
        arrived(m.v6, send.p3.at[n])
        return carry

    lax.fori_loop(1, COLS, column_sent, 0)

    def column_group_sent(n, carry):
        @pl.when(jnp.logical_not(at.is_worker(lax.div(n, 4), lax.rem(n, 4))))
        def _():
            arrived(m.zpack.at[0], send.z.at[n])

        @pl.when(jnp.logical_not(at.is_home(n)))
        def _():
            arrived(m.zout.at[0], send.dz.at[n])
            arrived(m.v5, send.p2.at[n])

        return carry

    lax.fori_loop(0, 8, column_group_sent, 0)
    for hh in range(2):
        for n in range(3):
            arrived(m.bias.at[0, 0], send.near.at[hh, n])
            for a in range(4):
                arrived(m.bias.at[0, 0], send.far.at[hh, a, n])
            arrived(m.d_far.at[0, 0], send.d_far.at[hh, n])
            arrived(m.d_near.at[0, 0], send.d_near.at[hh, n])
        arrived(m.bias.at[0], send.partner.at[hh])
        arrived(m.d_bias.at[0], send.back.at[hh])
    exchange_sent(at, m.m1, send.in1)
    exchange_sent(at, m.m2, send.in2)
    for s in range(OWN):
        exchange_sent(at, m.out.at[s], send.out.at[s])


STEPS = 2


def finish_kernel(
    land, proj_in, h_sum, unit, rstd, gain, w_bias_t, update, pair_grad, proj_out, w_rep, split, share
):
    tall = TALL // STEPS
    step = pl.program_id(0)

    @pl.when(step == 0)
    def _():
        proj_out[...] = proj_in[...].astype(F32)
        w_rep[...] = repeat_heads(w_bias_t)
        total = h_sum[...]
        for n in range(3):
            term = total.astype(BF16).astype(F32)
            split[n * WIDTH : (n + 1) * WIDTH, :] = term
            total = total - term

    landed = land[...].astype(F32)
    update[...] = landed[:, :, :WIDTH, :].reshape(tall, WIDTH, C).astype(BF16)
    share[...] = landed[:, :, WIDTH:, :].reshape(tall, WIDTH, C)
    terms = split[...].astype(BF16)
    for i in range(tall):
        parts = lax.dot_general(
            terms, only_row(w_rep[...], step * tall + i), NT, preferred_element_type=F32
        )
        grad = (parts[2 * WIDTH :] + parts[WIDTH : 2 * WIDTH]) + parts[:WIDTH]
        result = norm_backward(grad * gain[...], unit[i], rstd[i])
        pair_grad[i] = (share[i] + result).astype(BF16)


def vmem(count):
    return [pl.BlockSpec(memory_space=pltpu.VMEM)] * count


def shards(
    pair_act, cotangent, ln_gain, ln_shift, w_proj, gate_bias, w_bias, w_out, residue_mask, valid_length
):
    any_space = pl.BlockSpec(memory_space=pl.ANY)
    gain = ln_gain.reshape(1, C)
    sems = [pltpu.SemaphoreType.DMA(shape) for shape in MAIN_SEMS.values()]
    landing = jax.ShapeDtypeStruct((COLS, OWN, 2 * WIDTH, C), BF16)
    block = jax.ShapeDtypeStruct(pair_act.shape, F32)
    proj_shape = jax.ShapeDtypeStruct((C, 4 * HD), F32)
    land, proj, h_sum, unit, rstd = pl.pallas_call(
        main_kernel,
        out_shape=[
            landing,
            jax.ShapeDtypeStruct((C, 4 * HD), BF16),
            jax.ShapeDtypeStruct((WIDTH, H * SLOT), F32),
            block,
            block,
        ],
        in_specs=[pl.BlockSpec(memory_space=pltpu.SMEM)] + [any_space] * (MAIN_IN - 1),
        out_specs=[any_space] * 2 + vmem(1) + [any_space] * 2,
        scratch_shapes=[pltpu.VMEM(shape, dtype) for shape, dtype in MAIN_SCRATCH.values()] + sems + sems,
        compiler_params=pltpu.CompilerParams(
            collective_id=0, has_side_effects=True, vmem_limit_bytes=VMEM_LIMIT
        ),
        name="main",
    )(
        valid_length,
        pair_act,
        cotangent,
        residue_mask.reshape(1, WIDTH),
        gain,
        ln_shift.reshape(1, C),
        w_proj,
        gate_bias.reshape(1, HD),
        w_bias.T,
        w_out,
    )
    result = jax.ShapeDtypeStruct(pair_act.shape, BF16)
    tall = TALL // STEPS
    rows = pl.BlockSpec((tall, WIDTH, C), lambda n: (n, 0, 0))
    landed = pl.BlockSpec((COLS // STEPS, OWN, 2 * WIDTH, C), lambda n: (n, 0, 0, 0))

    def whole(*shape):
        return pl.BlockSpec(shape, lambda n: (0,) * len(shape))

    return pl.pallas_call(
        finish_kernel,
        out_shape=[result, result, proj_shape],
        grid=(STEPS,),
        in_specs=[
            landed,
            whole(C, 4 * HD),
            whole(WIDTH, H * SLOT),
            rows,
            rows,
            whole(1, C),
            whole(H, C),
        ],
        out_specs=[rows, rows, whole(C, 4 * HD)],
        scratch_shapes=[
            pltpu.VMEM((C, H * SLOT), BF16),
            pltpu.VMEM((3 * WIDTH, H * SLOT), F32),
            pltpu.VMEM((tall, WIDTH, C), F32),
        ],
        compiler_params=pltpu.CompilerParams(vmem_limit_bytes=VMEM_LIMIT),
        name="finish",
    )(land, proj, h_sum, unit, rstd, gain, w_bias.T)


def solution(mesh):
    return jax.shard_map(
        shards,
        mesh=mesh,
        in_specs=(
            P(("complex", "row"), "col", None),
            P(("complex", "row"), "col", None),
            P(),
            P(),
            P(),
            P(),
            P(),
            P(),
            P(("complex", "col")),
            P("complex"),
        ),
        out_specs=(
            P(("complex", "row"), "col", None),
            P(("complex", "row"), "col", None),
            P("complex", None),
        ),
        check_vma=False,
    )
```

```python
import jax
import jax.numpy as jnp
from jax import lax
from jax.experimental import pallas as pl
from jax.experimental.pallas import tpu as pltpu
from jax.sharding import PartitionSpec as P

MESH = pl.DeviceIdType.MESH
F32 = jnp.float32
BF16 = jnp.bfloat16
N = 384
C = 128
H = 4
DH = 32
HD = H * DH
COLS = 16
ROWS = 8
WIDTH = N // COLS
TALL = N // ROWS
OWN = 3
PART = OWN * WIDTH
PADDED = 80
SLOT = 64
PAIR = 2 * SLOT
SCALE = DH ** (-0.5)
VMEM_LIMIT = 60 * 1024 * 1024
NT = (((1,), (1,)), ((), ()))


class Place:
    def __init__(self):
        self.e = lax.axis_index("complex")
        self.z = lax.axis_index("row")
        self.c = lax.axis_index("col")
        self.part = lax.rem(self.z, 2)
        self.zz = lax.div(self.z, 2)
        self.stays = self.part == self.e
        self.y = lax.div(self.c, 4)
        self.x = lax.rem(self.c, 4)
        self.f = self.x * (1 - self.e) + self.y * self.e
        self.g = self.y * (1 - self.e) + self.x * self.e
        self.row0 = (self.zz * 2 + self.e) * TALL + self.c * OWN

    def swapped(self, c):
        return (self.part, self.zz * 2 + self.e, c)

    def col(self, f, g):
        return lax.rem(f, 4) * (1 + 3 * self.e) + lax.rem(g, 4) * (4 - 3 * self.e)

    def fpeer(self, n):
        return (self.e, self.z, self.col(self.f + n, self.g))

    def gpeer(self, n):
        return (self.e, self.z, self.col(self.f, self.g + n))

    def plane(self, n):
        return (self.e, self.z, lax.rem(self.c + n, COLS))

    def partner(self):
        return (1 - self.e, self.z, self.c)

    def worker(self, core, zz):
        return (core, zz * 2 + self.e, self.c)

    def home(self, z):
        return (self.part, z, self.c)

    def is_worker(self, core, zz):
        return jnp.logical_and(self.stays, jnp.logical_and(core == self.e, zz == self.zz))

    def is_home(self, z):
        return jnp.logical_and(self.stays, z == self.z)


def remote(src, dst, send, recv, device):
    return pltpu.make_async_remote_copy(
        src_ref=src, dst_ref=dst, send_sem=send, recv_sem=recv, device_id=device, device_id_type=MESH
    )


def arrived(ref, sem):
    pltpu.make_async_copy(ref, ref, sem).wait()


def send_or_copy(here, src, dst, send, recv, device):
    @pl.when(here)
    def _():
        pltpu.make_async_copy(src, dst, recv).start()

    @pl.when(jnp.logical_not(here))
    def _():
        remote(src, dst, send, recv, device).start()


def greet(device):
    pl.semaphore_signal(pltpu.get_barrier_semaphore(), inc=1, device_id=device, device_id_type=MESH)


def greet_all(at):
    def plane(n, carry):
        greet(at.plane(n))
        return carry

    lax.fori_loop(1, COLS, plane, 0)

    def worker(n, carry):
        core, zz = lax.div(n, 4), lax.rem(n, 4)

        @pl.when(jnp.logical_not(at.is_worker(core, zz)))
        def _():
            greet(at.worker(core, zz))

        return carry

    lax.fori_loop(0, 8, worker, 0)

    def home(n, carry):
        greet(at.home(n * 2 + 1 - at.e))
        return carry

    lax.fori_loop(0, 4, home, 0)

    @pl.when(jnp.logical_not(at.stays))
    def _():
        def column(n, carry):
            greet(at.swapped(n))
            return carry

        lax.fori_loop(0, COLS, column, 0)

    return jnp.where(at.stays, COLS - 1 + 7 + 4, COLS - 1 + 8 + 4 + COLS)


def exchange_start(at, source, slot, send, recv):
    def column(n, carry):
        t = lax.rem(at.c + n, COLS)
        here = jnp.logical_and(n == 0, at.stays)
        send_or_copy(here, source.at[t], slot, send.at[t], recv.at[at.c], at.swapped(t))
        return carry

    lax.fori_loop(0, COLS, column, 0)


def exchange_arrived(landing, recv):
    def column(n, carry):
        arrived(landing.at[n], recv.at[n])
        return carry

    lax.fori_loop(0, COLS, column, 0)


def exchange_sent(at, source, send):
    def column(n, carry):
        t = lax.rem(at.c + n, COLS)

        @pl.when(jnp.logical_or(n > 0, jnp.logical_not(at.stays)))
        def _():
            arrived(source.at[t], send.at[t])

        return carry

    lax.fori_loop(0, COLS, column, 0)


def repeat_heads(w_bias_t):
    wide = jnp.concatenate([w_bias_t[...].astype(F32), jnp.zeros((C - H, C), F32)], axis=0).T
    lane = lax.div(lax.broadcasted_iota(jnp.int32, (C, H * SLOT), 1), SLOT)
    total = jnp.zeros((C, H * SLOT), F32)
    for h in range(H):
        total = jnp.where(lane == h, wide[:, h : h + 1], total)
    return total.astype(BF16)


def only_row(repeated, i):
    lane = lax.rem(lax.broadcasted_iota(jnp.int32, (1, H * SLOT), 1), SLOT)
    return repeated * (lane == i).astype(F32).astype(BF16)


def standardize(values):
    centre = values - jnp.mean(values, axis=-1, keepdims=True)
    inverse = lax.rsqrt(jnp.mean(centre * centre, axis=-1, keepdims=True) + 1e-5)
    return centre * inverse, jnp.broadcast_to(inverse, values.shape)


def norm_backward(grad, unit, inverse):
    mean_grad = jnp.mean(grad, axis=-1, keepdims=True)
    mean_cross = jnp.mean(grad * unit, axis=-1, keepdims=True)
    return inverse * (grad - mean_grad - unit * mean_cross)


MAIN_SCRATCH = dict(
    pair=((TALL, WIDTH, C), BF16),
    cot=((TALL, WIDTH, C), BF16),
    residues=((1, WIDTH), jnp.int32),
    gain=((1, C), F32),
    shift=((1, C), F32),
    w_proj=((C, 4 * HD), BF16),
    gate_bias=((1, HD), F32),
    w_bias_t=((H, C), BF16),
    w_out=((HD, C), BF16),
    home_unit=((TALL, WIDTH, C), F32),
    home_rstd=((TALL, WIDTH, C), F32),
    scores=((H, OWN, N, N), F32),
    d_prob=((H, OWN, N, N), F32),
    m1=((COLS, PADDED, C), BF16),
    m2=((COLS, PADDED, C), BF16),
    in1=((COLS, PADDED, C), BF16),
    in2=((COLS, PADDED, C), BF16),
    flags=((WIDTH, C), F32),
    w_proj_t=((3 * HD, C), BF16),
    w_rep=((C, H * SLOT), BF16),
    home_rows=((TALL, WIDTH, C), F32),
    zpack=((2, WIDTH, PAIR), F32),
    zin=((ROWS, WIDTH, PAIR), F32),
    bias=((H, COLS, WIDTH, N), F32),
    d_bias=((H, COLS, WIDTH, N), F32),
    d_other=((2, COLS, WIDTH, N), F32),
    stage_far=((4, WIDTH, N), F32),
    d_far=((2, 3, 4 * WIDTH, N), BF16),
    d_far_in=((2, 3, 4 * WIDTH, N), BF16),
    d_near=((2, 4, WIDTH, N), F32),
    d_near_in=((2, 3, WIDTH, N), F32),
    zout=((ROWS, WIDTH, PAIR), F32),
    hin=((2, 4, WIDTH, PAIR), F32),
    mask=((COLS, WIDTH, C), F32),
    row_mask=((OWN, 1, C), F32),
    normed=((OWN, N, C), BF16),
    unit=((OWN, N, C), F32),
    rstd=((OWN, N, C), F32),
    q=((OWN, N, C), BF16),
    k=((OWN, N, C), BF16),
    v=((OWN, N, C), BF16),
    d=((OWN, N, C), BF16),
    q_t=((OWN, C, N), BF16),
    k_t=((OWN, C, N), BF16),
    v_t=((OWN, C, N), BF16),
    d_t=((OWN, C, N), BF16),
    gate=((OWN, N, C), F32),
    dgate=((OWN, N, C), F32),
    att_t=((OWN, HD, N), F32),

    dq_t=((OWN, HD, N), F32),
    dk=((OWN, N, HD), F32),
    dv=((OWN, N, HD), F32),
    proj=((C, 4 * HD), F32),
    proj_b=((C, 4 * HD), BF16),
    r5=((COLS, 16, 2 * HD), BF16),
    v5=((16, 2 * HD), F32),
    r6=((8, 16, 2 * HD), F32),
    v6=((16, 2 * HD), BF16),
    out=((OWN, COLS, 2 * WIDTH, C), BF16),
)
MAIN_SEMS = dict(
    operand=(9,),
    norm=(2,),
    in1=(COLS,),
    in2=(COLS,),
    z=(8,),
    near=(2, 3),
    far=(2, 4, 3),
    partner=(2,),
    back=(2,),
    d_far=(2, 3),
    d_near=(2, 3),
    dz=(8,),
    p1=(COLS,),
    p2=(8,),
    p3=(COLS,),
    out=(OWN, COLS),
)
MAIN_IN = 10
MAIN_OUT = 5


class Names:
    pass


def main_kernel(*refs):
    length, operands = refs[0], refs[1:MAIN_IN]
    (land, proj_out, h_sum, unit_out, rstd_out) = refs[MAIN_IN : MAIN_IN + MAIN_OUT]
    rest = refs[MAIN_IN + MAIN_OUT :]
    m, send, recv = Names(), Names(), Names()
    for name, ref in zip(MAIN_SCRATCH, rest):
        setattr(m, name, ref)
    rest = rest[len(MAIN_SCRATCH) :]
    for name, ref in zip(MAIN_SEMS, rest):
        setattr(send, name, ref)
    for name, ref in zip(MAIN_SEMS, rest[len(MAIN_SEMS) :]):
        setattr(recv, name, ref)
    held = (m.pair, m.cot, m.residues, m.gain, m.shift, m.w_proj, m.gate_bias, m.w_bias_t, m.w_out)
    pair, cot, residues, gain, shift, w_proj, gate_bias, w_bias_t, w_out = held
    for n in range(MAIN_IN - 1):
        pltpu.make_async_copy(operands[n], held[n], recv.operand.at[n]).start()
    at = Place()
    e = at.e
    count = greet_all(at)
    for n in range(MAIN_IN - 1):
        arrived(held[n], recv.operand.at[n])

    sublane = lax.broadcasted_iota(jnp.int32, (WIDTH, WIDTH), 0)
    lane = lax.broadcasted_iota(jnp.int32, (WIDTH, WIDTH), 1)
    valid = jnp.where(lane + at.c * WIDTH < length[0], residues[...], 0).astype(F32)
    valid = jnp.sum(jnp.where(lane == sublane, valid, 0.0), axis=1, keepdims=True)
    m.flags[...] = jnp.broadcast_to(valid, (WIDTH, C))
    lane = lax.broadcasted_iota(jnp.int32, (8, C), 1)
    packed_flags = jnp.where(
        lane == 0, m.flags[0:8, :], jnp.where(lane == 1, m.flags[8:16, :], m.flags[16:24, :])
    )
    pad = jnp.zeros((COLS, PADDED - PART, C), F32)
    m.m1[...] = jnp.concatenate(
        [
            pair[...].astype(F32).reshape(COLS, PART, C),
            jnp.broadcast_to(packed_flags[None], (COLS, PADDED - PART, C)),
        ],
        axis=1,
    ).astype(BF16)
    m.m2[...] = jnp.concatenate([cot[...].astype(F32).reshape(COLS, PART, C), pad], axis=1).astype(BF16)

    m.w_rep[...] = repeat_heads(w_bias_t)
    unit, inverse = standardize(pair[...].astype(F32).reshape(TALL * WIDTH, C))
    m.home_unit[...] = unit.reshape(TALL, WIDTH, C)
    m.home_rstd[...] = inverse.reshape(TALL, WIDTH, C)
    m.home_rows[...] = (unit * gain[...] + shift[...]).reshape(TALL, WIDTH, C)

    def home_bias(n, total):
        for i in range(8):
            rows = m.home_rows[n * 8 + i].astype(BF16)
            total = total + jnp.dot(rows, only_row(m.w_rep[...], n * 8 + i), preferred_element_type=F32)
        return total

    packed = lax.fori_loop(0, TALL // 8, home_bias, jnp.zeros((WIDTH, H * SLOT), F32))
    negative = (m.flags[...] - 1.0) * 1e9
    m.zpack[0] = packed[:, :PAIR] + negative
    m.zpack[1] = packed[:, PAIR:] + negative

    pl.semaphore_wait(pltpu.get_barrier_semaphore(), count)

    def to_workers(n, carry):
        core, zz = lax.div(n, 4), lax.rem(n, 4)
        send_or_copy(
            at.is_worker(core, zz),
            m.zpack.at[core],
            m.zin.at[at.z],
            send.z.at[n],
            recv.z.at[at.z],
            at.worker(core, zz),
        )
        return carry

    lax.fori_loop(0, 8, to_workers, 0)
    exchange_start(at, m.m1, m.in1.at[at.c], send.in1, recv.in1)
    exchange_start(at, m.m2, m.in2.at[at.c], send.in2, recv.in2)
    pltpu.make_async_copy(m.home_unit, unit_out, recv.norm.at[0]).start()
    pltpu.make_async_copy(m.home_rstd, rstd_out, recv.norm.at[1]).start()

    m.w_proj_t[...] = w_proj[:, : 3 * HD].astype(F32).T.astype(BF16)
    m.dk[...] = jnp.zeros_like(m.dk)
    m.dv[...] = jnp.zeros_like(m.dv)
    m.proj[...] = jnp.zeros_like(m.proj)
    exchange_arrived(m.in1, recv.in1)

    for s in range(OWN):
        values = m.in1[:, s * WIDTH : (s + 1) * WIDTH, :].astype(F32).reshape(N, C)
        unit, inverse = standardize(values)
        m.unit[s] = unit
        m.rstd[s] = inverse
        m.normed[s] = (unit * gain[...] + shift[...]).astype(BF16)

    def bias_block(hh, a, b):
        return m.bias.at[e * 2 + hh, at.col(at.f - a + 4, at.g - b + 4)]

    def to_far(hh, a):
        block = bias_block(hh, a, 0)
        for n in (1, 2, 3):
            remote(block, block, send.far.at[hh, a, n - 1], recv.far.at[hh, a, n - 1], at.gpeer(n)).start()

    def forward(hh):
        for n in (1, 2, 3):
            arrived(bias_block(hh, n, 0), recv.near.at[hh, n - 1])
            to_far(hh, n)

    for z in range(ROWS):
        arrived(m.zin.at[z], recv.z.at[z])
    for hh in range(2):
        head = e * 2 + hh
        m.bias[head, at.c] = jnp.concatenate(
            [m.zin[z][:, hh * SLOT : hh * SLOT + TALL] for z in range(ROWS)], axis=1
        )
        mine = m.bias.at[head, at.c]
        for n in (1, 2, 3):
            remote(mine, mine, send.near.at[hh, n - 1], recv.near.at[hh, n - 1], at.fpeer(n)).start()
        to_far(hh, 0)

    for s in range(OWN):
        rows = m.normed[s]
        flat = jnp.dot(rows, w_proj[...], preferred_element_type=F32)
        m.q[s] = (flat[:, :HD] * SCALE).astype(BF16)
        m.k[s] = flat[:, HD : 2 * HD].astype(BF16)
        m.v[s] = flat[:, 2 * HD : 3 * HD].astype(BF16)
        m.gate[s] = jax.nn.sigmoid(flat[:, 3 * HD :] + gate_bias[...])
        flat_t = lax.dot_general(m.w_proj_t[...], rows, NT, preferred_element_type=F32)
        m.q_t[s] = (flat_t[:HD] * SCALE).astype(BF16)
        m.k_t[s] = flat_t[HD : 2 * HD].astype(BF16)
        m.v_t[s] = flat_t[2 * HD : 3 * HD].astype(BF16)

    forward(0)
    forward(1)
    exchange_arrived(m.in2, recv.in2)
    tiles = m.in1[:, PART:, :].astype(F32)
    for t in range(3):
        rows = jnp.broadcast_to(tiles[:, :, t : t + 1], (COLS, 8, C))
        m.mask[:, t * 8 : (t + 1) * 8, :] = rows
    for s in range(OWN):
        values = m.in2[:, s * WIDTH : (s + 1) * WIDTH, :].astype(F32).reshape(N, C)
        row = at.row0 + s
        own_mask = m.mask[lax.div(row, WIDTH), pl.ds(lax.rem(row, WIDTH), 1), :]
        m.row_mask[s] = own_mask
        pair_mask = m.mask[...].reshape(N, C) * own_mask
        d_out = jnp.where(pair_mask > 0, values, 0.0).astype(BF16)
        d_gated = lax.dot_general(d_out, w_out[...], NT, preferred_element_type=F32)
        gates = m.gate[s]
        d_attn = d_gated * gates
        m.d[s] = d_attn.astype(BF16)
        m.d_t[s] = d_attn.T.astype(BF16)
        m.dgate[s] = d_attn * (1.0 - gates)

    def products(h, carry):
        row = lax.div(lax.broadcasted_iota(jnp.int32, (C, N), 0), DH)
        by_row = (row == h).astype(F32).astype(BF16)
        for s in range(OWN):
            m.scores[h, s] = jnp.dot(m.k[s], m.q_t[s] * by_row, preferred_element_type=F32)
            m.d_prob[h, s] = jnp.dot(m.v[s], m.d_t[s] * by_row, preferred_element_type=F32)
        return carry

    lax.fori_loop(0, H, products, 0)

    def own_bias_arrived(hh):
        for a in range(4):
            for n in (1, 2, 3):
                arrived(bias_block(hh, a, n), recv.far.at[hh, a, n - 1])
        whole = m.bias.at[e * 2 + hh]
        remote(whole, whole, send.partner.at[hh], recv.partner.at[hh], at.partner()).start()

    def other_bias_arrived(hh):
        arrived(m.bias.at[(1 - e) * 2 + hh], recv.partner.at[hh])

    def attend(h):
        here = pl.ds(pl.multiple_of(h * DH, DH), DH)
        lane = lax.div(lax.broadcasted_iota(jnp.int32, (1, C), 1), DH)
        by_lane = (lane == h).astype(F32).astype(BF16)
        dk, dv = [None] * OWN, [None] * OWN
        for n in range(3):
            lanes = slice(n * C, (n + 1) * C)
            d_bias = None
            for s in range(OWN):
                scores = m.scores[h, s, :, lanes] + m.bias[h, :, :, lanes].reshape(N, C)
                exponent = jnp.exp(scores - jnp.max(scores, axis=0, keepdims=True))
                weights = exponent * (1.0 / jnp.sum(exponent, axis=0, keepdims=True))
                weights_b = weights.astype(BF16)
                m.att_t[s, here, lanes] = jnp.dot(
                    m.v_t[s, here, :], weights_b, preferred_element_type=F32
                )
                d_prob = m.d_prob[h, s, :, lanes]
                d_score = weights * (d_prob - jnp.sum(weights * d_prob, axis=0, keepdims=True))
                d_score_b = d_score.astype(BF16)
                d_bias = d_score if d_bias is None else d_bias + d_score
                m.dq_t[s, here, lanes] = jnp.dot(
                    m.k_t[s, here, :], d_score_b, preferred_element_type=F32
                )
                dv_part = jnp.dot(weights_b, m.d[s, lanes, :] * by_lane, preferred_element_type=F32)
                dk_part = jnp.dot(d_score_b, m.q[s, lanes, :] * by_lane, preferred_element_type=F32)
                dv[s] = dv_part if dv[s] is None else dv[s] + dv_part
                dk[s] = dk_part if dk[s] is None else dk[s] + dk_part
            m.d_bias[h, :, :, lanes] = d_bias.reshape(COLS, WIDTH, C)
        for s in range(OWN):
            m.dk[s] += dk[s]
            m.dv[s] += dv[s]

    def to_other(hh):
        head = (1 - e) * 2 + hh
        remote(m.d_bias.at[head], m.d_other.at[hh], send.back.at[hh], recv.back.at[hh], at.partner()).start()

    def scatter_far(hh):
        head = e * 2 + hh
        arrived(m.d_other.at[hh], recv.back.at[hh])
        for n in (1, 2, 3, 0):
            for f in range(4):
                column = at.col(f, at.g + n)
                both = m.d_bias[head, column] + m.d_other[hh, column]
                if n == 0:
                    m.d_near[hh, f] = both
                else:
                    m.stage_far[f] = both
            if n > 0:
                m.d_far[hh, n - 1] = m.stage_far[...].reshape(4 * WIDTH, N).astype(BF16)
                remote(
                    m.d_far.at[hh, n - 1],
                    m.d_far_in.at[hh, n - 1],
                    send.d_far.at[hh, n - 1],
                    recv.d_far.at[hh, n - 1],
                    at.gpeer(n),
                ).start()

    def scatter_near(hh):
        for n in range(3):
            arrived(m.d_far_in.at[hh, n], recv.d_far.at[hh, n])
        far = (m.d_far_in[hh, 0].astype(F32) + m.d_far_in[hh, 1].astype(F32)) + m.d_far_in[hh, 2].astype(F32)
        m.d_near[hh] += far.reshape(4, WIDTH, N)
        for n in (1, 2, 3):
            remote(
                m.d_near.at[hh, lax.rem(at.f + n, 4)],
                m.d_near_in.at[hh, n - 1],
                send.d_near.at[hh, n - 1],
                recv.d_near.at[hh, n - 1],
                at.fpeer(n),
            ).start()

    def plane_sum(hh):
        for n in range(3):
            arrived(m.d_near_in.at[hh, n], recv.d_near.at[hh, n])
        return (m.d_near[hh, at.f] + m.d_near_in[hh, 0]) + (m.d_near_in[hh, 1] + m.d_near_in[hh, 2])

    def finish_row(s):
        attended = m.att_t[s].T
        gated = (m.gate[s] * attended).astype(BF16)
        pair_mask = m.mask[...].reshape(N, C) * m.row_mask[s]
        update = jnp.dot(gated, w_out[...], preferred_element_type=F32) * pair_mask
        d_proj = jnp.concatenate(
            [m.dq_t[s].T * SCALE, m.dk[s], m.dv[s], m.dgate[s] * attended], axis=1
        ).astype(BF16)
        d_normed = lax.dot_general(d_proj, w_proj[...], NT, preferred_element_type=F32)
        result = norm_backward(d_normed * gain[...], m.unit[s], m.rstd[s])
        m.out[s] = jnp.concatenate(
            [update.reshape(COLS, WIDTH, C), result.reshape(COLS, WIDTH, C)], axis=1
        ).astype(BF16)
        normed_t = m.normed[s].astype(F32).T.astype(BF16)
        m.proj[...] += jnp.dot(normed_t, d_proj, preferred_element_type=F32)

    own_bias_arrived(0)
    attend(e * 2)
    own_bias_arrived(1)
    other_bias_arrived(0)
    attend(2 - e * 2)
    to_other(0)
    other_bias_arrived(1)
    attend(3 - e * 2)
    to_other(1)
    scatter_far(0)
    attend(e * 2 + 1)
    scatter_far(1)
    for s in range(OWN):
        finish_row(s)

    def piece(ref, c):
        rows = pl.ds(pl.multiple_of(lax.div(c, 2) * 16, 16), 16)
        return ref.at[rows, pl.ds(pl.multiple_of(lax.rem(c, 2) * 2 * HD, 2 * HD), 2 * HD)]

    m.proj_b[...] = m.proj[...].astype(BF16)

    def scatter_proj(n, carry):
        t = lax.rem(at.c + n, COLS)
        remote(piece(m.proj_b, t), m.r5.at[n], send.p1.at[n], recv.p1.at[n], at.plane(n)).start()
        return carry

    lax.fori_loop(1, COLS, scatter_proj, 0)
    scatter_near(0)
    scatter_near(1)

    def proj_arrived(n, total):
        arrived(m.r5.at[n], recv.p1.at[n])
        return total + m.r5[n].astype(F32)

    m.v5[...] = lax.fori_loop(1, COLS, proj_arrived, piece(m.proj, at.c)[...])

    def proj_to_homes(z, carry):
        slot = e * 4 + at.zz
        send_or_copy(at.is_home(z), m.v5, m.r6.at[slot], send.p2.at[z], recv.p2.at[slot], at.home(z))
        return carry

    lax.fori_loop(0, ROWS, proj_to_homes, 0)

    for s in range(OWN):
        exchange_start(at, m.out.at[s], land.at[at.c, s], send.out.at[s], recv.out.at[s])
    halves = [plane_sum(0), plane_sum(1)]
    blank = jnp.zeros((WIDTH, SLOT - TALL), F32)
    for z in range(ROWS):
        mine = slice(z * TALL, (z + 1) * TALL)
        m.zout[z] = jnp.concatenate([halves[0][:, mine], blank, halves[1][:, mine], blank], axis=1)

    def to_homes(z, carry):
        send_or_copy(
            at.is_home(z),
            m.zout.at[z],
            m.hin.at[e, at.zz],
            send.dz.at[z],
            recv.dz.at[e * 4 + at.zz],
            at.home(z),
        )
        return carry

    lax.fori_loop(0, ROWS, to_homes, 0)


    def share_arrived(n, total):
        arrived(m.r6.at[n], recv.p2.at[n])
        return total + m.r6[n]

    m.v6[...] = lax.fori_loop(0, 8, share_arrived, jnp.zeros((16, 2 * HD), F32)).astype(BF16)
    own_piece = piece(proj_out, at.c)
    pltpu.make_async_copy(m.v6, own_piece, recv.p3.at[0]).start()

    def spread(n, carry):
        remote(m.v6, own_piece, send.p3.at[n], recv.p3.at[n], at.plane(n)).start()
        return carry

    lax.fori_loop(1, COLS, spread, 0)

    for core in range(2):
        for zz in range(4):
            arrived(m.hin.at[core, zz], recv.dz.at[core * 4 + zz])
        lanes = slice(core * PAIR, (core + 1) * PAIR)
        h_sum[:, lanes] = (m.hin[core, 0] + m.hin[core, 1]) + (m.hin[core, 2] + m.hin[core, 3])
    for s in range(OWN):
        exchange_arrived(land.at[:, s], recv.out.at[s])

    def out_arrived(n, carry):
        arrived(piece(proj_out, lax.rem(at.c - n + COLS, COLS)), recv.p3.at[n])
        return carry

    lax.fori_loop(0, COLS, out_arrived, 0)

    arrived(unit_out, recv.norm.at[0])
    arrived(rstd_out, recv.norm.at[1])

    def column_sent(n, carry):
        arrived(m.v6, send.p1.at[n])
        arrived(m.v6, send.p3.at[n])
        return carry

    lax.fori_loop(1, COLS, column_sent, 0)

    def column_group_sent(n, carry):
        @pl.when(jnp.logical_not(at.is_worker(lax.div(n, 4), lax.rem(n, 4))))
        def _():
            arrived(m.zpack.at[0], send.z.at[n])

        @pl.when(jnp.logical_not(at.is_home(n)))
        def _():
            arrived(m.zout.at[0], send.dz.at[n])
            arrived(m.v5, send.p2.at[n])

        return carry

    lax.fori_loop(0, 8, column_group_sent, 0)
    for hh in range(2):
        for n in range(3):
            arrived(m.bias.at[0, 0], send.near.at[hh, n])
            for a in range(4):
                arrived(m.bias.at[0, 0], send.far.at[hh, a, n])
            arrived(m.d_far.at[0, 0], send.d_far.at[hh, n])
            arrived(m.d_near.at[0, 0], send.d_near.at[hh, n])
        arrived(m.bias.at[0], send.partner.at[hh])
        arrived(m.d_bias.at[0], send.back.at[hh])
    exchange_sent(at, m.m1, send.in1)
    exchange_sent(at, m.m2, send.in2)
    for s in range(OWN):
        exchange_sent(at, m.out.at[s], send.out.at[s])


STEPS = 2


def finish_kernel(
    land, proj_in, h_sum, unit, rstd, gain, w_bias_t, update, pair_grad, proj_out, w_rep, split, share
):
    tall = TALL // STEPS
    step = pl.program_id(0)

    @pl.when(step == 0)
    def _():
        proj_out[...] = proj_in[...].astype(F32)
        w_rep[...] = repeat_heads(w_bias_t)
        total = h_sum[...]
        for n in range(3):
            term = total.astype(BF16).astype(F32)
            split[n * WIDTH : (n + 1) * WIDTH, :] = term
            total = total - term

    landed = land[...].astype(F32)
    update[...] = landed[:, :, :WIDTH, :].reshape(tall, WIDTH, C).astype(BF16)
    share[...] = landed[:, :, WIDTH:, :].reshape(tall, WIDTH, C)
    terms = split[...].astype(BF16)
    for i in range(tall):
        parts = lax.dot_general(
            terms, only_row(w_rep[...], step * tall + i), NT, preferred_element_type=F32
        )
        grad = (parts[2 * WIDTH :] + parts[WIDTH : 2 * WIDTH]) + parts[:WIDTH]
        result = norm_backward(grad * gain[...], unit[i], rstd[i])
        pair_grad[i] = (share[i] + result).astype(BF16)


def vmem(count):
    return [pl.BlockSpec(memory_space=pltpu.VMEM)] * count


def shards(
    pair_act, cotangent, ln_gain, ln_shift, w_proj, gate_bias, w_bias, w_out, residue_mask, valid_length
):
    any_space = pl.BlockSpec(memory_space=pl.ANY)
    gain = ln_gain.reshape(1, C)
    sems = [pltpu.SemaphoreType.DMA(shape) for shape in MAIN_SEMS.values()]
    landing = jax.ShapeDtypeStruct((COLS, OWN, 2 * WIDTH, C), BF16)
    block = jax.ShapeDtypeStruct(pair_act.shape, F32)
    proj_shape = jax.ShapeDtypeStruct((C, 4 * HD), F32)
    land, proj, h_sum, unit, rstd = pl.pallas_call(
        main_kernel,
        out_shape=[
            landing,
            jax.ShapeDtypeStruct((C, 4 * HD), BF16),
            jax.ShapeDtypeStruct((WIDTH, H * SLOT), F32),
            block,
            block,
        ],
        in_specs=[pl.BlockSpec(memory_space=pltpu.SMEM)] + [any_space] * (MAIN_IN - 1),
        out_specs=[any_space] * 2 + vmem(1) + [any_space] * 2,
        scratch_shapes=[pltpu.VMEM(shape, dtype) for shape, dtype in MAIN_SCRATCH.values()] + sems + sems,
        compiler_params=pltpu.CompilerParams(
            collective_id=0, has_side_effects=True, vmem_limit_bytes=VMEM_LIMIT
        ),
        name="main",
    )(
        valid_length,
        pair_act,
        cotangent,
        residue_mask.reshape(1, WIDTH),
        gain,
        ln_shift.reshape(1, C),
        w_proj,
        gate_bias.reshape(1, HD),
        w_bias.T,
        w_out,
    )
    result = jax.ShapeDtypeStruct(pair_act.shape, BF16)
    tall = TALL // STEPS
    rows = pl.BlockSpec((tall, WIDTH, C), lambda n: (n, 0, 0))
    landed = pl.BlockSpec((COLS // STEPS, OWN, 2 * WIDTH, C), lambda n: (n, 0, 0, 0))

    def whole(*shape):
        return pl.BlockSpec(shape, lambda n: (0,) * len(shape))

    return pl.pallas_call(
        finish_kernel,
        out_shape=[result, result, proj_shape],
        grid=(STEPS,),
        in_specs=[
            landed,
            whole(C, 4 * HD),
            whole(WIDTH, H * SLOT),
            rows,
            rows,
            whole(1, C),
            whole(H, C),
        ],
        out_specs=[rows, rows, whole(C, 4 * HD)],
        scratch_shapes=[
            pltpu.VMEM((C, H * SLOT), BF16),
            pltpu.VMEM((3 * WIDTH, H * SLOT), F32),
            pltpu.VMEM((tall, WIDTH, C), F32),
        ],
        compiler_params=pltpu.CompilerParams(vmem_limit_bytes=VMEM_LIMIT),
        name="finish",
    )(land, proj, h_sum, unit, rstd, gain, w_bias.T)


def solution(mesh):
    return jax.shard_map(
        shards,
        mesh=mesh,
        in_specs=(
            P(("complex", "row"), "col", None),
            P(("complex", "row"), "col", None),
            P(),
            P(),
            P(),
            P(),
            P(),
            P(),
            P(("complex", "col")),
            P("complex"),
        ),
        out_specs=(
            P(("complex", "row"), "col", None),
            P(("complex", "row"), "col", None),
            P("complex", None),
        ),
        check_vma=False,
    )
```

```python
import jax
import jax.numpy as jnp
from jax import lax
from jax.experimental import pallas as pl
from jax.experimental.pallas import tpu as pltpu
from jax.sharding import PartitionSpec as P

MESH = pl.DeviceIdType.MESH
F32 = jnp.float32
BF16 = jnp.bfloat16
N = 384
C = 128
H = 4
DH = 32
HD = H * DH
COLS = 16
ROWS = 8
WIDTH = N // COLS
TALL = N // ROWS
OWN = 3
PART = OWN * WIDTH
PADDED = 80
SLOT = 64
PAIR = 2 * SLOT
SCALE = DH ** (-0.5)
VMEM_LIMIT = 60 * 1024 * 1024
NT = (((1,), (1,)), ((), ()))


class Place:
    def __init__(self):
        self.e = lax.axis_index("complex")
        self.z = lax.axis_index("row")
        self.c = lax.axis_index("col")
        self.part = lax.rem(self.z, 2)
        self.zz = lax.div(self.z, 2)
        self.stays = self.part == self.e
        self.y = lax.div(self.c, 4)
        self.x = lax.rem(self.c, 4)
        self.f = self.x * (1 - self.e) + self.y * self.e
        self.g = self.y * (1 - self.e) + self.x * self.e
        self.row0 = (self.zz * 2 + self.e) * TALL + self.c * OWN

    def swapped(self, c):
        return (self.part, self.zz * 2 + self.e, c)

    def col(self, f, g):
        return lax.rem(f, 4) * (1 + 3 * self.e) + lax.rem(g, 4) * (4 - 3 * self.e)

    def fpeer(self, n):
        return (self.e, self.z, self.col(self.f + n, self.g))

    def gpeer(self, n):
        return (self.e, self.z, self.col(self.f, self.g + n))

    def plane(self, n):
        return (self.e, self.z, lax.rem(self.c + n, COLS))

    def partner(self):
        return (1 - self.e, self.z, self.c)

    def worker(self, core, zz):
        return (core, zz * 2 + self.e, self.c)

    def home(self, z):
        return (self.part, z, self.c)

    def is_worker(self, core, zz):
        return jnp.logical_and(self.stays, jnp.logical_and(core == self.e, zz == self.zz))

    def is_home(self, z):
        return jnp.logical_and(self.stays, z == self.z)


def remote(src, dst, send, recv, device):
    return pltpu.make_async_remote_copy(
        src_ref=src, dst_ref=dst, send_sem=send, recv_sem=recv, device_id=device, device_id_type=MESH
    )


def arrived(ref, sem):
    pltpu.make_async_copy(ref, ref, sem).wait()


def send_or_copy(here, src, dst, send, recv, device):
    @pl.when(here)
    def _():
        pltpu.make_async_copy(src, dst, recv).start()

    @pl.when(jnp.logical_not(here))
    def _():
        remote(src, dst, send, recv, device).start()


def greet(device):
    pl.semaphore_signal(pltpu.get_barrier_semaphore(), inc=1, device_id=device, device_id_type=MESH)


def greet_all(at):
    def plane(n, carry):
        greet(at.plane(n))
        return carry

    lax.fori_loop(1, COLS, plane, 0)

    def worker(n, carry):
        core, zz = lax.div(n, 4), lax.rem(n, 4)

        @pl.when(jnp.logical_not(at.is_worker(core, zz)))
        def _():
            greet(at.worker(core, zz))

        return carry

    lax.fori_loop(0, 8, worker, 0)

    def home(n, carry):
        greet(at.home(n * 2 + 1 - at.e))
        return carry

    lax.fori_loop(0, 4, home, 0)

    @pl.when(jnp.logical_not(at.stays))
    def _():
        def column(n, carry):
            greet(at.swapped(n))
            return carry

        lax.fori_loop(0, COLS, column, 0)

    return jnp.where(at.stays, COLS - 1 + 7 + 4, COLS - 1 + 8 + 4 + COLS)


def exchange_start(at, source, slot, send, recv):
    def column(n, carry):
        t = lax.rem(at.c + n, COLS)
        here = jnp.logical_and(n == 0, at.stays)
        send_or_copy(here, source.at[t], slot, send.at[t], recv.at[at.c], at.swapped(t))
        return carry

    lax.fori_loop(0, COLS, column, 0)


def exchange_arrived(landing, recv):
    def column(n, carry):
        arrived(landing.at[n], recv.at[n])
        return carry

    lax.fori_loop(0, COLS, column, 0)


def exchange_sent(at, source, send):
    def column(n, carry):
        t = lax.rem(at.c + n, COLS)

        @pl.when(jnp.logical_or(n > 0, jnp.logical_not(at.stays)))
        def _():
            arrived(source.at[t], send.at[t])

        return carry

    lax.fori_loop(0, COLS, column, 0)


def repeat_heads(w_bias_t):
    wide = jnp.concatenate([w_bias_t[...].astype(F32), jnp.zeros((C - H, C), F32)], axis=0).T
    lane = lax.div(lax.broadcasted_iota(jnp.int32, (C, H * SLOT), 1), SLOT)
    total = jnp.zeros((C, H * SLOT), F32)
    for h in range(H):
        total = jnp.where(lane == h, wide[:, h : h + 1], total)
    return total.astype(BF16)


def only_row(repeated, i):
    lane = lax.rem(lax.broadcasted_iota(jnp.int32, (1, H * SLOT), 1), SLOT)
    return repeated * (lane == i).astype(F32).astype(BF16)


def standardize(values):
    centre = values - jnp.mean(values, axis=-1, keepdims=True)
    inverse = lax.rsqrt(jnp.mean(centre * centre, axis=-1, keepdims=True) + 1e-5)
    return centre * inverse, jnp.broadcast_to(inverse, values.shape)


def norm_backward(grad, unit, inverse):
    mean_grad = jnp.mean(grad, axis=-1, keepdims=True)
    mean_cross = jnp.mean(grad * unit, axis=-1, keepdims=True)
    return inverse * (grad - mean_grad - unit * mean_cross)


MAIN_SCRATCH = dict(
    pair=((TALL, WIDTH, C), BF16),
    cot=((TALL, WIDTH, C), BF16),
    residues=((1, WIDTH), jnp.int32),
    gain=((1, C), F32),
    shift=((1, C), F32),
    w_proj=((C, 4 * HD), BF16),
    gate_bias=((1, HD), F32),
    w_bias_t=((H, C), BF16),
    w_out=((HD, C), BF16),
    home_unit=((TALL, WIDTH, C), F32),
    home_rstd=((TALL, WIDTH, C), F32),
    scores=((H, OWN, N, N), F32),
    d_prob=((H, OWN, N, N), F32),
    m1=((COLS, PADDED, C), BF16),
    m2=((COLS, PADDED, C), BF16),
    in1=((COLS, PADDED, C), BF16),
    in2=((COLS, PADDED, C), BF16),
    flags=((WIDTH, C), F32),
    w_proj_t=((3 * HD, C), BF16),
    w_rep=((C, H * SLOT), BF16),
    home_rows=((TALL, WIDTH, C), F32),
    zpack=((2, WIDTH, PAIR), F32),
    zin=((ROWS, WIDTH, PAIR), F32),
    bias=((H, COLS, WIDTH, N), F32),
    d_bias=((H, COLS, WIDTH, N), F32),
    d_other=((2, COLS, WIDTH, N), F32),
    stage_far=((4, WIDTH, N), F32),
    d_far=((2, 3, 4 * WIDTH, N), BF16),
    d_far_in=((2, 3, 4 * WIDTH, N), BF16),
    d_near=((2, 4, WIDTH, N), F32),
    d_near_in=((2, 3, WIDTH, N), F32),
    zout=((ROWS, WIDTH, PAIR), F32),
    hin=((2, 4, WIDTH, PAIR), F32),
    mask=((COLS, WIDTH, C), F32),
    row_mask=((OWN, 1, C), F32),
    normed=((OWN, N, C), BF16),
    unit=((OWN, N, C), F32),
    rstd=((OWN, N, C), F32),
    q=((OWN, N, C), BF16),
    k=((OWN, N, C), BF16),
    v=((OWN, N, C), BF16),
    d=((OWN, N, C), BF16),
    q_t=((OWN, C, N), BF16),
    k_t=((OWN, C, N), BF16),
    v_t=((OWN, C, N), BF16),
    d_t=((OWN, C, N), BF16),
    gate=((OWN, N, C), F32),
    dgate=((OWN, N, C), F32),
    att_t=((OWN, HD, N), F32),

    dq_t=((OWN, HD, N), F32),
    dk=((OWN, N, HD), F32),
    dv=((OWN, N, HD), F32),
    proj=((C, 4 * HD), F32),
    proj_b=((C, 4 * HD), BF16),
    r5=((COLS, 16, 2 * HD), BF16),
    v5=((16, 2 * HD), F32),
    r6=((8, 16, 2 * HD), F32),
    v6=((16, 2 * HD), BF16),
    out=((COLS, OWN, 2 * WIDTH, C), BF16),
)
MAIN_SEMS = dict(
    operand=(9,),
    norm=(2,),
    in1=(COLS,),
    in2=(COLS,),
    z=(8,),
    near=(2, 3),
    far=(2, 4, 3),
    partner=(2,),
    back=(2,),
    d_far=(2, 3),
    d_near=(2, 3),
    dz=(8,),
    p1=(COLS,),
    p2=(8,),
    p3=(COLS,),
    out=(2, COLS),
)
MAIN_IN = 10
MAIN_OUT = 5


class Names:
    pass


def main_kernel(*refs):
    length, operands = refs[0], refs[1:MAIN_IN]
    (land, proj_out, h_sum, unit_out, rstd_out) = refs[MAIN_IN : MAIN_IN + MAIN_OUT]
    rest = refs[MAIN_IN + MAIN_OUT :]
    m, send, recv = Names(), Names(), Names()
    for name, ref in zip(MAIN_SCRATCH, rest):
        setattr(m, name, ref)
    rest = rest[len(MAIN_SCRATCH) :]
    for name, ref in zip(MAIN_SEMS, rest):
        setattr(send, name, ref)
    for name, ref in zip(MAIN_SEMS, rest[len(MAIN_SEMS) :]):
        setattr(recv, name, ref)
    held = (m.pair, m.cot, m.residues, m.gain, m.shift, m.w_proj, m.gate_bias, m.w_bias_t, m.w_out)
    pair, cot, residues, gain, shift, w_proj, gate_bias, w_bias_t, w_out = held
    for n in range(MAIN_IN - 1):
        pltpu.make_async_copy(operands[n], held[n], recv.operand.at[n]).start()
    at = Place()
    e = at.e
    count = greet_all(at)
    for n in range(MAIN_IN - 1):
        arrived(held[n], recv.operand.at[n])

    sublane = lax.broadcasted_iota(jnp.int32, (WIDTH, WIDTH), 0)
    lane = lax.broadcasted_iota(jnp.int32, (WIDTH, WIDTH), 1)
    valid = jnp.where(lane + at.c * WIDTH < length[0], residues[...], 0).astype(F32)
    valid = jnp.sum(jnp.where(lane == sublane, valid, 0.0), axis=1, keepdims=True)
    m.flags[...] = jnp.broadcast_to(valid, (WIDTH, C))
    m.w_rep[...] = repeat_heads(w_bias_t)
    unit, inverse = standardize(pair[...].astype(F32).reshape(TALL * WIDTH, C))
    m.home_unit[...] = unit.reshape(TALL, WIDTH, C)
    m.home_rstd[...] = inverse.reshape(TALL, WIDTH, C)
    m.home_rows[...] = (unit * gain[...] + shift[...]).reshape(TALL, WIDTH, C)

    def home_bias(n, total):
        for i in range(8):
            rows = m.home_rows[n * 8 + i].astype(BF16)
            total = total + jnp.dot(rows, only_row(m.w_rep[...], n * 8 + i), preferred_element_type=F32)
        return total

    packed = lax.fori_loop(0, TALL // 8, home_bias, jnp.zeros((WIDTH, H * SLOT), F32))
    negative = (m.flags[...] - 1.0) * 1e9
    m.zpack[0] = packed[:, :PAIR] + negative
    m.zpack[1] = packed[:, PAIR:] + negative

    pl.semaphore_wait(pltpu.get_barrier_semaphore(), count)

    def to_workers(n, carry):
        core, zz = lax.div(n, 4), lax.rem(n, 4)
        send_or_copy(
            at.is_worker(core, zz),
            m.zpack.at[core],
            m.zin.at[at.z],
            send.z.at[n],
            recv.z.at[at.z],
            at.worker(core, zz),
        )
        return carry

    lax.fori_loop(0, 8, to_workers, 0)
    lane = lax.broadcasted_iota(jnp.int32, (8, C), 1)
    packed_flags = jnp.where(
        lane == 0, m.flags[0:8, :], jnp.where(lane == 1, m.flags[8:16, :], m.flags[16:24, :])
    )
    pad = jnp.zeros((COLS, PADDED - PART, C), F32)
    m.m1[...] = jnp.concatenate(
        [
            pair[...].astype(F32).reshape(COLS, PART, C),
            jnp.broadcast_to(packed_flags[None], (COLS, PADDED - PART, C)),
        ],
        axis=1,
    ).astype(BF16)
    m.m2[...] = jnp.concatenate([cot[...].astype(F32).reshape(COLS, PART, C), pad], axis=1).astype(BF16)

    exchange_start(at, m.m1, m.in1.at[at.c], send.in1, recv.in1)
    exchange_start(at, m.m2, m.in2.at[at.c], send.in2, recv.in2)
    pltpu.make_async_copy(m.home_unit, unit_out, recv.norm.at[0]).start()
    pltpu.make_async_copy(m.home_rstd, rstd_out, recv.norm.at[1]).start()

    m.w_proj_t[...] = w_proj[:, : 3 * HD].astype(F32).T.astype(BF16)
    m.dk[...] = jnp.zeros_like(m.dk)
    m.dv[...] = jnp.zeros_like(m.dv)
    m.proj[...] = jnp.zeros_like(m.proj)
    def bias_block(hh, a, b):
        return m.bias.at[e * 2 + hh, at.col(at.f - a + 4, at.g - b + 4)]

    def to_far(hh, a):
        block = bias_block(hh, a, 0)
        for n in (1, 2, 3):
            remote(block, block, send.far.at[hh, a, n - 1], recv.far.at[hh, a, n - 1], at.gpeer(n)).start()

    def forward(hh):
        for n in (1, 2, 3):
            arrived(bias_block(hh, n, 0), recv.near.at[hh, n - 1])
            to_far(hh, n)

    for z in range(ROWS):
        arrived(m.zin.at[z], recv.z.at[z])
    for hh in range(2):
        head = e * 2 + hh
        m.bias[head, at.c] = jnp.concatenate(
            [m.zin[z][:, hh * SLOT : hh * SLOT + TALL] for z in range(ROWS)], axis=1
        )
        mine = m.bias.at[head, at.c]
        for n in (1, 2, 3):
            remote(mine, mine, send.near.at[hh, n - 1], recv.near.at[hh, n - 1], at.fpeer(n)).start()
        to_far(hh, 0)

    forward(0)
    forward(1)
    exchange_arrived(m.in1, recv.in1)

    for s in range(OWN):
        values = m.in1[:, s * WIDTH : (s + 1) * WIDTH, :].astype(F32).reshape(N, C)
        unit, inverse = standardize(values)
        m.unit[s] = unit
        m.rstd[s] = inverse
        m.normed[s] = (unit * gain[...] + shift[...]).astype(BF16)

    for s in range(OWN):
        rows = m.normed[s]
        flat = jnp.dot(rows, w_proj[...], preferred_element_type=F32)
        m.q[s] = (flat[:, :HD] * SCALE).astype(BF16)
        m.k[s] = flat[:, HD : 2 * HD].astype(BF16)
        m.v[s] = flat[:, 2 * HD : 3 * HD].astype(BF16)
        m.gate[s] = jax.nn.sigmoid(flat[:, 3 * HD :] + gate_bias[...])
        flat_t = lax.dot_general(m.w_proj_t[...], rows, NT, preferred_element_type=F32)
        m.q_t[s] = (flat_t[:HD] * SCALE).astype(BF16)
        m.k_t[s] = flat_t[HD : 2 * HD].astype(BF16)
        m.v_t[s] = flat_t[2 * HD : 3 * HD].astype(BF16)

    exchange_arrived(m.in2, recv.in2)
    tiles = m.in1[:, PART:, :].astype(F32)
    for t in range(3):
        rows = jnp.broadcast_to(tiles[:, :, t : t + 1], (COLS, 8, C))
        m.mask[:, t * 8 : (t + 1) * 8, :] = rows
    for s in range(OWN):
        values = m.in2[:, s * WIDTH : (s + 1) * WIDTH, :].astype(F32).reshape(N, C)
        row = at.row0 + s
        own_mask = m.mask[lax.div(row, WIDTH), pl.ds(lax.rem(row, WIDTH), 1), :]
        m.row_mask[s] = own_mask
        pair_mask = m.mask[...].reshape(N, C) * own_mask
        d_out = jnp.where(pair_mask > 0, values, 0.0).astype(BF16)
        d_gated = lax.dot_general(d_out, w_out[...], NT, preferred_element_type=F32)
        gates = m.gate[s]
        d_attn = d_gated * gates
        m.d[s] = d_attn.astype(BF16)
        m.d_t[s] = d_attn.T.astype(BF16)
        m.dgate[s] = d_attn * (1.0 - gates)

    def products(h, carry):
        row = lax.div(lax.broadcasted_iota(jnp.int32, (C, N), 0), DH)
        by_row = (row == h).astype(F32).astype(BF16)
        for s in range(OWN):
            m.scores[h, s] = jnp.dot(m.k[s], m.q_t[s] * by_row, preferred_element_type=F32)
            m.d_prob[h, s] = jnp.dot(m.v[s], m.d_t[s] * by_row, preferred_element_type=F32)
        return carry

    lax.fori_loop(0, H, products, 0)

    def own_bias_arrived(hh):
        for a in range(4):
            for n in (1, 2, 3):
                arrived(bias_block(hh, a, n), recv.far.at[hh, a, n - 1])
        whole = m.bias.at[e * 2 + hh]
        remote(whole, whole, send.partner.at[hh], recv.partner.at[hh], at.partner()).start()

    def other_bias_arrived(hh):
        arrived(m.bias.at[(1 - e) * 2 + hh], recv.partner.at[hh])

    def attend(h):
        here = pl.ds(pl.multiple_of(h * DH, DH), DH)
        lane = lax.div(lax.broadcasted_iota(jnp.int32, (1, C), 1), DH)
        by_lane = (lane == h).astype(F32).astype(BF16)
        dk, dv = [None] * OWN, [None] * OWN
        for n in range(3):
            lanes = slice(n * C, (n + 1) * C)
            d_bias = None
            for s in range(OWN):
                scores = m.scores[h, s, :, lanes] + m.bias[h, :, :, lanes].reshape(N, C)
                exponent = jnp.exp(scores - jnp.max(scores, axis=0, keepdims=True))
                weights = exponent * (1.0 / jnp.sum(exponent, axis=0, keepdims=True))
                weights_b = weights.astype(BF16)
                m.att_t[s, here, lanes] = jnp.dot(
                    m.v_t[s, here, :], weights_b, preferred_element_type=F32
                )
                d_prob = m.d_prob[h, s, :, lanes]
                d_score = weights * (d_prob - jnp.sum(weights * d_prob, axis=0, keepdims=True))
                d_score_b = d_score.astype(BF16)
                d_bias = d_score if d_bias is None else d_bias + d_score
                m.dq_t[s, here, lanes] = jnp.dot(
                    m.k_t[s, here, :], d_score_b, preferred_element_type=F32
                )
                dv_part = jnp.dot(weights_b, m.d[s, lanes, :] * by_lane, preferred_element_type=F32)
                dk_part = jnp.dot(d_score_b, m.q[s, lanes, :] * by_lane, preferred_element_type=F32)
                dv[s] = dv_part if dv[s] is None else dv[s] + dv_part
                dk[s] = dk_part if dk[s] is None else dk[s] + dk_part
            m.d_bias[h, :, :, lanes] = d_bias.reshape(COLS, WIDTH, C)
        for s in range(OWN):
            m.dk[s] += dk[s]
            m.dv[s] += dv[s]

    def to_other(hh):
        head = (1 - e) * 2 + hh
        remote(m.d_bias.at[head], m.d_other.at[hh], send.back.at[hh], recv.back.at[hh], at.partner()).start()

    def scatter_far(hh):
        head = e * 2 + hh
        arrived(m.d_other.at[hh], recv.back.at[hh])
        for n in (1, 2, 3, 0):
            for f in range(4):
                column = at.col(f, at.g + n)
                both = m.d_bias[head, column] + m.d_other[hh, column]
                if n == 0:
                    m.d_near[hh, f] = both
                else:
                    m.stage_far[f] = both
            if n > 0:
                m.d_far[hh, n - 1] = m.stage_far[...].reshape(4 * WIDTH, N).astype(BF16)
                remote(
                    m.d_far.at[hh, n - 1],
                    m.d_far_in.at[hh, n - 1],
                    send.d_far.at[hh, n - 1],
                    recv.d_far.at[hh, n - 1],
                    at.gpeer(n),
                ).start()

    def scatter_near(hh):
        for n in range(3):
            arrived(m.d_far_in.at[hh, n], recv.d_far.at[hh, n])
        far = (m.d_far_in[hh, 0].astype(F32) + m.d_far_in[hh, 1].astype(F32)) + m.d_far_in[hh, 2].astype(F32)
        m.d_near[hh] += far.reshape(4, WIDTH, N)
        for n in (1, 2, 3):
            remote(
                m.d_near.at[hh, lax.rem(at.f + n, 4)],
                m.d_near_in.at[hh, n - 1],
                send.d_near.at[hh, n - 1],
                recv.d_near.at[hh, n - 1],
                at.fpeer(n),
            ).start()

    def plane_sum(hh):
        for n in range(3):
            arrived(m.d_near_in.at[hh, n], recv.d_near.at[hh, n])
        return (m.d_near[hh, at.f] + m.d_near_in[hh, 0]) + (m.d_near_in[hh, 1] + m.d_near_in[hh, 2])

    def finish_row(s):
        attended = m.att_t[s].T
        gated = (m.gate[s] * attended).astype(BF16)
        pair_mask = m.mask[...].reshape(N, C) * m.row_mask[s]
        update = jnp.dot(gated, w_out[...], preferred_element_type=F32) * pair_mask
        d_proj = jnp.concatenate(
            [m.dq_t[s].T * SCALE, m.dk[s], m.dv[s], m.dgate[s] * attended], axis=1
        ).astype(BF16)
        d_normed = lax.dot_general(d_proj, w_proj[...], NT, preferred_element_type=F32)
        result = norm_backward(d_normed * gain[...], m.unit[s], m.rstd[s])
        m.out[:, s] = jnp.concatenate(
            [update.reshape(COLS, WIDTH, C), result.reshape(COLS, WIDTH, C)], axis=1
        ).astype(BF16)
        normed_t = m.normed[s].astype(F32).T.astype(BF16)
        m.proj[...] += jnp.dot(normed_t, d_proj, preferred_element_type=F32)

    def back(n):
        rows = pl.ds(0, 2) if n == 0 else pl.ds(2, 1)
        exchange_start(
            at, m.out.at[:, rows], land.at[at.c, rows], send.out.at[n], recv.out.at[n]
        )

    own_bias_arrived(0)
    attend(e * 2)
    own_bias_arrived(1)
    other_bias_arrived(0)
    attend(2 - e * 2)
    to_other(0)
    other_bias_arrived(1)
    attend(3 - e * 2)
    to_other(1)
    scatter_far(0)
    attend(e * 2 + 1)
    scatter_far(1)
    for s in range(OWN):
        finish_row(s)

    def piece(ref, c):
        rows = pl.ds(pl.multiple_of(lax.div(c, 2) * 16, 16), 16)
        return ref.at[rows, pl.ds(pl.multiple_of(lax.rem(c, 2) * 2 * HD, 2 * HD), 2 * HD)]

    m.proj_b[...] = m.proj[...].astype(BF16)

    def scatter_proj(n, carry):
        t = lax.rem(at.c + n, COLS)
        remote(piece(m.proj_b, t), m.r5.at[n], send.p1.at[n], recv.p1.at[n], at.plane(n)).start()
        return carry

    lax.fori_loop(1, COLS, scatter_proj, 0)
    scatter_near(0)
    back(0)
    scatter_near(1)

    def proj_arrived(n, total):
        arrived(m.r5.at[n], recv.p1.at[n])
        return total + m.r5[n].astype(F32)

    m.v5[...] = lax.fori_loop(1, COLS, proj_arrived, piece(m.proj, at.c)[...])

    def proj_to_homes(z, carry):
        slot = e * 4 + at.zz
        send_or_copy(at.is_home(z), m.v5, m.r6.at[slot], send.p2.at[z], recv.p2.at[slot], at.home(z))
        return carry

    lax.fori_loop(0, ROWS, proj_to_homes, 0)

    back(1)
    halves = [plane_sum(0), plane_sum(1)]
    blank = jnp.zeros((WIDTH, SLOT - TALL), F32)
    for z in range(ROWS):
        mine = slice(z * TALL, (z + 1) * TALL)
        m.zout[z] = jnp.concatenate([halves[0][:, mine], blank, halves[1][:, mine], blank], axis=1)

    def to_homes(z, carry):
        send_or_copy(
            at.is_home(z),
            m.zout.at[z],
            m.hin.at[e, at.zz],
            send.dz.at[z],
            recv.dz.at[e * 4 + at.zz],
            at.home(z),
        )
        return carry

    lax.fori_loop(0, ROWS, to_homes, 0)


    def share_arrived(n, total):
        arrived(m.r6.at[n], recv.p2.at[n])
        return total + m.r6[n]

    m.v6[...] = lax.fori_loop(0, 8, share_arrived, jnp.zeros((16, 2 * HD), F32)).astype(BF16)
    own_piece = piece(proj_out, at.c)
    pltpu.make_async_copy(m.v6, own_piece, recv.p3.at[0]).start()

    def spread(n, carry):
        remote(m.v6, own_piece, send.p3.at[n], recv.p3.at[n], at.plane(n)).start()
        return carry

    lax.fori_loop(1, COLS, spread, 0)

    for core in range(2):
        for zz in range(4):
            arrived(m.hin.at[core, zz], recv.dz.at[core * 4 + zz])
        lanes = slice(core * PAIR, (core + 1) * PAIR)
        h_sum[:, lanes] = (m.hin[core, 0] + m.hin[core, 1]) + (m.hin[core, 2] + m.hin[core, 3])
    exchange_arrived(land.at[:, pl.ds(0, 2)], recv.out.at[0])
    exchange_arrived(land.at[:, pl.ds(2, 1)], recv.out.at[1])

    def out_arrived(n, carry):
        arrived(piece(proj_out, lax.rem(at.c - n + COLS, COLS)), recv.p3.at[n])
        return carry

    lax.fori_loop(0, COLS, out_arrived, 0)

    arrived(unit_out, recv.norm.at[0])
    arrived(rstd_out, recv.norm.at[1])

    def column_sent(n, carry):
        arrived(m.v6, send.p1.at[n])
        arrived(m.v6, send.p3.at[n])
        return carry

    lax.fori_loop(1, COLS, column_sent, 0)

    def column_group_sent(n, carry):
        @pl.when(jnp.logical_not(at.is_worker(lax.div(n, 4), lax.rem(n, 4))))
        def _():
            arrived(m.zpack.at[0], send.z.at[n])

        @pl.when(jnp.logical_not(at.is_home(n)))
        def _():
            arrived(m.zout.at[0], send.dz.at[n])
            arrived(m.v5, send.p2.at[n])

        return carry

    lax.fori_loop(0, 8, column_group_sent, 0)
    for hh in range(2):
        for n in range(3):
            arrived(m.bias.at[0, 0], send.near.at[hh, n])
            for a in range(4):
                arrived(m.bias.at[0, 0], send.far.at[hh, a, n])
            arrived(m.d_far.at[0, 0], send.d_far.at[hh, n])
            arrived(m.d_near.at[0, 0], send.d_near.at[hh, n])
        arrived(m.bias.at[0], send.partner.at[hh])
        arrived(m.d_bias.at[0], send.back.at[hh])
    exchange_sent(at, m.m1, send.in1)
    exchange_sent(at, m.m2, send.in2)
    exchange_sent(at, m.out.at[:, pl.ds(0, 2)], send.out.at[0])
    exchange_sent(at, m.out.at[:, pl.ds(2, 1)], send.out.at[1])


STEPS = 2


def finish_kernel(
    land, proj_in, h_sum, unit, rstd, gain, w_bias_t, update, pair_grad, proj_out, w_rep, split, share
):
    tall = TALL // STEPS
    step = pl.program_id(0)

    @pl.when(step == 0)
    def _():
        proj_out[...] = proj_in[...].astype(F32)
        w_rep[...] = repeat_heads(w_bias_t)
        total = h_sum[...]
        for n in range(3):
            term = total.astype(BF16).astype(F32)
            split[n * WIDTH : (n + 1) * WIDTH, :] = term
            total = total - term

    landed = land[...].astype(F32)
    update[...] = landed[:, :, :WIDTH, :].reshape(tall, WIDTH, C).astype(BF16)
    share[...] = landed[:, :, WIDTH:, :].reshape(tall, WIDTH, C)
    terms = split[...].astype(BF16)
    for i in range(tall):
        parts = lax.dot_general(
            terms, only_row(w_rep[...], step * tall + i), NT, preferred_element_type=F32
        )
        grad = (parts[2 * WIDTH :] + parts[WIDTH : 2 * WIDTH]) + parts[:WIDTH]
        result = norm_backward(grad * gain[...], unit[i], rstd[i])
        pair_grad[i] = (share[i] + result).astype(BF16)


def vmem(count):
    return [pl.BlockSpec(memory_space=pltpu.VMEM)] * count


def shards(
    pair_act, cotangent, ln_gain, ln_shift, w_proj, gate_bias, w_bias, w_out, residue_mask, valid_length
):
    any_space = pl.BlockSpec(memory_space=pl.ANY)
    gain = ln_gain.reshape(1, C)
    sems = [pltpu.SemaphoreType.DMA(shape) for shape in MAIN_SEMS.values()]
    landing = jax.ShapeDtypeStruct((COLS, OWN, 2 * WIDTH, C), BF16)
    block = jax.ShapeDtypeStruct(pair_act.shape, F32)
    proj_shape = jax.ShapeDtypeStruct((C, 4 * HD), F32)
    land, proj, h_sum, unit, rstd = pl.pallas_call(
        main_kernel,
        out_shape=[
            landing,
            jax.ShapeDtypeStruct((C, 4 * HD), BF16),
            jax.ShapeDtypeStruct((WIDTH, H * SLOT), F32),
            block,
            block,
        ],
        in_specs=[pl.BlockSpec(memory_space=pltpu.SMEM)] + [any_space] * (MAIN_IN - 1),
        out_specs=[any_space] * 2 + vmem(1) + [any_space] * 2,
        scratch_shapes=[pltpu.VMEM(shape, dtype) for shape, dtype in MAIN_SCRATCH.values()] + sems + sems,
        compiler_params=pltpu.CompilerParams(
            collective_id=0, has_side_effects=True, vmem_limit_bytes=VMEM_LIMIT
        ),
        name="main",
    )(
        valid_length,
        pair_act,
        cotangent,
        residue_mask.reshape(1, WIDTH),
        gain,
        ln_shift.reshape(1, C),
        w_proj,
        gate_bias.reshape(1, HD),
        w_bias.T,
        w_out,
    )
    result = jax.ShapeDtypeStruct(pair_act.shape, BF16)
    tall = TALL // STEPS
    rows = pl.BlockSpec((tall, WIDTH, C), lambda n: (n, 0, 0))
    landed = pl.BlockSpec((COLS // STEPS, OWN, 2 * WIDTH, C), lambda n: (n, 0, 0, 0))

    def whole(*shape):
        return pl.BlockSpec(shape, lambda n: (0,) * len(shape))

    return pl.pallas_call(
        finish_kernel,
        out_shape=[result, result, proj_shape],
        grid=(STEPS,),
        in_specs=[
            landed,
            whole(C, 4 * HD),
            whole(WIDTH, H * SLOT),
            rows,
            rows,
            whole(1, C),
            whole(H, C),
        ],
        out_specs=[rows, rows, whole(C, 4 * HD)],
        scratch_shapes=[
            pltpu.VMEM((C, H * SLOT), BF16),
            pltpu.VMEM((3 * WIDTH, H * SLOT), F32),
            pltpu.VMEM((tall, WIDTH, C), F32),
        ],
        compiler_params=pltpu.CompilerParams(vmem_limit_bytes=VMEM_LIMIT),
        name="finish",
    )(land, proj, h_sum, unit, rstd, gain, w_bias.T)


def solution(mesh):
    return jax.shard_map(
        shards,
        mesh=mesh,
        in_specs=(
            P(("complex", "row"), "col", None),
            P(("complex", "row"), "col", None),
            P(),
            P(),
            P(),
            P(),
            P(),
            P(),
            P(("complex", "col")),
            P("complex"),
        ),
        out_specs=(
            P(("complex", "row"), "col", None),
            P(("complex", "row"), "col", None),
            P("complex", None),
        ),
        check_vma=False,
    )
```

```python
import jax
import jax.numpy as jnp
from jax import lax
from jax.experimental import pallas as pl
from jax.experimental.pallas import tpu as pltpu
from jax.sharding import PartitionSpec as P

MESH = pl.DeviceIdType.MESH
F32 = jnp.float32
BF16 = jnp.bfloat16
N = 384
C = 128
H = 4
DH = 32
HD = H * DH
COLS = 16
ROWS = 8
WIDTH = N // COLS
TALL = N // ROWS
OWN = 3
PART = OWN * WIDTH
PADDED = 80
SLOT = 64
PAIR = 2 * SLOT
SCALE = DH ** (-0.5)
VMEM_LIMIT = 60 * 1024 * 1024
NT = (((1,), (1,)), ((), ()))


class Place:
    def __init__(self):
        self.e = lax.axis_index("complex")
        self.z = lax.axis_index("row")
        self.c = lax.axis_index("col")
        self.part = lax.rem(self.z, 2)
        self.zz = lax.div(self.z, 2)
        self.stays = self.part == self.e
        self.y = lax.div(self.c, 4)
        self.x = lax.rem(self.c, 4)
        self.f = self.x * (1 - self.e) + self.y * self.e
        self.g = self.y * (1 - self.e) + self.x * self.e
        self.row0 = (self.zz * 2 + self.e) * TALL + self.c * OWN

    def swapped(self, c):
        return (self.part, self.zz * 2 + self.e, c)

    def col(self, f, g):
        return lax.rem(f, 4) * (1 + 3 * self.e) + lax.rem(g, 4) * (4 - 3 * self.e)

    def fpeer(self, n):
        return (self.e, self.z, self.col(self.f + n, self.g))

    def gpeer(self, n):
        return (self.e, self.z, self.col(self.f, self.g + n))

    def plane(self, n):
        return (self.e, self.z, lax.rem(self.c + n, COLS))

    def partner(self):
        return (1 - self.e, self.z, self.c)

    def worker(self, core, zz):
        return (core, zz * 2 + self.e, self.c)

    def home(self, z):
        return (self.part, z, self.c)

    def is_worker(self, core, zz):
        return jnp.logical_and(self.stays, jnp.logical_and(core == self.e, zz == self.zz))

    def is_home(self, z):
        return jnp.logical_and(self.stays, z == self.z)


def remote(src, dst, send, recv, device):
    return pltpu.make_async_remote_copy(
        src_ref=src, dst_ref=dst, send_sem=send, recv_sem=recv, device_id=device, device_id_type=MESH
    )


def arrived(ref, sem):
    pltpu.make_async_copy(ref, ref, sem).wait()


def send_or_copy(here, src, dst, send, recv, device):
    @pl.when(here)
    def _():
        pltpu.make_async_copy(src, dst, recv).start()

    @pl.when(jnp.logical_not(here))
    def _():
        remote(src, dst, send, recv, device).start()


def unrolled(low, high, body, carry):
    for n in range(low, high):
        carry = body(n, carry)
    return carry


def greet(device):
    pl.semaphore_signal(pltpu.get_barrier_semaphore(), inc=1, device_id=device, device_id_type=MESH)


def greet_all(at):
    def plane(n, carry):
        greet(at.plane(n))
        return carry

    unrolled(1, COLS, plane, 0)

    def worker(n, carry):
        core, zz = lax.div(n, 4), lax.rem(n, 4)

        @pl.when(jnp.logical_not(at.is_worker(core, zz)))
        def _():
            greet(at.worker(core, zz))

        return carry

    unrolled(0, 8, worker, 0)

    def home(n, carry):
        greet(at.home(n * 2 + 1 - at.e))
        return carry

    unrolled(0, 4, home, 0)

    @pl.when(jnp.logical_not(at.stays))
    def _():
        for n in range(COLS):
            greet(at.swapped(n))

    return jnp.where(at.stays, COLS - 1 + 7 + 4, COLS - 1 + 8 + 4 + COLS)


def exchange_start(at, source, slot, send, recv):
    def column(n, carry):
        t = lax.rem(at.c + n, COLS)
        here = jnp.logical_and(n == 0, at.stays)
        send_or_copy(here, source.at[t], slot, send.at[t], recv.at[at.c], at.swapped(t))
        return carry

    unrolled(0, COLS, column, 0)


def exchange_arrived(landing, recv):
    def column(n, carry):
        arrived(landing.at[n], recv.at[n])
        return carry

    unrolled(0, COLS, column, 0)


def exchange_sent(at, source, send):
    def column(n, carry):
        t = lax.rem(at.c + n, COLS)

        @pl.when(jnp.logical_or(n > 0, jnp.logical_not(at.stays)))
        def _():
            arrived(source.at[t], send.at[t])

        return carry

    unrolled(0, COLS, column, 0)


def repeat_heads(w_bias_t):
    wide = jnp.concatenate([w_bias_t[...].astype(F32), jnp.zeros((C - H, C), F32)], axis=0).T
    lane = lax.div(lax.broadcasted_iota(jnp.int32, (C, H * SLOT), 1), SLOT)
    total = jnp.zeros((C, H * SLOT), F32)
    for h in range(H):
        total = jnp.where(lane == h, wide[:, h : h + 1], total)
    return total.astype(BF16)


def only_row(repeated, i):
    lane = lax.rem(lax.broadcasted_iota(jnp.int32, (1, H * SLOT), 1), SLOT)
    return repeated * (lane == i).astype(F32).astype(BF16)


def standardize(values):
    centre = values - jnp.mean(values, axis=-1, keepdims=True)
    inverse = lax.rsqrt(jnp.mean(centre * centre, axis=-1, keepdims=True) + 1e-5)
    return centre * inverse, jnp.broadcast_to(inverse, values.shape)


def norm_backward(grad, unit, inverse):
    mean_grad = jnp.mean(grad, axis=-1, keepdims=True)
    mean_cross = jnp.mean(grad * unit, axis=-1, keepdims=True)
    return inverse * (grad - mean_grad - unit * mean_cross)


MAIN_SCRATCH = dict(
    pair=((TALL, WIDTH, C), BF16),
    cot=((TALL, WIDTH, C), BF16),
    residues=((1, WIDTH), jnp.int32),
    gain=((1, C), F32),
    shift=((1, C), F32),
    w_proj=((C, 4 * HD), BF16),
    gate_bias=((1, HD), F32),
    w_bias_t=((H, C), BF16),
    w_out=((HD, C), BF16),
    home_unit=((TALL, WIDTH, C), F32),
    home_rstd=((TALL, WIDTH, C), F32),
    scores=((H, OWN, N, N), F32),
    d_prob=((H, OWN, N, N), F32),
    m1=((COLS, PADDED, C), BF16),
    m2=((COLS, PADDED, C), BF16),
    in1=((COLS, PADDED, C), BF16),
    in2=((COLS, PADDED, C), BF16),
    flags=((WIDTH, C), F32),
    w_proj_t=((3 * HD, C), BF16),
    w_rep=((C, H * SLOT), BF16),
    home_rows=((TALL, WIDTH, C), F32),
    zpack=((2, WIDTH, PAIR), F32),
    zin=((ROWS, WIDTH, PAIR), F32),
    bias=((H, COLS, WIDTH, N), F32),
    d_bias=((H, COLS, WIDTH, N), F32),
    d_other=((2, COLS, WIDTH, N), F32),
    stage_far=((4, WIDTH, N), F32),
    d_far=((2, 3, 4 * WIDTH, N), BF16),
    d_far_in=((2, 3, 4 * WIDTH, N), BF16),
    d_near=((2, 4, WIDTH, N), F32),
    d_near_in=((2, 3, WIDTH, N), F32),
    zout=((ROWS, WIDTH, PAIR), F32),
    hin=((2, 4, WIDTH, PAIR), F32),
    mask=((COLS, WIDTH, C), F32),
    row_mask=((OWN, 1, C), F32),
    normed=((OWN, N, C), BF16),
    unit=((OWN, N, C), F32),
    rstd=((OWN, N, C), F32),
    q=((OWN, N, C), BF16),
    k=((OWN, N, C), BF16),
    v=((OWN, N, C), BF16),
    d=((OWN, N, C), BF16),
    q_t=((OWN, C, N), BF16),
    k_t=((OWN, C, N), BF16),
    v_t=((OWN, C, N), BF16),
    d_t=((OWN, C, N), BF16),
    gate=((OWN, N, C), F32),
    dgate=((OWN, N, C), F32),
    att_t=((OWN, HD, N), F32),

    dq_t=((OWN, HD, N), F32),
    dk=((OWN, N, HD), F32),
    dv=((OWN, N, HD), F32),
    proj=((C, 4 * HD), F32),
    proj_b=((C, 4 * HD), BF16),
    r5=((COLS, 16, 2 * HD), BF16),
    v5=((16, 2 * HD), F32),
    r6=((8, 16, 2 * HD), F32),
    v6=((16, 2 * HD), BF16),
    out=((COLS, OWN, 2 * WIDTH, C), BF16),
)
MAIN_SEMS = dict(
    operand=(9,),
    norm=(2,),
    in1=(COLS,),
    in2=(COLS,),
    z=(8,),
    near=(2, 3),
    far=(2, 4, 3),
    partner=(2,),
    back=(2,),
    d_far=(2, 3),
    d_near=(2, 3),
    dz=(8,),
    p1=(COLS,),
    p2=(8,),
    p3=(COLS,),
    out=(2, COLS),
)
MAIN_IN = 10
MAIN_OUT = 5


class Names:
    pass


def main_kernel(*refs):
    length, operands = refs[0], refs[1:MAIN_IN]
    (land, proj_out, h_sum, unit_out, rstd_out) = refs[MAIN_IN : MAIN_IN + MAIN_OUT]
    rest = refs[MAIN_IN + MAIN_OUT :]
    m, send, recv = Names(), Names(), Names()
    for name, ref in zip(MAIN_SCRATCH, rest):
        setattr(m, name, ref)
    rest = rest[len(MAIN_SCRATCH) :]
    for name, ref in zip(MAIN_SEMS, rest):
        setattr(send, name, ref)
    for name, ref in zip(MAIN_SEMS, rest[len(MAIN_SEMS) :]):
        setattr(recv, name, ref)
    held = (m.pair, m.cot, m.residues, m.gain, m.shift, m.w_proj, m.gate_bias, m.w_bias_t, m.w_out)
    pair, cot, residues, gain, shift, w_proj, gate_bias, w_bias_t, w_out = held
    for n in range(MAIN_IN - 1):
        pltpu.make_async_copy(operands[n], held[n], recv.operand.at[n]).start()
    at = Place()
    e = at.e
    count = greet_all(at)
    for n in range(MAIN_IN - 1):
        arrived(held[n], recv.operand.at[n])

    sublane = lax.broadcasted_iota(jnp.int32, (WIDTH, WIDTH), 0)
    lane = lax.broadcasted_iota(jnp.int32, (WIDTH, WIDTH), 1)
    valid = jnp.where(lane + at.c * WIDTH < length[0], residues[...], 0).astype(F32)
    valid = jnp.sum(jnp.where(lane == sublane, valid, 0.0), axis=1, keepdims=True)
    m.flags[...] = jnp.broadcast_to(valid, (WIDTH, C))
    m.w_rep[...] = repeat_heads(w_bias_t)
    unit, inverse = standardize(pair[...].astype(F32).reshape(TALL * WIDTH, C))
    m.home_unit[...] = unit.reshape(TALL, WIDTH, C)
    m.home_rstd[...] = inverse.reshape(TALL, WIDTH, C)
    m.home_rows[...] = (unit * gain[...] + shift[...]).reshape(TALL, WIDTH, C)

    def home_bias(n, total):
        for i in range(8):
            rows = m.home_rows[n * 8 + i].astype(BF16)
            total = total + jnp.dot(rows, only_row(m.w_rep[...], n * 8 + i), preferred_element_type=F32)
        return total

    packed = lax.fori_loop(0, TALL // 8, home_bias, jnp.zeros((WIDTH, H * SLOT), F32))
    negative = (m.flags[...] - 1.0) * 1e9
    m.zpack[0] = packed[:, :PAIR] + negative
    m.zpack[1] = packed[:, PAIR:] + negative

    pl.semaphore_wait(pltpu.get_barrier_semaphore(), count)

    def to_workers(n, carry):
        core, zz = lax.div(n, 4), lax.rem(n, 4)
        send_or_copy(
            at.is_worker(core, zz),
            m.zpack.at[core],
            m.zin.at[at.z],
            send.z.at[n],
            recv.z.at[at.z],
            at.worker(core, zz),
        )
        return carry

    unrolled(0, 8, to_workers, 0)
    lane = lax.broadcasted_iota(jnp.int32, (8, C), 1)
    packed_flags = jnp.where(
        lane == 0, m.flags[0:8, :], jnp.where(lane == 1, m.flags[8:16, :], m.flags[16:24, :])
    )
    pad = jnp.zeros((COLS, PADDED - PART, C), F32)
    m.m1[...] = jnp.concatenate(
        [
            pair[...].astype(F32).reshape(COLS, PART, C),
            jnp.broadcast_to(packed_flags[None], (COLS, PADDED - PART, C)),
        ],
        axis=1,
    ).astype(BF16)
    m.m2[...] = jnp.concatenate([cot[...].astype(F32).reshape(COLS, PART, C), pad], axis=1).astype(BF16)

    exchange_start(at, m.m1, m.in1.at[at.c], send.in1, recv.in1)
    exchange_start(at, m.m2, m.in2.at[at.c], send.in2, recv.in2)
    pltpu.make_async_copy(m.home_unit, unit_out, recv.norm.at[0]).start()
    pltpu.make_async_copy(m.home_rstd, rstd_out, recv.norm.at[1]).start()

    m.w_proj_t[...] = w_proj[:, : 3 * HD].astype(F32).T.astype(BF16)
    m.dk[...] = jnp.zeros_like(m.dk)
    m.dv[...] = jnp.zeros_like(m.dv)
    m.proj[...] = jnp.zeros_like(m.proj)
    def bias_block(hh, a, b):
        return m.bias.at[e * 2 + hh, at.col(at.f - a + 4, at.g - b + 4)]

    def to_far(hh, a):
        block = bias_block(hh, a, 0)
        for n in (1, 2, 3):
            remote(block, block, send.far.at[hh, a, n - 1], recv.far.at[hh, a, n - 1], at.gpeer(n)).start()

    def forward(hh):
        for n in (1, 2, 3):
            arrived(bias_block(hh, n, 0), recv.near.at[hh, n - 1])
            to_far(hh, n)

    for z in range(ROWS):
        arrived(m.zin.at[z], recv.z.at[z])
    for hh in range(2):
        head = e * 2 + hh
        m.bias[head, at.c] = jnp.concatenate(
            [m.zin[z][:, hh * SLOT : hh * SLOT + TALL] for z in range(ROWS)], axis=1
        )
        mine = m.bias.at[head, at.c]
        for n in (1, 2, 3):
            remote(mine, mine, send.near.at[hh, n - 1], recv.near.at[hh, n - 1], at.fpeer(n)).start()
        to_far(hh, 0)

    forward(0)
    forward(1)
    exchange_arrived(m.in1, recv.in1)

    for s in range(OWN):
        values = m.in1[:, s * WIDTH : (s + 1) * WIDTH, :].astype(F32).reshape(N, C)
        unit, inverse = standardize(values)
        m.unit[s] = unit
        m.rstd[s] = inverse
        m.normed[s] = (unit * gain[...] + shift[...]).astype(BF16)

    for s in range(OWN):
        rows = m.normed[s]
        flat = jnp.dot(rows, w_proj[...], preferred_element_type=F32)
        m.q[s] = (flat[:, :HD] * SCALE).astype(BF16)
        m.k[s] = flat[:, HD : 2 * HD].astype(BF16)
        m.v[s] = flat[:, 2 * HD : 3 * HD].astype(BF16)
        m.gate[s] = jax.nn.sigmoid(flat[:, 3 * HD :] + gate_bias[...])
        flat_t = lax.dot_general(m.w_proj_t[...], rows, NT, preferred_element_type=F32)
        m.q_t[s] = (flat_t[:HD] * SCALE).astype(BF16)
        m.k_t[s] = flat_t[HD : 2 * HD].astype(BF16)
        m.v_t[s] = flat_t[2 * HD : 3 * HD].astype(BF16)

    exchange_arrived(m.in2, recv.in2)
    tiles = m.in1[:, PART:, :].astype(F32)
    for t in range(3):
        rows = jnp.broadcast_to(tiles[:, :, t : t + 1], (COLS, 8, C))
        m.mask[:, t * 8 : (t + 1) * 8, :] = rows
    for s in range(OWN):
        values = m.in2[:, s * WIDTH : (s + 1) * WIDTH, :].astype(F32).reshape(N, C)
        row = at.row0 + s
        own_mask = m.mask[lax.div(row, WIDTH), pl.ds(lax.rem(row, WIDTH), 1), :]
        m.row_mask[s] = own_mask
        pair_mask = m.mask[...].reshape(N, C) * own_mask
        d_out = jnp.where(pair_mask > 0, values, 0.0).astype(BF16)
        d_gated = lax.dot_general(d_out, w_out[...], NT, preferred_element_type=F32)
        gates = m.gate[s]
        d_attn = d_gated * gates
        m.d[s] = d_attn.astype(BF16)
        m.d_t[s] = d_attn.T.astype(BF16)
        m.dgate[s] = d_attn * (1.0 - gates)

    def products(h, carry):
        row = lax.div(lax.broadcasted_iota(jnp.int32, (C, N), 0), DH)
        by_row = (row == h).astype(F32).astype(BF16)
        for s in range(OWN):
            m.scores[h, s] = jnp.dot(m.k[s], m.q_t[s] * by_row, preferred_element_type=F32)
            m.d_prob[h, s] = jnp.dot(m.v[s], m.d_t[s] * by_row, preferred_element_type=F32)
        return carry

    lax.fori_loop(0, H, products, 0)

    def own_bias_arrived(hh):
        for a in range(4):
            for n in (1, 2, 3):
                arrived(bias_block(hh, a, n), recv.far.at[hh, a, n - 1])
        whole = m.bias.at[e * 2 + hh]
        remote(whole, whole, send.partner.at[hh], recv.partner.at[hh], at.partner()).start()

    def other_bias_arrived(hh):
        arrived(m.bias.at[(1 - e) * 2 + hh], recv.partner.at[hh])

    def attend(h):
        here = pl.ds(pl.multiple_of(h * DH, DH), DH)
        lane = lax.div(lax.broadcasted_iota(jnp.int32, (1, C), 1), DH)
        by_lane = (lane == h).astype(F32).astype(BF16)
        dk, dv = [None] * OWN, [None] * OWN
        for n in range(3):
            lanes = slice(n * C, (n + 1) * C)
            d_bias = None
            for s in range(OWN):
                scores = m.scores[h, s, :, lanes] + m.bias[h, :, :, lanes].reshape(N, C)
                exponent = jnp.exp(scores - jnp.max(scores, axis=0, keepdims=True))
                weights = exponent * (1.0 / jnp.sum(exponent, axis=0, keepdims=True))
                weights_b = weights.astype(BF16)
                m.att_t[s, here, lanes] = jnp.dot(
                    m.v_t[s, here, :], weights_b, preferred_element_type=F32
                )
                d_prob = m.d_prob[h, s, :, lanes]
                d_score = weights * (d_prob - jnp.sum(weights * d_prob, axis=0, keepdims=True))
                d_score_b = d_score.astype(BF16)
                d_bias = d_score if d_bias is None else d_bias + d_score
                m.dq_t[s, here, lanes] = jnp.dot(
                    m.k_t[s, here, :], d_score_b, preferred_element_type=F32
                )
                dv_part = jnp.dot(weights_b, m.d[s, lanes, :] * by_lane, preferred_element_type=F32)
                dk_part = jnp.dot(d_score_b, m.q[s, lanes, :] * by_lane, preferred_element_type=F32)
                dv[s] = dv_part if dv[s] is None else dv[s] + dv_part
                dk[s] = dk_part if dk[s] is None else dk[s] + dk_part
            m.d_bias[h, :, :, lanes] = d_bias.reshape(COLS, WIDTH, C)
        for s in range(OWN):
            m.dk[s] += dk[s]
            m.dv[s] += dv[s]

    def to_other(hh):
        head = (1 - e) * 2 + hh
        remote(m.d_bias.at[head], m.d_other.at[hh], send.back.at[hh], recv.back.at[hh], at.partner()).start()

    def scatter_far(hh):
        head = e * 2 + hh
        arrived(m.d_other.at[hh], recv.back.at[hh])
        for n in (1, 2, 3, 0):
            for f in range(4):
                column = at.col(f, at.g + n)
                both = m.d_bias[head, column] + m.d_other[hh, column]
                if n == 0:
                    m.d_near[hh, f] = both
                else:
                    m.stage_far[f] = both
            if n > 0:
                m.d_far[hh, n - 1] = m.stage_far[...].reshape(4 * WIDTH, N).astype(BF16)
                remote(
                    m.d_far.at[hh, n - 1],
                    m.d_far_in.at[hh, n - 1],
                    send.d_far.at[hh, n - 1],
                    recv.d_far.at[hh, n - 1],
                    at.gpeer(n),
                ).start()

    def scatter_near(hh):
        for n in range(3):
            arrived(m.d_far_in.at[hh, n], recv.d_far.at[hh, n])
        far = (m.d_far_in[hh, 0].astype(F32) + m.d_far_in[hh, 1].astype(F32)) + m.d_far_in[hh, 2].astype(F32)
        m.d_near[hh] += far.reshape(4, WIDTH, N)
        for n in (1, 2, 3):
            remote(
                m.d_near.at[hh, lax.rem(at.f + n, 4)],
                m.d_near_in.at[hh, n - 1],
                send.d_near.at[hh, n - 1],
                recv.d_near.at[hh, n - 1],
                at.fpeer(n),
            ).start()

    def plane_sum(hh):
        for n in range(3):
            arrived(m.d_near_in.at[hh, n], recv.d_near.at[hh, n])
        return (m.d_near[hh, at.f] + m.d_near_in[hh, 0]) + (m.d_near_in[hh, 1] + m.d_near_in[hh, 2])

    def finish_row(s):
        attended = m.att_t[s].T
        gated = (m.gate[s] * attended).astype(BF16)
        pair_mask = m.mask[...].reshape(N, C) * m.row_mask[s]
        update = jnp.dot(gated, w_out[...], preferred_element_type=F32) * pair_mask
        d_proj = jnp.concatenate(
            [m.dq_t[s].T * SCALE, m.dk[s], m.dv[s], m.dgate[s] * attended], axis=1
        ).astype(BF16)
        d_normed = lax.dot_general(d_proj, w_proj[...], NT, preferred_element_type=F32)
        result = norm_backward(d_normed * gain[...], m.unit[s], m.rstd[s])
        m.out[:, s] = jnp.concatenate(
            [update.reshape(COLS, WIDTH, C), result.reshape(COLS, WIDTH, C)], axis=1
        ).astype(BF16)
        normed_t = m.normed[s].astype(F32).T.astype(BF16)
        m.proj[...] += jnp.dot(normed_t, d_proj, preferred_element_type=F32)

    def back(n):
        rows = pl.ds(0, 2) if n == 0 else pl.ds(2, 1)
        exchange_start(
            at, m.out.at[:, rows], land.at[at.c, rows], send.out.at[n], recv.out.at[n]
        )

    own_bias_arrived(0)
    attend(e * 2)
    own_bias_arrived(1)
    other_bias_arrived(0)
    attend(2 - e * 2)
    to_other(0)
    other_bias_arrived(1)
    attend(3 - e * 2)
    to_other(1)
    scatter_far(0)
    attend(e * 2 + 1)
    scatter_far(1)
    for s in range(OWN):
        finish_row(s)

    def piece(ref, c):
        rows = pl.ds(pl.multiple_of(lax.div(c, 2) * 16, 16), 16)
        return ref.at[rows, pl.ds(pl.multiple_of(lax.rem(c, 2) * 2 * HD, 2 * HD), 2 * HD)]

    m.proj_b[...] = m.proj[...].astype(BF16)

    def scatter_proj(n, carry):
        t = lax.rem(at.c + n, COLS)
        remote(piece(m.proj_b, t), m.r5.at[n], send.p1.at[n], recv.p1.at[n], at.plane(n)).start()
        return carry

    unrolled(1, COLS, scatter_proj, 0)
    scatter_near(0)
    back(0)
    scatter_near(1)

    def proj_arrived(n, total):
        arrived(m.r5.at[n], recv.p1.at[n])
        return total + m.r5[n].astype(F32)

    m.v5[...] = unrolled(1, COLS, proj_arrived, piece(m.proj, at.c)[...])

    def proj_to_homes(z, carry):
        slot = e * 4 + at.zz
        send_or_copy(at.is_home(z), m.v5, m.r6.at[slot], send.p2.at[z], recv.p2.at[slot], at.home(z))
        return carry

    unrolled(0, ROWS, proj_to_homes, 0)

    back(1)
    halves = [plane_sum(0), plane_sum(1)]
    blank = jnp.zeros((WIDTH, SLOT - TALL), F32)
    for z in range(ROWS):
        mine = slice(z * TALL, (z + 1) * TALL)
        m.zout[z] = jnp.concatenate([halves[0][:, mine], blank, halves[1][:, mine], blank], axis=1)

    def to_homes(z, carry):
        send_or_copy(
            at.is_home(z),
            m.zout.at[z],
            m.hin.at[e, at.zz],
            send.dz.at[z],
            recv.dz.at[e * 4 + at.zz],
            at.home(z),
        )
        return carry

    unrolled(0, ROWS, to_homes, 0)


    def share_arrived(n, total):
        arrived(m.r6.at[n], recv.p2.at[n])
        return total + m.r6[n]

    m.v6[...] = unrolled(0, 8, share_arrived, jnp.zeros((16, 2 * HD), F32)).astype(BF16)
    own_piece = piece(proj_out, at.c)
    pltpu.make_async_copy(m.v6, own_piece, recv.p3.at[0]).start()

    def spread(n, carry):
        remote(m.v6, own_piece, send.p3.at[n], recv.p3.at[n], at.plane(n)).start()
        return carry

    unrolled(1, COLS, spread, 0)

    for core in range(2):
        for zz in range(4):
            arrived(m.hin.at[core, zz], recv.dz.at[core * 4 + zz])
        lanes = slice(core * PAIR, (core + 1) * PAIR)
        h_sum[:, lanes] = (m.hin[core, 0] + m.hin[core, 1]) + (m.hin[core, 2] + m.hin[core, 3])
    exchange_arrived(land.at[:, pl.ds(0, 2)], recv.out.at[0])
    exchange_arrived(land.at[:, pl.ds(2, 1)], recv.out.at[1])

    def out_arrived(n, carry):
        arrived(piece(proj_out, lax.rem(at.c - n + COLS, COLS)), recv.p3.at[n])
        return carry

    lax.fori_loop(0, COLS, out_arrived, 0)

    arrived(unit_out, recv.norm.at[0])
    arrived(rstd_out, recv.norm.at[1])

    def column_sent(n, carry):
        arrived(m.v6, send.p1.at[n])
        arrived(m.v6, send.p3.at[n])
        return carry

    lax.fori_loop(1, COLS, column_sent, 0)

    def column_group_sent(n, carry):
        @pl.when(jnp.logical_not(at.is_worker(lax.div(n, 4), lax.rem(n, 4))))
        def _():
            arrived(m.zpack.at[0], send.z.at[n])

        @pl.when(jnp.logical_not(at.is_home(n)))
        def _():
            arrived(m.zout.at[0], send.dz.at[n])
            arrived(m.v5, send.p2.at[n])

        return carry

    lax.fori_loop(0, 8, column_group_sent, 0)
    for hh in range(2):
        for n in range(3):
            arrived(m.bias.at[0, 0], send.near.at[hh, n])
            for a in range(4):
                arrived(m.bias.at[0, 0], send.far.at[hh, a, n])
            arrived(m.d_far.at[0, 0], send.d_far.at[hh, n])
            arrived(m.d_near.at[0, 0], send.d_near.at[hh, n])
        arrived(m.bias.at[0], send.partner.at[hh])
        arrived(m.d_bias.at[0], send.back.at[hh])
    exchange_sent(at, m.m1, send.in1)
    exchange_sent(at, m.m2, send.in2)
    exchange_sent(at, m.out.at[:, pl.ds(0, 2)], send.out.at[0])
    exchange_sent(at, m.out.at[:, pl.ds(2, 1)], send.out.at[1])


STEPS = 2


def finish_kernel(
    land, proj_in, h_sum, unit, rstd, gain, w_bias_t, update, pair_grad, proj_out, w_rep, split, share
):
    tall = TALL // STEPS
    step = pl.program_id(0)

    @pl.when(step == 0)
    def _():
        proj_out[...] = proj_in[...].astype(F32)
        w_rep[...] = repeat_heads(w_bias_t)
        total = h_sum[...]
        for n in range(3):
            term = total.astype(BF16).astype(F32)
            split[n * WIDTH : (n + 1) * WIDTH, :] = term
            total = total - term

    landed = land[...].astype(F32)
    update[...] = landed[:, :, :WIDTH, :].reshape(tall, WIDTH, C).astype(BF16)
    share[...] = landed[:, :, WIDTH:, :].reshape(tall, WIDTH, C)
    terms = split[...].astype(BF16)
    for i in range(tall):
        parts = lax.dot_general(
            terms, only_row(w_rep[...], step * tall + i), NT, preferred_element_type=F32
        )
        grad = (parts[2 * WIDTH :] + parts[WIDTH : 2 * WIDTH]) + parts[:WIDTH]
        result = norm_backward(grad * gain[...], unit[i], rstd[i])
        pair_grad[i] = (share[i] + result).astype(BF16)


def vmem(count):
    return [pl.BlockSpec(memory_space=pltpu.VMEM)] * count


def shards(
    pair_act, cotangent, ln_gain, ln_shift, w_proj, gate_bias, w_bias, w_out, residue_mask, valid_length
):
    any_space = pl.BlockSpec(memory_space=pl.ANY)
    gain = ln_gain.reshape(1, C)
    sems = [pltpu.SemaphoreType.DMA(shape) for shape in MAIN_SEMS.values()]
    landing = jax.ShapeDtypeStruct((COLS, OWN, 2 * WIDTH, C), BF16)
    block = jax.ShapeDtypeStruct(pair_act.shape, F32)
    proj_shape = jax.ShapeDtypeStruct((C, 4 * HD), F32)
    land, proj, h_sum, unit, rstd = pl.pallas_call(
        main_kernel,
        out_shape=[
            landing,
            jax.ShapeDtypeStruct((C, 4 * HD), BF16),
            jax.ShapeDtypeStruct((WIDTH, H * SLOT), F32),
            block,
            block,
        ],
        in_specs=[pl.BlockSpec(memory_space=pltpu.SMEM)] + [any_space] * (MAIN_IN - 1),
        out_specs=[any_space] * 2 + vmem(1) + [any_space] * 2,
        scratch_shapes=[pltpu.VMEM(shape, dtype) for shape, dtype in MAIN_SCRATCH.values()] + sems + sems,
        compiler_params=pltpu.CompilerParams(
            collective_id=0, has_side_effects=True, vmem_limit_bytes=VMEM_LIMIT
        ),
        name="main",
    )(
        valid_length,
        pair_act,
        cotangent,
        residue_mask.reshape(1, WIDTH),
        gain,
        ln_shift.reshape(1, C),
        w_proj,
        gate_bias.reshape(1, HD),
        w_bias.T,
        w_out,
    )
    result = jax.ShapeDtypeStruct(pair_act.shape, BF16)
    tall = TALL // STEPS
    rows = pl.BlockSpec((tall, WIDTH, C), lambda n: (n, 0, 0))
    landed = pl.BlockSpec((COLS // STEPS, OWN, 2 * WIDTH, C), lambda n: (n, 0, 0, 0))

    def whole(*shape):
        return pl.BlockSpec(shape, lambda n: (0,) * len(shape))

    return pl.pallas_call(
        finish_kernel,
        out_shape=[result, result, proj_shape],
        grid=(STEPS,),
        in_specs=[
            landed,
            whole(C, 4 * HD),
            whole(WIDTH, H * SLOT),
            rows,
            rows,
            whole(1, C),
            whole(H, C),
        ],
        out_specs=[rows, rows, whole(C, 4 * HD)],
        scratch_shapes=[
            pltpu.VMEM((C, H * SLOT), BF16),
            pltpu.VMEM((3 * WIDTH, H * SLOT), F32),
            pltpu.VMEM((tall, WIDTH, C), F32),
        ],
        compiler_params=pltpu.CompilerParams(vmem_limit_bytes=VMEM_LIMIT),
        name="finish",
    )(land, proj, h_sum, unit, rstd, gain, w_bias.T)


def solution(mesh):
    return jax.shard_map(
        shards,
        mesh=mesh,
        in_specs=(
            P(("complex", "row"), "col", None),
            P(("complex", "row"), "col", None),
            P(),
            P(),
            P(),
            P(),
            P(),
            P(),
            P(("complex", "col")),
            P("complex"),
        ),
        out_specs=(
            P(("complex", "row"), "col", None),
            P(("complex", "row"), "col", None),
            P("complex", None),
        ),
        check_vma=False,
    )
```

```python
import jax
import jax.numpy as jnp
from jax import lax
from jax.experimental import pallas as pl
from jax.experimental.pallas import tpu as pltpu
from jax.sharding import PartitionSpec as P

MESH = pl.DeviceIdType.MESH
F32 = jnp.float32
BF16 = jnp.bfloat16
N = 384
C = 128
H = 4
DH = 32
HD = H * DH
COLS = 16
ROWS = 8
WIDTH = N // COLS
TALL = N // ROWS
OWN = 3
PART = OWN * WIDTH
PADDED = 80
SLOT = 64
PAIR = 2 * SLOT
SCALE = DH ** (-0.5)
VMEM_LIMIT = 60 * 1024 * 1024
NT = (((1,), (1,)), ((), ()))


class Place:
    def __init__(self):
        self.e = lax.axis_index("complex")
        self.z = lax.axis_index("row")
        self.c = lax.axis_index("col")
        self.part = lax.rem(self.z, 2)
        self.zz = lax.div(self.z, 2)
        self.stays = self.part == self.e
        self.y = lax.div(self.c, 4)
        self.x = lax.rem(self.c, 4)
        self.f = self.x * (1 - self.e) + self.y * self.e
        self.g = self.y * (1 - self.e) + self.x * self.e
        self.row0 = (self.zz * 2 + self.e) * TALL + self.c * OWN

    def swapped(self, c):
        return (self.part, self.zz * 2 + self.e, c)

    def col(self, f, g):
        return lax.rem(f, 4) * (1 + 3 * self.e) + lax.rem(g, 4) * (4 - 3 * self.e)

    def fpeer(self, n):
        return (self.e, self.z, self.col(self.f + n, self.g))

    def gpeer(self, n):
        return (self.e, self.z, self.col(self.f, self.g + n))

    def plane(self, n):
        return (self.e, self.z, lax.rem(self.c + n, COLS))

    def partner(self):
        return (1 - self.e, self.z, self.c)

    def worker(self, core, zz):
        return (core, zz * 2 + self.e, self.c)

    def home(self, z):
        return (self.part, z, self.c)

    def is_worker(self, core, zz):
        return jnp.logical_and(self.stays, jnp.logical_and(core == self.e, zz == self.zz))

    def is_home(self, z):
        return jnp.logical_and(self.stays, z == self.z)


def remote(src, dst, send, recv, device):
    return pltpu.make_async_remote_copy(
        src_ref=src, dst_ref=dst, send_sem=send, recv_sem=recv, device_id=device, device_id_type=MESH
    )


def arrived(ref, sem):
    pltpu.make_async_copy(ref, ref, sem).wait()


def send_or_copy(here, src, dst, send, recv, device):
    @pl.when(here)
    def _():
        pltpu.make_async_copy(src, dst, recv).start()

    @pl.when(jnp.logical_not(here))
    def _():
        remote(src, dst, send, recv, device).start()


def unrolled(low, high, body, carry):
    for n in range(low, high):
        carry = body(n, carry)
    return carry


def greet(device):
    pl.semaphore_signal(pltpu.get_barrier_semaphore(), inc=1, device_id=device, device_id_type=MESH)


def greet_all(at):
    def plane(n, carry):
        greet(at.plane(n))
        return carry

    unrolled(1, COLS, plane, 0)

    def worker(n, carry):
        core, zz = lax.div(n, 4), lax.rem(n, 4)

        @pl.when(jnp.logical_not(at.is_worker(core, zz)))
        def _():
            greet(at.worker(core, zz))

        return carry

    unrolled(0, 8, worker, 0)

    def home(n, carry):
        greet(at.home(n * 2 + 1 - at.e))
        return carry

    unrolled(0, 4, home, 0)

    @pl.when(jnp.logical_not(at.stays))
    def _():
        for n in range(COLS):
            greet(at.swapped(n))

    return jnp.where(at.stays, COLS - 1 + 7 + 4, COLS - 1 + 8 + 4 + COLS)


def exchange_start(at, source, slot, send, recv):
    def column(n, carry):
        t = lax.rem(at.c + n, COLS)
        here = jnp.logical_and(n == 0, at.stays)
        send_or_copy(here, source.at[t], slot, send.at[t], recv.at[at.c], at.swapped(t))
        return carry

    unrolled(0, COLS, column, 0)


def exchange_arrived(landing, recv):
    def column(n, carry):
        arrived(landing.at[n], recv.at[n])
        return carry

    unrolled(0, COLS, column, 0)


def exchange_sent(at, source, send):
    def column(n, carry):
        t = lax.rem(at.c + n, COLS)

        @pl.when(jnp.logical_or(n > 0, jnp.logical_not(at.stays)))
        def _():
            arrived(source.at[t], send.at[t])

        return carry

    unrolled(0, COLS, column, 0)


def repeat_heads(w_bias_t):
    wide = jnp.concatenate([w_bias_t[...].astype(F32), jnp.zeros((C - H, C), F32)], axis=0).T
    lane = lax.div(lax.broadcasted_iota(jnp.int32, (C, H * SLOT), 1), SLOT)
    total = jnp.zeros((C, H * SLOT), F32)
    for h in range(H):
        total = jnp.where(lane == h, wide[:, h : h + 1], total)
    return total.astype(BF16)


def only_row(repeated, i):
    lane = lax.rem(lax.broadcasted_iota(jnp.int32, (1, H * SLOT), 1), SLOT)
    return repeated * (lane == i).astype(F32).astype(BF16)


def standardize(values):
    centre = values - jnp.mean(values, axis=-1, keepdims=True)
    inverse = lax.rsqrt(jnp.mean(centre * centre, axis=-1, keepdims=True) + 1e-5)
    return centre * inverse, jnp.broadcast_to(inverse, values.shape)


def norm_backward(grad, unit, inverse):
    mean_grad = jnp.mean(grad, axis=-1, keepdims=True)
    mean_cross = jnp.mean(grad * unit, axis=-1, keepdims=True)
    return inverse * (grad - mean_grad - unit * mean_cross)


MAIN_SCRATCH = dict(
    pair=((TALL * WIDTH, C), BF16),
    cot=((TALL * WIDTH, C), BF16),
    residues=((1, WIDTH), jnp.int32),
    gain=((1, C), F32),
    shift=((1, C), F32),
    w_proj=((C, 4 * HD), BF16),
    gate_bias=((1, HD), F32),
    w_out=((HD, C), BF16),
    home_unit=((TALL, WIDTH, C), F32),
    home_rstd=((TALL, WIDTH, C), F32),
    scores=((H, OWN, N, N), F32),
    d_prob=((H, OWN, N, N), F32),
    m1=((COLS, PADDED, C), BF16),
    m2=((COLS, PADDED, C), BF16),
    in1=((COLS, PADDED, C), BF16),
    in2=((COLS, PADDED, C), BF16),
    flags=((WIDTH, C), F32),
    w_proj_t=((3 * HD, C), BF16),
    w_rep=((C, H * SLOT), BF16),
    home_rows=((TALL, WIDTH, C), F32),
    zpack=((2, WIDTH, PAIR), F32),
    zin=((ROWS, WIDTH, PAIR), F32),
    bias=((H, COLS, WIDTH, N), F32),
    d_bias=((H, COLS, WIDTH, N), F32),
    d_other=((2, COLS, WIDTH, N), F32),
    stage_far=((4, WIDTH, N), F32),
    d_far=((2, 3, 4 * WIDTH, N), BF16),
    d_far_in=((2, 3, 4 * WIDTH, N), BF16),
    d_near=((2, 4, WIDTH, N), F32),
    d_near_in=((2, 3, WIDTH, N), F32),
    zout=((ROWS, WIDTH, PAIR), F32),
    hin=((2, 4, WIDTH, PAIR), F32),
    mask=((COLS, WIDTH, C), F32),
    row_mask=((OWN, 1, C), F32),
    normed=((OWN, N, C), BF16),
    unit=((OWN, N, C), F32),
    rstd=((OWN, N, C), F32),
    q=((OWN, N, C), BF16),
    k=((OWN, N, C), BF16),
    v=((OWN, N, C), BF16),
    d=((OWN, N, C), BF16),
    q_t=((OWN, C, N), BF16),
    k_t=((OWN, C, N), BF16),
    v_t=((OWN, C, N), BF16),
    d_t=((OWN, C, N), BF16),
    gate=((OWN, N, C), F32),
    dgate=((OWN, N, C), F32),
    att_t=((OWN, HD, N), F32),

    dq_t=((OWN, HD, N), F32),
    dk=((OWN, N, HD), F32),
    dv=((OWN, N, HD), F32),
    proj=((C, 4 * HD), F32),
    proj_b=((C, 4 * HD), BF16),
    r5=((COLS, 16, 2 * HD), BF16),
    v5=((16, 2 * HD), F32),
    r6=((8, 16, 2 * HD), F32),
    v6=((16, 2 * HD), BF16),
    out=((COLS, OWN, 2 * WIDTH, C), BF16),
)
MAIN_SEMS = dict(
    operand=(8,),
    norm=(2,),
    in1=(COLS,),
    in2=(COLS,),
    z=(8,),
    near=(2, 3),
    far=(2, 4, 3),
    partner=(2,),
    back=(2,),
    d_far=(2, 3),
    d_near=(2, 3),
    dz=(8,),
    p1=(COLS,),
    p2=(8,),
    p3=(COLS,),
    out=(2, COLS),
)
MAIN_IN = 10
MAIN_OUT = 5


class Names:
    pass


def main_kernel(*refs):
    length, w_bias_t, operands = refs[0], refs[1], refs[2:MAIN_IN]
    (land, proj_out, h_sum, unit_out, rstd_out) = refs[MAIN_IN : MAIN_IN + MAIN_OUT]
    rest = refs[MAIN_IN + MAIN_OUT :]
    m, send, recv = Names(), Names(), Names()
    for name, ref in zip(MAIN_SCRATCH, rest):
        setattr(m, name, ref)
    rest = rest[len(MAIN_SCRATCH) :]
    for name, ref in zip(MAIN_SEMS, rest):
        setattr(send, name, ref)
    for name, ref in zip(MAIN_SEMS, rest[len(MAIN_SEMS) :]):
        setattr(recv, name, ref)
    held = (m.pair, m.cot, m.residues, m.gain, m.shift, m.w_proj, m.gate_bias, m.w_out)
    pair, cot, residues, gain, shift, w_proj, gate_bias, w_out = held
    loads = [pltpu.make_async_copy(operands[n], held[n], recv.operand.at[n]) for n in range(len(held))]
    for load in loads:
        load.start()
    at = Place()
    e = at.e
    count = greet_all(at)
    for load in loads:
        load.wait()

    sublane = lax.broadcasted_iota(jnp.int32, (WIDTH, WIDTH), 0)
    lane = lax.broadcasted_iota(jnp.int32, (WIDTH, WIDTH), 1)
    valid = jnp.where(lane + at.c * WIDTH < length[0], residues[...], 0).astype(F32)
    valid = jnp.sum(jnp.where(lane == sublane, valid, 0.0), axis=1, keepdims=True)
    m.flags[...] = jnp.broadcast_to(valid, (WIDTH, C))
    m.w_rep[...] = repeat_heads(w_bias_t)
    unit, inverse = standardize(pair[...].astype(F32).reshape(TALL * WIDTH, C))
    m.home_unit[...] = unit.reshape(TALL, WIDTH, C)
    m.home_rstd[...] = inverse.reshape(TALL, WIDTH, C)
    m.home_rows[...] = (unit * gain[...] + shift[...]).reshape(TALL, WIDTH, C)

    def home_bias(n, total):
        for i in range(8):
            rows = m.home_rows[n * 8 + i].astype(BF16)
            total = total + jnp.dot(rows, only_row(m.w_rep[...], n * 8 + i), preferred_element_type=F32)
        return total

    packed = lax.fori_loop(0, TALL // 8, home_bias, jnp.zeros((WIDTH, H * SLOT), F32))
    negative = (m.flags[...] - 1.0) * 1e9
    m.zpack[0] = packed[:, :PAIR] + negative
    m.zpack[1] = packed[:, PAIR:] + negative

    pl.semaphore_wait(pltpu.get_barrier_semaphore(), count)

    def to_workers(n, carry):
        core, zz = lax.div(n, 4), lax.rem(n, 4)
        send_or_copy(
            at.is_worker(core, zz),
            m.zpack.at[core],
            m.zin.at[at.z],
            send.z.at[n],
            recv.z.at[at.z],
            at.worker(core, zz),
        )
        return carry

    unrolled(0, 8, to_workers, 0)
    lane = lax.broadcasted_iota(jnp.int32, (8, C), 1)
    packed_flags = jnp.where(
        lane == 0, m.flags[0:8, :], jnp.where(lane == 1, m.flags[8:16, :], m.flags[16:24, :])
    )
    pad = jnp.zeros((COLS, PADDED - PART, C), F32)
    m.m1[...] = jnp.concatenate(
        [
            pair[...].astype(F32).reshape(COLS, PART, C),
            jnp.broadcast_to(packed_flags[None], (COLS, PADDED - PART, C)),
        ],
        axis=1,
    ).astype(BF16)
    m.m2[...] = jnp.concatenate([cot[...].astype(F32).reshape(COLS, PART, C), pad], axis=1).astype(BF16)

    exchange_start(at, m.m1, m.in1.at[at.c], send.in1, recv.in1)
    exchange_start(at, m.m2, m.in2.at[at.c], send.in2, recv.in2)
    pltpu.make_async_copy(m.home_unit, unit_out, recv.norm.at[0]).start()
    pltpu.make_async_copy(m.home_rstd, rstd_out, recv.norm.at[1]).start()

    m.w_proj_t[...] = w_proj[:, : 3 * HD].astype(F32).T.astype(BF16)
    m.dk[...] = jnp.zeros_like(m.dk)
    m.dv[...] = jnp.zeros_like(m.dv)
    m.proj[...] = jnp.zeros_like(m.proj)
    def bias_block(hh, a, b):
        return m.bias.at[e * 2 + hh, at.col(at.f - a + 4, at.g - b + 4)]

    def to_far(hh, a):
        block = bias_block(hh, a, 0)
        for n in (1, 2, 3):
            remote(block, block, send.far.at[hh, a, n - 1], recv.far.at[hh, a, n - 1], at.gpeer(n)).start()

    def forward(hh):
        for n in (1, 2, 3):
            arrived(bias_block(hh, n, 0), recv.near.at[hh, n - 1])
            to_far(hh, n)

    for z in range(ROWS):
        arrived(m.zin.at[z], recv.z.at[z])
    for hh in range(2):
        head = e * 2 + hh
        m.bias[head, at.c] = jnp.concatenate(
            [m.zin[z][:, hh * SLOT : hh * SLOT + TALL] for z in range(ROWS)], axis=1
        )
        mine = m.bias.at[head, at.c]
        for n in (1, 2, 3):
            remote(mine, mine, send.near.at[hh, n - 1], recv.near.at[hh, n - 1], at.fpeer(n)).start()
        to_far(hh, 0)

    forward(0)
    forward(1)
    exchange_arrived(m.in1, recv.in1)

    for s in range(OWN):
        values = m.in1[:, s * WIDTH : (s + 1) * WIDTH, :].astype(F32).reshape(N, C)
        unit, inverse = standardize(values)
        m.unit[s] = unit
        m.rstd[s] = inverse
        m.normed[s] = (unit * gain[...] + shift[...]).astype(BF16)

    for s in range(OWN):
        rows = m.normed[s]
        flat = jnp.dot(rows, w_proj[...], preferred_element_type=F32)
        m.q[s] = (flat[:, :HD] * SCALE).astype(BF16)
        m.k[s] = flat[:, HD : 2 * HD].astype(BF16)
        m.v[s] = flat[:, 2 * HD : 3 * HD].astype(BF16)
        m.gate[s] = jax.nn.sigmoid(flat[:, 3 * HD :] + gate_bias[...])
        flat_t = lax.dot_general(m.w_proj_t[...], rows, NT, preferred_element_type=F32)
        m.q_t[s] = (flat_t[:HD] * SCALE).astype(BF16)
        m.k_t[s] = flat_t[HD : 2 * HD].astype(BF16)
        m.v_t[s] = flat_t[2 * HD : 3 * HD].astype(BF16)

    exchange_arrived(m.in2, recv.in2)
    tiles = m.in1[:, PART:, :].astype(F32)
    for t in range(3):
        rows = jnp.broadcast_to(tiles[:, :, t : t + 1], (COLS, 8, C))
        m.mask[:, t * 8 : (t + 1) * 8, :] = rows
    for s in range(OWN):
        values = m.in2[:, s * WIDTH : (s + 1) * WIDTH, :].astype(F32).reshape(N, C)
        row = at.row0 + s
        own_mask = m.mask[lax.div(row, WIDTH), pl.ds(lax.rem(row, WIDTH), 1), :]
        m.row_mask[s] = own_mask
        pair_mask = m.mask[...].reshape(N, C) * own_mask
        d_out = jnp.where(pair_mask > 0, values, 0.0).astype(BF16)
        d_gated = lax.dot_general(d_out, w_out[...], NT, preferred_element_type=F32)
        gates = m.gate[s]
        d_attn = d_gated * gates
        m.d[s] = d_attn.astype(BF16)
        m.d_t[s] = d_attn.T.astype(BF16)
        m.dgate[s] = d_attn * (1.0 - gates)

    def products(h, carry):
        row = lax.div(lax.broadcasted_iota(jnp.int32, (C, N), 0), DH)
        by_row = (row == h).astype(F32).astype(BF16)
        for s in range(OWN):
            m.scores[h, s] = jnp.dot(m.k[s], m.q_t[s] * by_row, preferred_element_type=F32)
            m.d_prob[h, s] = jnp.dot(m.v[s], m.d_t[s] * by_row, preferred_element_type=F32)
        return carry

    lax.fori_loop(0, H, products, 0)

    def own_bias_arrived(hh):
        for a in range(4):
            for n in (1, 2, 3):
                arrived(bias_block(hh, a, n), recv.far.at[hh, a, n - 1])
        whole = m.bias.at[e * 2 + hh]
        remote(whole, whole, send.partner.at[hh], recv.partner.at[hh], at.partner()).start()

    def other_bias_arrived(hh):
        arrived(m.bias.at[(1 - e) * 2 + hh], recv.partner.at[hh])

    def attend(h):
        here = pl.ds(pl.multiple_of(h * DH, DH), DH)
        lane = lax.div(lax.broadcasted_iota(jnp.int32, (1, C), 1), DH)
        by_lane = (lane == h).astype(F32).astype(BF16)
        dk, dv = [None] * OWN, [None] * OWN
        for n in range(3):
            lanes = slice(n * C, (n + 1) * C)
            d_bias = None
            for s in range(OWN):
                scores = m.scores[h, s, :, lanes] + m.bias[h, :, :, lanes].reshape(N, C)
                exponent = jnp.exp(scores - jnp.max(scores, axis=0, keepdims=True))
                weights = exponent * (1.0 / jnp.sum(exponent, axis=0, keepdims=True))
                weights_b = weights.astype(BF16)
                m.att_t[s, here, lanes] = jnp.dot(
                    m.v_t[s, here, :], weights_b, preferred_element_type=F32
                )
                d_prob = m.d_prob[h, s, :, lanes]
                d_score = weights * (d_prob - jnp.sum(weights * d_prob, axis=0, keepdims=True))
                d_score_b = d_score.astype(BF16)
                d_bias = d_score if d_bias is None else d_bias + d_score
                m.dq_t[s, here, lanes] = jnp.dot(
                    m.k_t[s, here, :], d_score_b, preferred_element_type=F32
                )
                dv_part = jnp.dot(weights_b, m.d[s, lanes, :] * by_lane, preferred_element_type=F32)
                dk_part = jnp.dot(d_score_b, m.q[s, lanes, :] * by_lane, preferred_element_type=F32)
                dv[s] = dv_part if dv[s] is None else dv[s] + dv_part
                dk[s] = dk_part if dk[s] is None else dk[s] + dk_part
            m.d_bias[h, :, :, lanes] = d_bias.reshape(COLS, WIDTH, C)
        for s in range(OWN):
            m.dk[s] += dk[s]
            m.dv[s] += dv[s]

    def to_other(hh):
        head = (1 - e) * 2 + hh
        remote(m.d_bias.at[head], m.d_other.at[hh], send.back.at[hh], recv.back.at[hh], at.partner()).start()

    def scatter_far(hh):
        head = e * 2 + hh
        arrived(m.d_other.at[hh], recv.back.at[hh])
        for n in (1, 2, 3, 0):
            for f in range(4):
                column = at.col(f, at.g + n)
                both = m.d_bias[head, column] + m.d_other[hh, column]
                if n == 0:
                    m.d_near[hh, f] = both
                else:
                    m.stage_far[f] = both
            if n > 0:
                m.d_far[hh, n - 1] = m.stage_far[...].reshape(4 * WIDTH, N).astype(BF16)
                remote(
                    m.d_far.at[hh, n - 1],
                    m.d_far_in.at[hh, n - 1],
                    send.d_far.at[hh, n - 1],
                    recv.d_far.at[hh, n - 1],
                    at.gpeer(n),
                ).start()

    def scatter_near(hh):
        for n in range(3):
            arrived(m.d_far_in.at[hh, n], recv.d_far.at[hh, n])
        far = (m.d_far_in[hh, 0].astype(F32) + m.d_far_in[hh, 1].astype(F32)) + m.d_far_in[hh, 2].astype(F32)
        m.d_near[hh] += far.reshape(4, WIDTH, N)
        for n in (1, 2, 3):
            remote(
                m.d_near.at[hh, lax.rem(at.f + n, 4)],
                m.d_near_in.at[hh, n - 1],
                send.d_near.at[hh, n - 1],
                recv.d_near.at[hh, n - 1],
                at.fpeer(n),
            ).start()

    def plane_sum(hh):
        for n in range(3):
            arrived(m.d_near_in.at[hh, n], recv.d_near.at[hh, n])
        return (m.d_near[hh, at.f] + m.d_near_in[hh, 0]) + (m.d_near_in[hh, 1] + m.d_near_in[hh, 2])

    def finish_row(s):
        attended = m.att_t[s].T
        gated = (m.gate[s] * attended).astype(BF16)
        pair_mask = m.mask[...].reshape(N, C) * m.row_mask[s]
        update = jnp.dot(gated, w_out[...], preferred_element_type=F32) * pair_mask
        d_proj = jnp.concatenate(
            [m.dq_t[s].T * SCALE, m.dk[s], m.dv[s], m.dgate[s] * attended], axis=1
        ).astype(BF16)
        d_normed = lax.dot_general(d_proj, w_proj[...], NT, preferred_element_type=F32)
        result = norm_backward(d_normed * gain[...], m.unit[s], m.rstd[s])
        m.out[:, s] = jnp.concatenate(
            [update.reshape(COLS, WIDTH, C), result.reshape(COLS, WIDTH, C)], axis=1
        ).astype(BF16)
        normed_t = m.normed[s].astype(F32).T.astype(BF16)
        m.proj[...] += jnp.dot(normed_t, d_proj, preferred_element_type=F32)

    def back(n):
        rows = pl.ds(0, 2) if n == 0 else pl.ds(2, 1)
        exchange_start(
            at, m.out.at[:, rows], land.at[at.c, rows], send.out.at[n], recv.out.at[n]
        )

    own_bias_arrived(0)
    attend(e * 2)
    own_bias_arrived(1)
    other_bias_arrived(0)
    attend(2 - e * 2)
    to_other(0)
    other_bias_arrived(1)
    attend(3 - e * 2)
    to_other(1)
    scatter_far(0)
    attend(e * 2 + 1)
    scatter_far(1)
    for s in range(OWN):
        finish_row(s)

    def piece(ref, c):
        rows = pl.ds(pl.multiple_of(lax.div(c, 2) * 16, 16), 16)
        return ref.at[rows, pl.ds(pl.multiple_of(lax.rem(c, 2) * 2 * HD, 2 * HD), 2 * HD)]

    m.proj_b[...] = m.proj[...].astype(BF16)

    def scatter_proj(n, carry):
        t = lax.rem(at.c + n, COLS)
        remote(piece(m.proj_b, t), m.r5.at[n], send.p1.at[n], recv.p1.at[n], at.plane(n)).start()
        return carry

    unrolled(1, COLS, scatter_proj, 0)
    scatter_near(0)
    back(0)
    scatter_near(1)

    def proj_arrived(n, total):
        arrived(m.r5.at[n], recv.p1.at[n])
        return total + m.r5[n].astype(F32)

    m.v5[...] = unrolled(1, COLS, proj_arrived, piece(m.proj, at.c)[...])

    def proj_to_homes(z, carry):
        slot = e * 4 + at.zz
        send_or_copy(at.is_home(z), m.v5, m.r6.at[slot], send.p2.at[z], recv.p2.at[slot], at.home(z))
        return carry

    unrolled(0, ROWS, proj_to_homes, 0)

    back(1)
    halves = [plane_sum(0), plane_sum(1)]
    blank = jnp.zeros((WIDTH, SLOT - TALL), F32)
    for z in range(ROWS):
        mine = slice(z * TALL, (z + 1) * TALL)
        m.zout[z] = jnp.concatenate([halves[0][:, mine], blank, halves[1][:, mine], blank], axis=1)

    def to_homes(z, carry):
        send_or_copy(
            at.is_home(z),
            m.zout.at[z],
            m.hin.at[e, at.zz],
            send.dz.at[z],
            recv.dz.at[e * 4 + at.zz],
            at.home(z),
        )
        return carry

    unrolled(0, ROWS, to_homes, 0)


    def share_arrived(n, total):
        arrived(m.r6.at[n], recv.p2.at[n])
        return total + m.r6[n]

    m.v6[...] = unrolled(0, 8, share_arrived, jnp.zeros((16, 2 * HD), F32)).astype(BF16)
    own_piece = piece(proj_out, at.c)
    pltpu.make_async_copy(m.v6, own_piece, recv.p3.at[0]).start()

    def spread(n, carry):
        remote(m.v6, own_piece, send.p3.at[n], recv.p3.at[n], at.plane(n)).start()
        return carry

    unrolled(1, COLS, spread, 0)

    for core in range(2):
        for zz in range(4):
            arrived(m.hin.at[core, zz], recv.dz.at[core * 4 + zz])
        lanes = slice(core * PAIR, (core + 1) * PAIR)
        h_sum[:, lanes] = (m.hin[core, 0] + m.hin[core, 1]) + (m.hin[core, 2] + m.hin[core, 3])
    exchange_arrived(land.at[:, pl.ds(0, 2)], recv.out.at[0])
    exchange_arrived(land.at[:, pl.ds(2, 1)], recv.out.at[1])

    def out_arrived(n, carry):
        arrived(piece(proj_out, lax.rem(at.c - n + COLS, COLS)), recv.p3.at[n])
        return carry

    lax.fori_loop(0, COLS, out_arrived, 0)

    arrived(unit_out, recv.norm.at[0])
    arrived(rstd_out, recv.norm.at[1])

    def column_sent(n, carry):
        arrived(m.v6, send.p1.at[n])
        arrived(m.v6, send.p3.at[n])
        return carry

    lax.fori_loop(1, COLS, column_sent, 0)

    def column_group_sent(n, carry):
        @pl.when(jnp.logical_not(at.is_worker(lax.div(n, 4), lax.rem(n, 4))))
        def _():
            arrived(m.zpack.at[0], send.z.at[n])

        @pl.when(jnp.logical_not(at.is_home(n)))
        def _():
            arrived(m.zout.at[0], send.dz.at[n])
            arrived(m.v5, send.p2.at[n])

        return carry

    lax.fori_loop(0, 8, column_group_sent, 0)
    for hh in range(2):
        for n in range(3):
            arrived(m.bias.at[0, 0], send.near.at[hh, n])
            for a in range(4):
                arrived(m.bias.at[0, 0], send.far.at[hh, a, n])
            arrived(m.d_far.at[0, 0], send.d_far.at[hh, n])
            arrived(m.d_near.at[0, 0], send.d_near.at[hh, n])
        arrived(m.bias.at[0], send.partner.at[hh])
        arrived(m.d_bias.at[0], send.back.at[hh])
    exchange_sent(at, m.m1, send.in1)
    exchange_sent(at, m.m2, send.in2)
    exchange_sent(at, m.out.at[:, pl.ds(0, 2)], send.out.at[0])
    exchange_sent(at, m.out.at[:, pl.ds(2, 1)], send.out.at[1])


STEPS = 2


def finish_kernel(
    land, proj_in, h_sum, unit, rstd, gain, w_bias_t, update, pair_grad, proj_out, w_rep, split, share
):
    tall = TALL // STEPS
    step = pl.program_id(0)

    @pl.when(step == 0)
    def _():
        proj_out[...] = proj_in[...].astype(F32)
        w_rep[...] = repeat_heads(w_bias_t)
        total = h_sum[...]
        for n in range(3):
            term = total.astype(BF16).astype(F32)
            split[n * WIDTH : (n + 1) * WIDTH, :] = term
            total = total - term

    landed = land[...].astype(F32)
    update[...] = landed[:, :, :WIDTH, :].reshape(tall, WIDTH, C).astype(BF16)
    share[...] = landed[:, :, WIDTH:, :].reshape(tall, WIDTH, C)
    terms = split[...].astype(BF16)
    for i in range(tall):
        parts = lax.dot_general(
            terms, only_row(w_rep[...], step * tall + i), NT, preferred_element_type=F32
        )
        grad = (parts[2 * WIDTH :] + parts[WIDTH : 2 * WIDTH]) + parts[:WIDTH]
        result = norm_backward(grad * gain[...], unit[i], rstd[i])
        pair_grad[i] = (share[i] + result).astype(BF16)


def vmem(count):
    return [pl.BlockSpec(memory_space=pltpu.VMEM)] * count


def shards(
    pair_act, cotangent, ln_gain, ln_shift, w_proj, gate_bias, w_bias, w_out, residue_mask, valid_length
):
    any_space = pl.BlockSpec(memory_space=pl.ANY)
    gain = ln_gain.reshape(1, C)
    sems = [pltpu.SemaphoreType.DMA(shape) for shape in MAIN_SEMS.values()]
    landing = jax.ShapeDtypeStruct((COLS, OWN, 2 * WIDTH, C), BF16)
    block = jax.ShapeDtypeStruct(pair_act.shape, F32)
    proj_shape = jax.ShapeDtypeStruct((C, 4 * HD), F32)
    land, proj, h_sum, unit, rstd = pl.pallas_call(
        main_kernel,
        out_shape=[
            landing,
            jax.ShapeDtypeStruct((C, 4 * HD), BF16),
            jax.ShapeDtypeStruct((WIDTH, H * SLOT), F32),
            block,
            block,
        ],
        in_specs=[pl.BlockSpec(memory_space=pltpu.SMEM)] + vmem(1) + [any_space] * (MAIN_IN - 2),
        out_specs=[any_space] * 2 + vmem(1) + [any_space] * 2,
        scratch_shapes=[pltpu.VMEM(shape, dtype) for shape, dtype in MAIN_SCRATCH.values()] + sems + sems,
        compiler_params=pltpu.CompilerParams(
            collective_id=0, has_side_effects=True, vmem_limit_bytes=VMEM_LIMIT
        ),
        name="main",
    )(
        valid_length,
        w_bias.T,
        pair_act.reshape(TALL * WIDTH, C),
        cotangent.reshape(TALL * WIDTH, C),
        residue_mask.reshape(1, WIDTH),
        gain,
        ln_shift.reshape(1, C),
        w_proj,
        gate_bias.reshape(1, HD),
        w_out,
    )
    result = jax.ShapeDtypeStruct(pair_act.shape, BF16)
    tall = TALL // STEPS
    rows = pl.BlockSpec((tall, WIDTH, C), lambda n: (n, 0, 0))
    landed = pl.BlockSpec((COLS // STEPS, OWN, 2 * WIDTH, C), lambda n: (n, 0, 0, 0))

    def whole(*shape):
        return pl.BlockSpec(shape, lambda n: (0,) * len(shape))

    return pl.pallas_call(
        finish_kernel,
        out_shape=[result, result, proj_shape],
        grid=(STEPS,),
        in_specs=[
            landed,
            whole(C, 4 * HD),
            whole(WIDTH, H * SLOT),
            rows,
            rows,
            whole(1, C),
            whole(H, C),
        ],
        out_specs=[rows, rows, whole(C, 4 * HD)],
        scratch_shapes=[
            pltpu.VMEM((C, H * SLOT), BF16),
            pltpu.VMEM((3 * WIDTH, H * SLOT), F32),
            pltpu.VMEM((tall, WIDTH, C), F32),
        ],
        compiler_params=pltpu.CompilerParams(vmem_limit_bytes=VMEM_LIMIT),
        name="finish",
    )(land, proj, h_sum, unit, rstd, gain, w_bias.T)


def solution(mesh):
    return jax.shard_map(
        shards,
        mesh=mesh,
        in_specs=(
            P(("complex", "row"), "col", None),
            P(("complex", "row"), "col", None),
            P(),
            P(),
            P(),
            P(),
            P(),
            P(),
            P(("complex", "col")),
            P("complex"),
        ),
        out_specs=(
            P(("complex", "row"), "col", None),
            P(("complex", "row"), "col", None),
            P("complex", None),
        ),
        check_vma=False,
    )
```
